128 devices in a mesh: seq: 16 (over y_hi, z, core), fsdp: 8 (over x, y_lo).
Axes of the slice: x: 4, y: 4 (y_hi: 2, y_lo: 2; y = y_hi * 2 + y_lo), z: 4, core: 2. Of those that a mesh axis runs over, the one named last changes fastest.
Arguments:
- tokens: bfloat16 [8, 2048, 4096], P('fsdp', 'seq'), may hold values from -40 to 40
- cotangent: bfloat16 [8, 2048, 4096], P('fsdp', 'seq'), may hold values from -6 to 6
- w_query: bfloat16 [4096, 2048], P(None, 'fsdp'), may hold values from -0.09375 to 0.09375
- w_key: bfloat16 [4096, 2048], P(None, 'fsdp'), may hold values from -0.09375 to 0.09375
- w_value: bfloat16 [4096, 2048], P(None, 'fsdp'), may hold values from -0.09375 to 0.09375
- w_output: bfloat16 [2048, 4096], P('fsdp'), may hold values from -0.125 to 0.125
- global_pos: int32 [8, 128], replicated, may hold values from 0 to 2047
- pattern: int32 [8, 32, 2], P(None, 'seq'), may hold values 0 or 1
Outputs:
- grad_tokens: bfloat16 [8, 2048, 4096], P('fsdp', 'seq')
- grad_query: float32 [4096, 2048], P('seq', 'fsdp')
- grad_key: float32 [4096, 2048], P('seq', 'fsdp')
- grad_value: float32 [4096, 2048], P('seq', 'fsdp')
- grad_output: float32 [2048, 4096], P('fsdp', 'seq')
The draws below stay inside these ranges and needn't reach their ends.
All inputs are finite; a program needn't handle non-finite values. No bound on the sum of `pattern` on one device may be relied on, other than what follows from the above.
Results may differ from the reference program's by a relative error of at most 0.019.
Values may be sent and summed in bfloat16 or wider, within the bound.
A program may use at most 192 MiB of HBM per device.

```python
import jax
import jax.numpy as jnp
from jax import lax

D = 4096
HEADS = 16
HDIM = 128
BLOCK = 64
NGLOB = 128
TOK_DEV = 128
DOCUMENT_COUNT = 8
SEQUENCE_LENGTH = 2048
NBLOCKS = 32
N_SEQ = 16
N_FSDP = 8


def draw_tokens(key, part):
    key = jax.random.fold_in(key, 11)
    first_key = jax.random.fold_in(key, 0)
    dims_shape = (DOCUMENT_COUNT, SEQUENCE_LENGTH, D)
    value_rows = jax.random.normal(first_key, dims_shape, jnp.float32)
    return jnp.clip(value_rows, -40.0, 40.0).astype(jnp.bfloat16)


def touch_ends(drawn, rng, least, top_value):
    spot = [jax.random.randint(jax.random.fold_in(rng, axis), (), 0, length) for axis, length in enumerate(drawn.shape)]
    longest = drawn.shape.index(max(drawn.shape))
    next_to = spot[:longest] + [(spot[longest] + 1) % drawn.shape[longest]] + spot[longest + 1:]
    return drawn.at[tuple(spot)].set(least).at[tuple(next_to)].set(top_value)


def steps_of(key, extent, shards, least, high):
    level = 1.0
    for position, parts in shards:
        steps = jax.random.uniform(jax.random.fold_in(jax.random.fold_in(key, 6), position), (parts,), jnp.float32, least / len(shards), high / len(shards))
        level = level * jnp.repeat(jnp.exp(steps), extent[position] // parts).reshape((-1,) + (1,) * (len(extent) - 1 - position))
    return level


def noise(key, extent, width, reach, cuts=(), kind=jnp.bfloat16):
    level = steps_of(key, extent, cuts, -0.22, 0.18) if cuts else 1.0
    values = jax.random.normal(key, extent, jnp.float32) * width * level
    return jnp.minimum(jnp.maximum(values, -reach), reach).astype(kind)


def setup_inputs(seed: int = 0) -> dict:
    key_of = jax.random.split(jax.random.key(seed), 9)
    tokens = draw_tokens(jax.random.fold_in(key_of[8], 71), 0)
    cotangent = noise(key_of[1], (DOCUMENT_COUNT, SEQUENCE_LENGTH, D), 1.0, 6.0, ((0, 8), (1, 16)))
    w_query = noise(key_of[2], (D, HEADS * HDIM), D ** -0.5, 0.09375, ((1, 8),))
    w_key = noise(key_of[3], (D, HEADS * HDIM), D ** -0.5, 0.09375, ((1, 8),))
    w_value = noise(key_of[4], (D, HEADS * HDIM), D ** -0.5, 0.09375, ((1, 8),))
    w_output = noise(key_of[5], (HEADS * HDIM, D), (HEADS * HDIM) ** -0.5, 0.125, ((0, 8),))
    global_pos = touch_ends(jax.random.randint(key_of[6], (DOCUMENT_COUNT, NGLOB), 0, SEQUENCE_LENGTH), jax.random.fold_in(key_of[6], 1), 0, SEQUENCE_LENGTH - 1).astype(jnp.int32)
    pattern = touch_ends((jax.random.randint(key_of[7], (DOCUMENT_COUNT, NBLOCKS, 2), 0, 4) < 3).astype(jnp.int32), jax.random.fold_in(key_of[7], 1), 0, 1)
    return {"tokens": tokens, "cotangent": cotangent, "w_query": w_query, "w_key": w_key, "w_value": w_value, "w_output": w_output, "global_pos": global_pos, "pattern": pattern}


def product(form, left, right):
    return jnp.einsum(form, left.astype(jnp.float32), right.astype(jnp.float32))


def block_mask(pattern, first_block, block_total):
    block_count = pattern.shape[0]
    index = first_block + jnp.arange(block_count, dtype=jnp.int32)
    before = (pattern[:, 0] == 1) & (index > 0)
    after = (pattern[:, 1] == 1) & (index < block_total - 1)
    middle = jnp.ones((block_count, BLOCK), jnp.bool_)
    return jnp.concatenate([jnp.broadcast_to(before[:, None], (block_count, BLOCK)), middle,
                            jnp.broadcast_to(after[:, None], (block_count, BLOCK))], axis=1)


def windows(extended, block_count):
    blocks = extended.reshape(block_count + 2, BLOCK, extended.shape[-1])
    return jnp.concatenate([blocks[:block_count], blocks[1:block_count + 1], blocks[2:]], axis=1)


def unwindow(grads, block_count):
    lower = grads[:, :BLOCK]
    center = grads[:, BLOCK:2 * BLOCK]
    upper = grads[:, 2 * BLOCK:]
    summed = jnp.pad(lower, ((0, 2), (0, 0), (0, 0))) + jnp.pad(center, ((1, 1), (0, 0), (0, 0)))
    summed = summed + jnp.pad(upper, ((2, 0), (0, 0), (0, 0)))
    return summed.reshape((block_count + 2) * BLOCK, grads.shape[-1])


def doc_attention(query, extended, global_kv, pattern, grad_ctx, first_block, block_total):
    row_count, head_width = query.shape
    block_count = row_count // BLOCK
    head_count = head_width // HDIM
    scale = HDIM ** -0.5
    window_kv = windows(extended, block_count)
    key_win = window_kv[..., :head_width].reshape(block_count, 3 * BLOCK, head_count, HDIM)
    value_win = window_kv[..., head_width:].reshape(block_count, 3 * BLOCK, head_count, HDIM)
    key_glob = global_kv[:, :head_width].reshape(-1, head_count, HDIM)
    value_glob = global_kv[:, head_width:].reshape(-1, head_count, HDIM)
    queries = query.reshape(block_count, BLOCK, head_count, HDIM)
    grad_out = grad_ctx.reshape(block_count, BLOCK, head_count, HDIM)
    mask = block_mask(pattern, first_block, block_total)
    local = product('nqhe,nkhe->nhqk', queries, key_win) * scale
    local = jnp.where(mask[:, None, None, :], local, -jnp.inf)
    remote = product('nqhe,ghe->nhqg', queries, key_glob) * scale
    top = jnp.maximum(local.max(-1), remote.max(-1))[..., None]
    local_exp = jnp.exp(local - top)
    remote_exp = jnp.exp(remote - top)
    denom = local_exp.sum(-1, keepdims=True) + remote_exp.sum(-1, keepdims=True)
    p_local = local_exp / denom
    p_remote = remote_exp / denom
    p_local_b = p_local.astype(jnp.bfloat16)
    p_remote_b = p_remote.astype(jnp.bfloat16)
    context = (product('nhqk,nkhe->nqhe', p_local_b, value_win)
               + product('nhqg,ghe->nqhe', p_remote_b, value_glob)).astype(jnp.bfloat16)
    d_local = product('nqhe,nkhe->nhqk', grad_out, value_win)
    d_remote = product('nqhe,ghe->nhqg', grad_out, value_glob)
    delta = (p_local * d_local).sum(-1, keepdims=True) + (p_remote * d_remote).sum(-1, keepdims=True)
    s_local = (p_local * (d_local - delta) * scale).astype(jnp.bfloat16)
    s_remote = (p_remote * (d_remote - delta) * scale).astype(jnp.bfloat16)
    grad_q = (product('nhqk,nkhe->nqhe', s_local, key_win)
              + product('nhqg,ghe->nqhe', s_remote, key_glob)).astype(jnp.bfloat16)
    dkey_win = product('nhqk,nqhe->nkhe', s_local, queries)
    dvalue_win = product('nhqk,nqhe->nkhe', p_local_b, grad_out)
    dkey_glob = product('nhqg,nqhe->ghe', s_remote, queries)
    dvalue_glob = product('nhqg,nqhe->ghe', p_remote_b, grad_out)
    grad_ext = unwindow(jnp.concatenate([dkey_win.reshape(block_count, 3 * BLOCK, head_width),
                                         dvalue_win.reshape(block_count, 3 * BLOCK, head_width)], -1), block_count)
    grad_glob = jnp.concatenate([dkey_glob.reshape(-1, head_width), dvalue_glob.reshape(-1, head_width)], -1)
    return context.reshape(row_count, head_width), grad_q.reshape(row_count, head_width), grad_ext, grad_glob


def contract_rows(left, right):
    return lax.dot_general(left, right, (((0,), (0,)), ((), ())), preferred_element_type=jnp.float32)


def contract_cols(left, right):
    return lax.dot_general(left, right, (((1,), (1,)), ((), ())), preferred_element_type=jnp.float32)


def reference(tokens, cotangent, w_query, w_key, w_value, w_output, global_pos, pattern):
    head_width = HEADS * HDIM
    flat = tokens.reshape(-1, D)
    query = jnp.dot(flat, w_query, preferred_element_type=jnp.float32).astype(jnp.bfloat16)
    keys = jnp.dot(flat, w_key, preferred_element_type=jnp.float32).astype(jnp.bfloat16)
    value_rows = jnp.dot(flat, w_value, preferred_element_type=jnp.float32).astype(jnp.bfloat16)
    grads_flat = cotangent.reshape(-1, D)
    grad_ctx = contract_cols(grads_flat, w_output).astype(jnp.bfloat16)

    def per_doc(items):
        doc_query, doc_keys, doc_values, doc_grad, doc_pos, doc_pattern = items
        keys_vals = jnp.concatenate([doc_keys, doc_values], -1)
        extended = jnp.pad(keys_vals, ((BLOCK, BLOCK), (0, 0)))
        global_kv = jnp.take(keys_vals, doc_pos, axis=0)
        context, grad_q, grad_ext, grad_glob = doc_attention(doc_query, extended, global_kv, doc_pattern,
                                                             doc_grad, 0, NBLOCKS)
        owned = grad_ext[BLOCK:-BLOCK].at[doc_pos].add(grad_glob)
        return (context, grad_q, owned[:, :head_width].astype(jnp.bfloat16),
                owned[:, head_width:].astype(jnp.bfloat16))

    def shaped(array):
        return array.reshape(DOCUMENT_COUNT, SEQUENCE_LENGTH, head_width)

    context, grad_q, grad_k, grad_v = lax.map(per_doc, (shaped(query), shaped(keys), shaped(value_rows),
                                                        shaped(grad_ctx), global_pos, pattern))
    flat_q = grad_q.reshape(-1, head_width)
    flat_k = grad_k.reshape(-1, head_width)
    flat_v = grad_v.reshape(-1, head_width)
    group = head_width // N_FSDP
    grad_sum = jnp.zeros((DOCUMENT_COUNT * SEQUENCE_LENGTH, D), jnp.float32)
    for index in range(N_FSDP):
        lo_col = index * group
        hi_col = lo_col + group
        term = (contract_cols(flat_q[:, lo_col:hi_col], w_query[:, lo_col:hi_col])
                + contract_cols(flat_k[:, lo_col:hi_col], w_key[:, lo_col:hi_col])
                + contract_cols(flat_v[:, lo_col:hi_col], w_value[:, lo_col:hi_col]))
        grad_sum = grad_sum + term.astype(jnp.bfloat16).astype(jnp.float32)
    grad_tokens = grad_sum.astype(jnp.bfloat16).reshape(DOCUMENT_COUNT, SEQUENCE_LENGTH, D)

    def shard_term(accum, shard):
        begin = shard * TOK_DEV

        def take(array):
            return lax.dynamic_slice_in_dim(array, begin, TOK_DEV, 1).reshape(DOCUMENT_COUNT * TOK_DEV, array.shape[-1])

        inputs = take(tokens)
        grads_in = take(cotangent)
        term = jnp.concatenate([contract_rows(inputs, take(grad_q)), contract_rows(inputs, take(grad_k)),
                                contract_rows(inputs, take(grad_v)), contract_rows(grads_in, take(context))], 1)
        return accum + term.astype(jnp.bfloat16).astype(jnp.float32), None

    accum, unused = lax.scan(shard_term, jnp.zeros((D, 4 * head_width), jnp.float32),
                             jnp.arange(N_SEQ, dtype=jnp.int32))
    grad_query = accum[:, :head_width]
    grad_key = accum[:, head_width:2 * head_width]
    grad_value = accum[:, 2 * head_width:3 * head_width]
    grad_output = accum[:, 3 * head_width:].T
    return grad_tokens, grad_query, grad_key, grad_value, grad_output
```

```python
import jax
import jax.numpy as jnp
from jax import lax
from jax.experimental import pallas as pl
from jax.experimental.pallas import tpu as pltpu
from jax.sharding import PartitionSpec as P

BLOCK = 64
HDIM = 128
ROWS = 128
CHIP_ROWS = 256
D = 4096
BF = jnp.bfloat16
F32 = jnp.float32
MESH = pl.DeviceIdType.MESH
ANY = pl.BlockSpec(memory_space=pl.ANY)
NT = (((1,), (1,)), ((), ()))
TN = (((0,), (0,)), ((), ()))


def place():
    f = lax.axis_index("fsdp")
    s = lax.axis_index("seq")
    x, p = lax.div(f, 2), lax.rem(f, 2)
    yh, z, c = lax.div(s, 8), lax.rem(lax.div(s, 2), 4), lax.rem(s, 2)
    return x, 2 * yh + p, z, c


def device(x, y, z, c):
    return {"seq": lax.div(y, 2) * 8 + z * 2 + c, "fsdp": x * 2 + lax.rem(y, 2)}


def mod4(v):
    return lax.rem(v + 4, 4)


def al(v, n):
    return pl.multiple_of(v, n)


def remote(src, dst, send, recv, where):
    return pltpu.make_async_remote_copy(
        src_ref=src, dst_ref=dst, send_sem=send, recv_sem=recv, device_id=where, device_id_type=MESH
    )


def meet(devices):
    barrier = pltpu.get_barrier_semaphore()
    for where in devices:
        pl.semaphore_signal(barrier, inc=1, device_id=where, device_id_type=MESH)
    pl.semaphore_wait(barrier, len(devices))


def chip_peer(x, y, z, c, k):
    j = lax.rem(lax.div(y, 2) * 4 + z + k, 8)
    return j, device(x, lax.div(j, 4) * 2 + lax.rem(y, 2), lax.rem(j, 4), c)


def gather_kernel(
    tok_in, cot_in, wq, wk, wv, wo,
    tok_out, cot_out, w_out, r_out,
    tok, cot, w, wov, stage,
    ssem, rsem, wssem, wrsem, lsem, assem, arsem, bssem, brsem, osem,
):
    x, y, z, c = place()
    p = lax.rem(y, 2)
    xr, xl, x2 = mod4(x + 1), mod4(x - 1), mod4(x + 2)
    right, left = device(xr, y, z, c), device(xl, y, z, c)
    sib = device(x, y, z, 1 - c)
    me = lax.div(y, 2) * 4 + z
    peers = [chip_peer(x, y, z, c, k) for k in range(1, 8)]
    up, down = mod4(y + 1), mod4(y - 1)
    meet(
        [right, left, sib]
        + [device(x, v, z, core) for v in (up, down) for core in (0, 1)]
        + [where for _, where in peers]
    )
    own = pl.ds(al(c * ROWS, ROWS), ROWS)
    first = pl.ds(al(c * ROWS, 64), 64)
    second = pl.ds(al(c * ROWS + 64, 64), 64)

    def sends(a, given, buf):
        def cp(kind, src, dst, where):
            return remote(src, dst, ssem.at[a, kind], rsem.at[a, kind], where)

        return [
            cp(0, given, buf.at[x, own], right),
            cp(1, given, buf.at[x, own], left),
            cp(2, given, buf.at[x, own], sib),
            cp(3, buf.at[xl, first], buf.at[xl, first], right),
            cp(4, buf.at[xr, second], buf.at[xr, second], left),
            cp(5, buf.at[xl, own], buf.at[xl, own], sib),
            cp(6, buf.at[xr, own], buf.at[xr, own], sib),
            cp(7, buf.at[x2, first], buf.at[x2, first], sib),
            cp(8, buf.at[x2, second], buf.at[x2, second], sib),
        ]

    tsend = sends(0, tok_in, tok)
    csend = sends(1, cot_in, cot)
    ydst = mod4(y + 1 + 2 * c)
    wdev = device(x, ydst, z, p)
    half = pl.ds(al(c * 2048, 2048), 2048)
    half_o = pl.ds(al(c * 128, 128), 128)
    wsend = [
        remote(src.at[half], w.at[t, half], wssem.at[t], wrsem.at[t, c], wdev)
        for t, src in enumerate((wq, wk, wv))
    ]
    wsend.append(remote(wo.at[half_o], wov.at[half_o], wssem.at[3], wrsem.at[3, c], wdev))
    wlocal = [pltpu.make_async_copy(src, w.at[t], lsem.at[t]) for t, src in enumerate((wq, wk, wv))]
    wlocal.append(pltpu.make_async_copy(wo, wov, lsem.at[3]))
    tlocal = pltpu.make_async_copy(tok_in, tok.at[x, own], lsem.at[4])
    clocal = pltpu.make_async_copy(cot_in, cot.at[x, own], lsem.at[5])

    for k in (0, 1, 2):
        tsend[k].start()
    for cp in wsend:
        cp.start()
    tlocal.start()
    clocal.start()

    @pl.when(c == p)
    def _():
        for cp in wlocal:
            cp.start()

    def relay(copies):
        copies[0].wait_recv()
        copies[3].start()
        copies[5].start()
        copies[1].wait_recv()
        copies[4].start()
        copies[6].start()

    relay(tsend)
    for k in (0, 1, 2):
        csend[k].start()
    tsend[3].wait_recv()
    tsend[7].start()
    tsend[4].wait_recv()
    tsend[8].start()
    tlocal.wait()
    clocal.wait()

    def weights_here(ts):
        @pl.when(c == p)
        def _():
            for t in ts:
                wlocal[t].wait()

        @pl.when(c != p)
        def _():
            for t in ts:
                for h in (0, 1):
                    if t < 3:
                        ref = w.at[t, pl.ds(h * 2048, 2048)]
                    else:
                        ref = wov.at[pl.ds(h * 128, 128)]
                    remote(ref, ref, wssem.at[t], wrsem.at[t, h], sib).wait_recv()

    weights_here((0, 1, 2))
    for k in (2, 5, 6, 7, 8):
        tsend[k].wait_recv()
    out_t = pltpu.make_async_copy(tok, tok_out, osem.at[0])
    out_t.start()
    out_w = pltpu.make_async_copy(w, w_out, osem.at[2])
    out_w.start()

    @pl.loop(0, 4)
    def _(doc):
        @pl.loop(0, 3)
        def _(t):
            got = jnp.dot(tok[doc], w[t], preferred_element_type=F32).astype(BF)
            stage[2 * doc, t] = got[:, :HDIM]
            stage[2 * doc + 1, t] = got[:, HDIM:]

    mine = pl.ds(al(me * CHIP_ROWS, CHIP_ROWS), CHIP_ROWS)
    qkv = [
        remote(stage.at[j, pl.ds(0, 3)], r_out.at[pl.ds(0, 3), mine], assem.at[k], arsem.at[k], where)
        for k, (j, where) in enumerate(peers)
    ]
    for cp in qkv:
        cp.start()
    qkv_own = pltpu.make_async_copy(stage.at[me, pl.ds(0, 3)], r_out.at[pl.ds(0, 3), mine], lsem.at[6])
    qkv_own.start()

    relay(csend)
    weights_here((3,))

    def back(doc):
        got = lax.dot_general(cot[doc], wov[...], NT, preferred_element_type=F32).astype(BF)
        stage[2 * doc, 3] = got[:, :HDIM]
        stage[2 * doc + 1, 3] = got[:, HDIM:]
        for h in (0, 1):
            j = 2 * doc + h
            where = device(x, lax.div(j, 4) * 2 + p, lax.rem(j, 4), c)

            @pl.when(j != me)
            def _():
                remote(stage.at[j, 3], r_out.at[3, mine], bssem.at[j], brsem.at[me], where).start()

            @pl.when(j == me)
            def _():
                pltpu.make_async_copy(stage.at[j, 3], r_out.at[3, mine], lsem.at[7]).start()

    csend[2].wait_recv()
    back(x)
    csend[5].wait_recv()
    back(xl)
    csend[6].wait_recv()
    back(xr)
    csend[3].wait_recv()
    csend[7].start()
    csend[4].wait_recv()
    csend[8].start()
    csend[7].wait_recv()
    csend[8].wait_recv()
    back(x2)
    out_c = pltpu.make_async_copy(cot, cot_out, osem.at[1])
    out_c.start()
    for cp in tsend + csend + wsend:
        cp.wait_send()
    for cp in qkv:
        cp.wait()
    qkv_own.wait()
    for j in range(8):

        @pl.when(j != me)
        def _():
            cp = remote(stage.at[j, 3], r_out.at[3, pl.ds(j * CHIP_ROWS, CHIP_ROWS)], bssem.at[j], brsem.at[j], sib)
            cp.wait_send()
            cp.wait_recv()

    pltpu.make_async_copy(stage.at[me, 3], r_out.at[3, mine], lsem.at[7]).wait()
    out_t.wait()
    out_w.wait()
    out_c.wait()


def gather(tokens, cotangent, wq, wk, wv, wo):
    dma = pltpu.SemaphoreType.DMA
    return pl.pallas_call(
        gather_kernel,
        out_shape=(
            jax.ShapeDtypeStruct((4, CHIP_ROWS, D), BF),
            jax.ShapeDtypeStruct((4, CHIP_ROWS, D), BF),
            jax.ShapeDtypeStruct((3, D, 256), BF),
            jax.ShapeDtypeStruct((4, 2048, HDIM), BF),
        ),
        in_specs=[ANY] * 6,
        out_specs=(ANY,) * 4,
        scratch_shapes=[
            pltpu.VMEM((4, CHIP_ROWS, D), BF),
            pltpu.VMEM((4, CHIP_ROWS, D), BF),
            pltpu.VMEM((3, D, 256), BF),
            pltpu.VMEM((256, D), BF),
            pltpu.VMEM((8, 4, CHIP_ROWS, HDIM), BF),
            dma((2, 9)), dma((2, 9)), dma((4,)), dma((4, 2)), dma((8,)),
            dma((7,)), dma((7,)), dma((8,)), dma((8,)), dma((3,)),
        ],
        compiler_params=pltpu.CompilerParams(
            collective_id=0, has_side_effects=True, vmem_limit_bytes=44 << 20
        ),
        cost_estimate=pl.CostEstimate(flops=9 * 10**9, bytes_accessed=60 << 20, transcendentals=0),
    )(tokens, cotangent, wq, wk, wv, wo)


def attention_kernel(flags, pos_row, pos_col, r, o, kp, vp, dkp, dvp, kg, vg, dkg, dvg):
    n = 2048
    scale = HDIM**-0.5
    for dst, t in ((kp, 1), (vp, 2)):
        dst[:BLOCK] = jnp.zeros((BLOCK, HDIM), BF)
        dst[BLOCK : BLOCK + n] = r[t]
        dst[BLOCK + n :] = jnp.zeros((BLOCK, HDIM), BF)
    dkp[...] = jnp.zeros_like(dkp)
    dvp[...] = jnp.zeros_like(dvp)
    dkg[...] = jnp.zeros_like(dkg)
    dvg[...] = jnp.zeros_like(dvg)
    pick = (pos_col[...] == lax.broadcasted_iota(jnp.int32, (128, n), 1)).astype(F32).astype(BF)
    kg[...] = jnp.dot(pick, r[1], preferred_element_type=F32).astype(BF)
    vg[...] = jnp.dot(pick, r[2], preferred_element_type=F32).astype(BF)
    col = lax.div(lax.broadcasted_iota(jnp.int32, (1, 256), 1), 64)
    low = lax.broadcasted_iota(jnp.int32, (128, 256), 0) < BLOCK

    def nt(a, b):
        return lax.dot_general(a, b, NT, preferred_element_type=F32)

    def tn(a, b):
        return lax.dot_general(a, b, TN, preferred_element_type=F32)

    def step(i, _):
        rows = pl.ds(al(i * 128, 128), 128)
        win = pl.ds(al(i * 128, 128), 256)
        q, do = r[0, rows], r[3, rows]
        k, v = kp[win], vp[win]
        prev0 = jnp.where(i > 0, flags[4 * i], 0)
        next0 = flags[4 * i + 1]
        prev1 = flags[4 * i + 2]
        next1 = jnp.where(i < 15, flags[4 * i + 3], 0)
        m0 = jnp.where(col == 0, prev0, jnp.where(col == 1, 1, jnp.where(col == 2, next0, 0)))
        m1 = jnp.where(col == 0, 0, jnp.where(col == 1, prev1, jnp.where(col == 2, 1, next1)))
        seen = jnp.where(low, m0, m1) == 1
        sl = jnp.where(seen, nt(q, k) * scale, -jnp.inf)
        sg = nt(q, kg[...]) * scale
        top = jnp.maximum(sl.max(-1, keepdims=True), sg.max(-1, keepdims=True))
        el, eg = jnp.exp(sl - top), jnp.exp(sg - top)
        inv = 1.0 / (el.sum(-1, keepdims=True) + eg.sum(-1, keepdims=True))
        pl_, pg = el * inv, eg * inv
        plb, pgb = pl_.astype(BF), pg.astype(BF)
        ctx = jnp.dot(plb, v, preferred_element_type=F32) + jnp.dot(pgb, vg[...], preferred_element_type=F32)
        o[3, rows] = ctx.astype(BF)
        dl, dg = nt(do, v), nt(do, vg[...])
        delta = (pl_ * dl).sum(-1, keepdims=True) + (pg * dg).sum(-1, keepdims=True)
        zl = (pl_ * (dl - delta) * scale).astype(BF)
        zg = (pg * (dg - delta) * scale).astype(BF)
        gq = jnp.dot(zl, k, preferred_element_type=F32) + jnp.dot(zg, kg[...], preferred_element_type=F32)
        o[0, rows] = gq.astype(BF)
        dkp[win] += tn(zl, q)
        dvp[win] += tn(plb, do)
        dkg[...] += tn(zg, q)
        dvg[...] += tn(pgb, do)
        return 0

    lax.fori_loop(0, 16, step, 0)

    def split(a):
        high = a.astype(BF)
        return high, (a - high.astype(F32)).astype(BF)

    kh, klo = split(dkg[...])
    vh, vlo = split(dvg[...])

    def finish(i, _):
        rows = pl.ds(al(i * 128, 128), 128)
        inner = pl.ds(al(i * 128 + BLOCK, 64), 128)
        put = (pos_row[...] == i * 128 + lax.broadcasted_iota(jnp.int32, (128, 128), 0)).astype(F32).astype(BF)

        def dot(b):
            return jnp.dot(put, b, preferred_element_type=F32)

        o[1, rows] = (dkp[inner] + dot(kh) + dot(klo)).astype(BF)
        o[2, rows] = (dvp[inner] + dot(vh) + dot(vlo)).astype(BF)
        return 0

    lax.fori_loop(0, 16, finish, 0)


def attention(flags, pos, r):
    vm = pl.BlockSpec(memory_space=pltpu.VMEM)
    return pl.pallas_call(
        attention_kernel,
        out_shape=jax.ShapeDtypeStruct((4, 2048, HDIM), BF),
        in_specs=[pl.BlockSpec(memory_space=pltpu.SMEM), vm, vm, vm],
        out_specs=vm,
        scratch_shapes=[
            pltpu.VMEM((2176, HDIM), BF), pltpu.VMEM((2176, HDIM), BF),
            pltpu.VMEM((2176, HDIM), F32), pltpu.VMEM((2176, HDIM), F32),
            pltpu.VMEM((128, HDIM), BF), pltpu.VMEM((128, HDIM), BF),
            pltpu.VMEM((128, HDIM), F32), pltpu.VMEM((128, HDIM), F32),
        ],
        compiler_params=pltpu.CompilerParams(vmem_limit_bytes=32 << 20),
        cost_estimate=pl.CostEstimate(flops=2 * 10**9, bytes_accessed=4 << 20, transcendentals=10**6),
    )(flags, pos.reshape(1, 128), pos.reshape(128, 1), r)


def scatter_kernel(
    o_in, tok, cot, w_in,
    gt_out, wg_out,
    w, g, gt, part, pr, xa, xf, wp, za, zf, tb, cb, ya, yf, fs, gto,
    lsem, assem, arsem, sssem, srsem, xssem, xrsem, zssem, zrsem, yssem, yrsem, tsem, csem,
):
    x, y, z, c = place()
    p, yh = lax.rem(y, 2), lax.div(y, 2)
    xr, xl, x2 = mod4(x + 1), mod4(x - 1), mod4(x + 2)
    zr, zl, z2 = mod4(z + 1), mod4(z - 1), mod4(z + 2)
    right, left = device(xr, y, z, c), device(xl, y, z, c)
    front, rear = device(x, y, zr, c), device(x, y, zl, c)
    up, down = mod4(y + 1), mod4(y - 1)
    above, below = device(x, up, z, c), device(x, down, z, c)
    sib = device(x, y, z, 1 - c)
    me = yh * 4 + z
    peers = [chip_peer(x, y, z, c, k) for k in range(1, 8)]
    meet([right, left, sib, above, below] + [where for _, where in peers])

    def spot(j):
        return g.at[
            :, pl.ds(al(lax.div(j, 2) * CHIP_ROWS, CHIP_ROWS), CHIP_ROWS), pl.ds(al(lax.rem(j, 2) * HDIM, HDIM), HDIM)
        ]

    def rows_of(j):
        return o_in.at[:, pl.ds(al(j * CHIP_ROWS, CHIP_ROWS), CHIP_ROWS)]

    a2a = [
        remote(rows_of(j), spot(me), assem.at[k], arsem.at[k], where) for k, (j, where) in enumerate(peers)
    ]
    for cp in a2a:
        cp.start()
    own_part = pltpu.make_async_copy(rows_of(me), spot(me), lsem.at[0])
    own_part.start()
    w_load = pltpu.make_async_copy(w_in, w, lsem.at[1])

    groups = (z2, zr, zl, z)
    order = [(0, 0), (0, 1), (1, 1), (2, 0), (1, 0), (2, 1), (3, 0), (3, 1)]

    def load(n):
        o, ab = order[n]
        cols = pl.ds(al(ab * 2048 + groups[o] * 512, 512), 512)
        slot = n % 2
        return (
            pltpu.make_async_copy(tok.at[:, :, cols], tb.at[slot], tsem.at[slot]),
            pltpu.make_async_copy(cot.at[:, :, cols], cb.at[slot], csem.at[slot]),
        )

    def fetch(n):
        for cp in load(n):
            cp.start()

    fetch(0)
    w_load.start()
    for cp in a2a:
        cp.wait()
    own_part.wait()

    @pl.loop(0, 4)
    def _(t):
        for i in range(4):
            rows = pl.ds(i * 256, 256)
            gt[pl.ds(al(t * 256, 256), 256), rows] = g[t, rows].T

    def piece(n):
        o, ab = order[n]
        slot = n % 2
        if n + 1 < len(order):
            fetch(n + 1)
        for cp in load(n):
            cp.wait()

        def body(src):
            def run(i):
                rows = pl.ds(al(i * 256, 256), 256)
                acc = jnp.zeros((256, 512), F32)
                for b in range(4):
                    acc += jnp.dot(
                        gt[rows, pl.ds(b * 256, 256)], src[slot, b], preferred_element_type=F32
                    )
                wp[o, ab, rows] = acc.astype(BF)

            return run

        pl.loop(0, 3)(body(tb))
        body(cb)(3)

    docs = (x2, xr, xl, x)
    own = pl.ds(al(c * ROWS, ROWS), ROWS)
    other = pl.ds(al((1 - c) * ROWS, ROWS), ROWS)
    to_sib = [remote(part.at[o, other], pr.at[o], sssem.at[o], srsem.at[o], sib) for o in range(4)]

    def tokens_part(o):
        rows = pl.ds(al(docs[o] * CHIP_ROWS, CHIP_ROWS), CHIP_ROWS)

        @pl.loop(0, 8)
        def _(n):
            cols = pl.ds(al(n * 512, 512), 512)
            acc = jnp.zeros((CHIP_ROWS, 512), F32)
            for t in range(3):
                acc += lax.dot_general(g[t, rows], w[t, cols], NT, preferred_element_type=F32)
            part[o, :, cols] = acc.astype(BF)

        to_sib[o].start()

    def z_copy(i, src, dst, where):
        return remote(src, dst, zssem.at[i], zrsem.at[i], where)

    zc = [
        z_copy(0, wp.at[0, 0], za.at[0], front),
        z_copy(1, wp.at[0, 1], za.at[1], rear),
        z_copy(2, wp.at[1, 1], zf.at[0, 1], front),
        z_copy(3, wp.at[2, 0], zf.at[1, 0], rear),
        z_copy(4, wp.at[1, 0], zf.at[0, 0], front),
        z_copy(5, wp.at[2, 1], zf.at[1, 1], rear),
    ]
    xc = [
        remote(pr.at[0, pl.ds(0, 64)], xa.at[pl.ds(0, 64)], xssem.at[0], xrsem.at[0], right),
        remote(pr.at[0, pl.ds(64, 64)], xa.at[pl.ds(64, 64)], xssem.at[1], xrsem.at[1], left),
        remote(pr.at[1], xf.at[0], xssem.at[2], xrsem.at[2], right),
        remote(pr.at[2], xf.at[1], xssem.at[3], xrsem.at[3], left),
    ]

    piece(0)
    zc[0].start()
    piece(1)
    zc[1].start()
    w_load.wait()
    tokens_part(0)
    piece(2)
    zc[2].start()
    tokens_part(1)
    piece(3)
    zc[3].start()

    def sum_rows(o, extra=None):
        @pl.loop(0, 8)
        def _(n):
            cols = pl.ds(al(n * 512, 512), 512)
            for h in range(2):
                rows = pl.ds(h * 64, 64)
                mine = pl.ds(al(c * ROWS + h * 64, 64), 64)
                total = part[o, mine, cols].astype(F32) + pr[o, rows, cols].astype(F32)
                if extra is not None and extra == h:
                    total += xa[rows, cols].astype(F32)
                pr[o, rows, cols] = total.astype(BF)

    to_sib[0].wait_recv()
    sum_rows(0)
    xc[0].start()
    xc[1].start()
    tokens_part(2)
    tokens_part(3)
    piece(4)
    piece(5)
    piece(6)
    piece(7)
    to_sib[1].wait_recv()
    to_sib[2].wait_recv()
    to_sib[3].wait_recv()
    xc[0].wait_recv()
    sum_rows(1, 0)
    xc[2].start()
    xc[1].wait_recv()
    sum_rows(2, 1)
    xc[3].start()

    def add_piece(o, ab, src):
        @pl.loop(0, 16)
        def _(i):
            rows = pl.ds(al(i * 64, 64), 64)
            total = wp[o, ab, rows].astype(F32) + src[rows].astype(F32)
            wp[o, ab, rows] = total.astype(BF)

    zc[0].wait_recv()
    add_piece(1, 0, za.at[0])
    zc[4].start()
    zc[1].wait_recv()
    add_piece(2, 1, za.at[1])
    zc[5].start()

    xc[2].wait_recv()
    xc[3].wait_recv()

    @pl.loop(0, 8)
    def _(n):
        cols = pl.ds(al(n * 512, 512), 512)
        total = part[3, own, cols].astype(F32) + pr[3, :, cols].astype(F32)
        total += xf[0, :, cols].astype(F32) + xf[1, :, cols].astype(F32)
        gto[:, cols] = total.astype(BF)

    gt_copy = pltpu.make_async_copy(gto, gt_out, lsem.at[2])
    gt_copy.start()

    for i in (2, 3, 4, 5):
        zc[i].wait_recv()
    for ab in range(2):

        @pl.loop(0, 16)
        def _(i):
            rows = pl.ds(al(i * 64, 64), 64)
            total = wp[3, ab, rows].astype(F32) + zf[0, ab, rows].astype(F32) + zf[1, ab, rows].astype(F32)
            wp[3, ab, rows] = total.astype(BF)

    lo, hi = pl.ds(0, 512), pl.ds(512, 512)

    def y_copy(i, src, dst, where):
        return remote(src, dst, yssem.at[i], yrsem.at[i], where)

    give = [
        y_copy(0, wp.at[3, 1 - yh, lo], ya.at[0], above),
        y_copy(1, wp.at[3, 1 - yh, hi], ya.at[1], below),
    ]
    pass_on = [
        y_copy(2, wp.at[3, lax.div(up, 2)], yf.at[0], above),
        y_copy(3, wp.at[3, lax.div(down, 2)], yf.at[1], below),
    ]
    final = remote(fs.at[1], wg_out, yssem.at[4], yrsem.at[4], sib)
    final_own = pltpu.make_async_copy(fs.at[0], wg_out, lsem.at[3])

    @pl.when(c == p)
    def _():
        for cp in give:
            cp.start()
        for cp in pass_on:
            cp.wait_recv()

        @pl.loop(0, 16)
        def _(i):
            rows = pl.ds(al(i * 64, 64), 64)

            def total(cols):
                return (
                    wp[3, yh, rows, cols].astype(F32) + yf[0, rows, cols].astype(F32) + yf[1, rows, cols].astype(F32)
                )

            fs[0, rows] = total(pl.ds(al(c * 256, 256), 256))
            fs[1, rows] = total(pl.ds(al((1 - c) * 256, 256), 256))

        final.start()
        final_own.start()
        for cp in give:
            cp.wait_send()
        final.wait_send()
        final_own.wait()

    @pl.when(c != p)
    def _():
        for i, cp in enumerate(give):
            cp.wait_recv()
            idx = lax.div((up, down)[i], 2)

            @pl.loop(0, 8)
            def _(n):
                part_rows = pl.ds(al(n * 64, 64), 64)
                rows = pl.ds(al(i * 512 + n * 64, 64), 64)
                total = wp[3, idx, rows].astype(F32) + ya[i, part_rows].astype(F32)
                wp[3, idx, rows] = total.astype(BF)

            pass_on[i].start()
        for cp in pass_on:
            cp.wait_send()
        final.wait_recv()

    for cp in to_sib + xc + zc:
        cp.wait_send()
    gt_copy.wait()


def scatter(o, tok, cot, w):
    dma = pltpu.SemaphoreType.DMA
    vm = pltpu.VMEM
    return pl.pallas_call(
        scatter_kernel,
        out_shape=(jax.ShapeDtypeStruct((ROWS, D), BF), jax.ShapeDtypeStruct((1024, 256), F32)),
        in_specs=[ANY] * 4,
        out_specs=(ANY,) * 2,
        scratch_shapes=[
            vm((3, D, 256), BF),
            vm((4, 1024, 256), BF),
            vm((1024, 1024), BF),
            vm((4, CHIP_ROWS, D), BF),
            vm((4, ROWS, D), BF),
            vm((ROWS, D), BF),
            vm((2, ROWS, D), BF),
            vm((4, 2, 1024, 512), BF),
            vm((2, 1024, 512), BF),
            vm((2, 2, 1024, 512), BF),
            vm((2, 4, CHIP_ROWS, 512), BF),
            vm((2, 4, CHIP_ROWS, 512), BF),
            vm((2, 512, 512), BF),
            vm((2, 1024, 512), BF),
            vm((2, 1024, 256), F32),
            vm((ROWS, D), BF),
            dma((4,)), dma((7,)), dma((7,)), dma((4,)), dma((4,)), dma((4,)), dma((4,)),
            dma((6,)), dma((6,)), dma((5,)), dma((5,)), dma((2,)), dma((2,)),
        ],
        compiler_params=pltpu.CompilerParams(
            collective_id=1, has_side_effects=True, vmem_limit_bytes=58 << 20
        ),
        cost_estimate=pl.CostEstimate(flops=15 * 10**9, bytes_accessed=60 << 20, transcendentals=0),
    )(o, tok, cot, w)


def on_device(tokens, cotangent, w_query, w_key, w_value, w_output, global_pos, pattern):
    flags = lax.all_gather(pattern, "seq", axis=1, tiled=True)
    tok, cot, w, r = gather(tokens[0], cotangent[0], w_query, w_key, w_value, w_output)
    x, y, z, c = place()
    doc = lax.div(lax.div(y, 2) * 4 + z, 2) * 2 + lax.rem(y, 2)
    pos = lax.dynamic_index_in_dim(global_pos, doc, 0, keepdims=False)
    flag = lax.dynamic_index_in_dim(flags, doc, 0, keepdims=False).reshape(-1)
    o = attention(flag, pos, r)
    grad_tokens, grads = scatter(o, tok, cot, w)
    return (
        grad_tokens[None],
        grads[:256].T,
        grads[256:512].T,
        grads[512:768].T,
        grads[768:],
    )


def solution(mesh):
    in_specs = (
        P("fsdp", "seq", None),
        P("fsdp", "seq", None),
        P(None, "fsdp"),
        P(None, "fsdp"),
        P(None, "fsdp"),
        P("fsdp", None),
        P(),
        P(None, "seq", None),
    )
    out_specs = (
        P("fsdp", "seq", None),
        P("seq", "fsdp"),
        P("seq", "fsdp"),
        P("seq", "fsdp"),
        P("fsdp", "seq"),
    )
    return jax.shard_map(
        on_device, mesh=mesh, in_specs=in_specs, out_specs=out_specs, check_vma=False
    )
```

```python
import jax
import jax.numpy as jnp
from jax import lax
from jax.experimental import pallas as pl
from jax.experimental.pallas import tpu as pltpu
from jax.sharding import PartitionSpec as P

BLOCK = 64
HDIM = 128
ROWS = 128
CHIP_ROWS = 256
D = 4096
BF = jnp.bfloat16
F32 = jnp.float32
MESH = pl.DeviceIdType.MESH
ANY = pl.BlockSpec(memory_space=pl.ANY)
NT = (((1,), (1,)), ((), ()))
TN = (((0,), (0,)), ((), ()))


def place():
    f = lax.axis_index("fsdp")
    s = lax.axis_index("seq")
    x, p = lax.div(f, 2), lax.rem(f, 2)
    yh, z, c = lax.div(s, 8), lax.rem(lax.div(s, 2), 4), lax.rem(s, 2)
    return x, 2 * yh + p, z, c


def device(x, y, z, c):
    return {"seq": lax.div(y, 2) * 8 + z * 2 + c, "fsdp": x * 2 + lax.rem(y, 2)}


def mod4(v):
    return lax.rem(v + 4, 4)


def al(v, n):
    return pl.multiple_of(v, n)


def remote(src, dst, send, recv, where):
    return pltpu.make_async_remote_copy(
        src_ref=src, dst_ref=dst, send_sem=send, recv_sem=recv, device_id=where, device_id_type=MESH
    )


def meet(devices):
    barrier = pltpu.get_barrier_semaphore()
    for where in devices:
        pl.semaphore_signal(barrier, inc=1, device_id=where, device_id_type=MESH)
    pl.semaphore_wait(barrier, len(devices))


def chip_peer(x, y, z, c, k):
    j = lax.rem(lax.div(y, 2) * 4 + z + k, 8)
    return j, device(x, lax.div(j, 4) * 2 + lax.rem(y, 2), lax.rem(j, 4), c)


HALF_Q, HALF_O = 384, 128


class Reduce:
    def __init__(self, at, rows, bufs, sems):
        self.at, self.rows = at, rows
        self.wz, self.za, self.zf, self.yf, self.wy, self.yg, self.zb, self.zg = bufs
        ss, rs = sems
        half = rows // 2
        lo, hi = pl.ds(0, half), pl.ds(half, half)
        self.lo, self.hi = lo, hi
        wz, za, zf, yf, wy, yg, zb, zg = bufs
        up, down, yh = at["up"], at["down"], at["yh"]
        front, rear, above, below = at["front"], at["rear"], at["above"], at["below"]
        up_i, down_i = lax.div(up, 2), lax.div(down, 2)
        self.up_i, self.down_i, self.yh = up_i, down_i, yh

        def cp(i, src, dst, where):
            return remote(src, dst, ss.at[i], rs.at[i], where)

        self.z = [
            cp(0, wz.at[0, 0], za.at[0], front),
            cp(1, wz.at[0, 1], za.at[1], rear),
            cp(2, wz.at[1, 1], zf.at[0, 1], front),
            cp(3, wz.at[2, 0], zf.at[1, 0], rear),
            cp(4, wz.at[1, 0], zf.at[0, 0], front),
            cp(5, wz.at[2, 1], zf.at[1, 1], rear),
        ]
        self.give = [
            cp(6, wy.at[1 - yh, :, lo], yg.at[0, :, lo], above),
            cp(7, wy.at[1 - yh, :, hi], yg.at[1, :, lo], below),
        ]
        self.free = [
            cp(8, wy.at[up_i, :, hi], yg.at[0, :, hi], above),
            cp(9, wy.at[down_i, :, lo], yg.at[1, :, lo], below),
        ]
        self.dep = [
            cp(6, wy.at[up_i, :, lo], yg.at[0, :, lo], above),
            cp(7, wy.at[down_i, :, hi], yg.at[1, :, hi], below),
        ]
        self.zy_give = [
            cp(10, wz.at[3, 1 - yh, lo], yf.at[0, lo], above),
            cp(11, wz.at[3, 1 - yh, hi], yf.at[1, lo], below),
        ]
        self.zy_pass = [
            cp(12, wz.at[3, up_i], yf.at[0], above),
            cp(13, wz.at[3, down_i], yf.at[1], below),
        ]
        self.yz = [
            cp(14, wy.at[yh, 0, lo], zb.at[0], front),
            cp(15, wy.at[yh, 0, hi], zb.at[1], rear),
            cp(16, wy.at[yh, 1], zg.at[0], front),
            cp(17, wy.at[yh, 2], zg.at[1], rear),
        ]

    def add(self, rows, dst, *srcs):
        @pl.loop(0, rows // 64)
        def _(i):
            r = pl.ds(al(i * 64, 64), 64)
            total = dst[r].astype(F32)
            for s in srcs:
                total += s[r].astype(F32)
            dst[r] = total.astype(BF)

    def start_y(self):
        @pl.when(self.at["owner"])
        def _():
            for cp in self.give:
                cp.start()

        @pl.when(self.at["middle"])
        def _():
            for cp in self.free:
                cp.start()

    def dep_z(self):
        self.z[0].wait_recv()
        self.add(self.rows, self.wz.at[1, 0], self.za.at[0])
        self.z[4].start()
        self.z[1].wait_recv()
        self.add(self.rows, self.wz.at[2, 1], self.za.at[1])
        self.z[5].start()

    def dep_y(self):
        half = self.rows // 2

        @pl.when(self.at["middle"])
        def _():
            for i, (idx, part) in enumerate(((self.up_i, self.lo), (self.down_i, self.hi))):
                self.give[i].wait_recv()
                for o in range(4):
                    self.add(half, self.wy.at[idx, o, part], self.yg.at[i, o, self.lo])
                self.dep[i].start()

    def mid_z(self):
        for i in (2, 3, 4, 5):
            self.z[i].wait_recv()
        for ab in range(2):
            self.add(self.rows, self.wz.at[3, ab], self.zf.at[0, ab], self.zf.at[1, ab])

        @pl.when(self.at["owner"])
        def _():
            for cp in self.zy_give:
                cp.start()

    def mid_y(self):
        @pl.when(self.at["owner"])
        def _():
            for cp in self.free + self.dep:
                cp.wait_recv()
            for cp in self.give:
                cp.wait_send()
            for o in range(4):
                self.add(self.rows, self.wy.at[self.yh, o], self.yg.at[0, o], self.yg.at[1, o])
                if o == 0:
                    self.yz[0].start()
                    self.yz[1].start()

    def last_z(self):
        half = self.rows // 2

        @pl.when(self.at["middle"])
        def _():
            for i, (idx, part) in enumerate(((self.up_i, self.lo), (self.down_i, self.hi))):
                self.zy_give[i].wait_recv()
                self.add(half, self.wz.at[3, idx, part], self.yf.at[i, self.lo])
                self.zy_pass[i].start()

    def last_y(self):
        half = self.rows // 2

        @pl.when(self.at["owner"])
        def _():
            self.yz[0].wait_recv()
            self.add(half, self.wy.at[self.yh, 1, self.lo], self.zb.at[0])
            self.yz[2].start()
            self.yz[1].wait_recv()
            self.add(half, self.wy.at[self.yh, 2, self.hi], self.zb.at[1])
            self.yz[3].start()

    def result(self, put):
        for cp in self.zy_pass:
            cp.wait_recv()
        for n in range(self.rows // 128):
            rows = pl.ds(n * 128, 128)
            put(0, n, lambda cols: (
                self.wz[3, self.yh, rows, cols].astype(F32)
                + self.yf[0, rows, cols].astype(F32) + self.yf[1, rows, cols].astype(F32)))
        for cp in self.yz[2:]:
            cp.wait_recv()
        for n in range(self.rows // 128):
            rows = pl.ds(n * 128, 128)
            put(1, n, lambda cols: (
                self.wy[self.yh, 3, rows, cols].astype(F32)
                + self.zg[0, rows, cols].astype(F32) + self.zg[1, rows, cols].astype(F32)))

    def drain(self):
        for cp in self.z:
            cp.wait_send()

        @pl.when(self.at["owner"])
        def _():
            for cp in self.zy_give + self.yz:
                cp.wait_send()

        @pl.when(self.at["middle"])
        def _():
            for cp in self.free + self.dep + self.zy_pass:
                cp.wait_send()


def reduce_scratch(rows):
    vm = pltpu.VMEM
    return [
        vm((4, 2, rows, 512), BF), vm((2, rows, 512), BF), vm((2, 2, rows, 512), BF), vm((2, rows, 512), BF),
        vm((2, 4, rows, 512), BF), vm((2, 4, rows, 512), BF), vm((2, rows // 2, 512), BF), vm((2, rows, 512), BF),
        pltpu.SemaphoreType.DMA((18,)), pltpu.SemaphoreType.DMA((18,)),
    ]


def kernel(
    pat, gpos, tok_in, cot_in, wq, wk, wv, wo,
    gt_out, gq_out, gk_out, gv_out, go_out,
    tok, cot, w, wov, r, g, gt, mask, masks, kg, vg, dkg, dvg, dkp, dvp, pr, xa, xf, fs,
    *rest,
):
    o_bufs, o_sems, q_bufs, q_sems = rest[:8], rest[8:10], rest[10:18], rest[18:20]
    (ssem, rsem, wssem, wrsem, lsem, mssem, mrsem, assem, arsem, bssem, brsem,
     cssem, crsem, dssem, drsem, essem, ersem, sssem, srsem, xssem, xrsem, fssem, frsem, flsem) = rest[20:]
    x, y, z, c = place()
    p, yh = lax.rem(y, 2), lax.div(y, 2)
    seq = lax.axis_index("seq")
    xr, xl, x2 = mod4(x + 1), mod4(x - 1), mod4(x + 2)
    zr, zl, z2 = mod4(z + 1), mod4(z - 1), mod4(z + 2)
    up, down = mod4(y + 1), mod4(y - 1)
    right, left = device(xr, y, z, c), device(xl, y, z, c)
    sib = device(x, y, z, 1 - c)
    me = yh * 4 + z
    my_doc = lax.div(me, 2) * 2 + p
    peers = [chip_peer(x, y, z, c, k) for k in range(1, 8)]

    kb = lax.div(lax.broadcasted_iota(jnp.int32, (8, 256), 1), 64)
    upper = lax.broadcasted_iota(jnp.int32, (8, 256), 0) == 0

    @pl.loop(0, 8)
    def _(d):
        prev0 = jnp.where(seq > 0, pat[d, 0, 0], 0)
        next0, prev1 = pat[d, 0, 1], pat[d, 1, 0]
        next1 = jnp.where(seq < 15, pat[d, 1, 1], 0)
        m0 = jnp.where(kb == 0, prev0, jnp.where(kb == 1, 1, jnp.where(kb == 2, next0, 0)))
        m1 = jnp.where(kb == 0, 0, jnp.where(kb == 1, prev1, jnp.where(kb == 2, 1, next1)))
        mask[c, d] = jnp.where(jnp.where(upper, m0, m1) == 1, 0.0, -jnp.inf)

    for t in (1, 2):
        r[t, :BLOCK] = jnp.zeros((BLOCK, HDIM), BF)
        r[t, BLOCK + 2048 :] = jnp.zeros((BLOCK, HDIM), BF)

    meet(
        [right, left, sib]
        + [device(x, v, z, core) for v in (up, down) for core in (0, 1)]
        + [where for _, where in peers]
    )
    own = pl.ds(al(c * ROWS, ROWS), ROWS)
    other = pl.ds(al((1 - c) * ROWS, ROWS), ROWS)
    first = pl.ds(al(c * ROWS, 64), 64)
    second = pl.ds(al(c * ROWS + 64, 64), 64)

    def sends(a, given, buf):
        def cp(kind, src, dst, where):
            return remote(src, dst, ssem.at[a, kind], rsem.at[a, kind], where)

        return [
            cp(0, given, buf.at[x, own], right),
            cp(1, given, buf.at[x, own], left),
            cp(2, given, buf.at[x, own], sib),
            cp(3, buf.at[xl, first], buf.at[xl, first], right),
            cp(4, buf.at[xr, second], buf.at[xr, second], left),
            cp(5, buf.at[xl, own], buf.at[xl, own], sib),
            cp(6, buf.at[xr, own], buf.at[xr, own], sib),
            cp(7, buf.at[x2, first], buf.at[x2, first], sib),
            cp(8, buf.at[x2, second], buf.at[x2, second], sib),
        ]

    tsend = sends(0, tok_in, tok)
    csend = sends(1, cot_in, cot)
    wdev = device(x, mod4(y + 1 + 2 * c), z, p)
    half = pl.ds(al(c * 2048, 2048), 2048)
    half_o = pl.ds(al(c * 128, 128), 128)
    wsend = [
        remote(src.at[half], w.at[t, half], wssem.at[t], wrsem.at[t, c], wdev)
        for t, src in enumerate((wq, wk, wv))
    ]
    wsend.append(remote(wo.at[half_o], wov.at[half_o], wssem.at[3], wrsem.at[3, c], wdev))
    wlocal = [pltpu.make_async_copy(src, w.at[t], lsem.at[t]) for t, src in enumerate((wq, wk, wv))]
    wlocal.append(pltpu.make_async_copy(wo, wov, lsem.at[3]))
    tlocal = pltpu.make_async_copy(tok_in, tok.at[x, own], lsem.at[4])
    clocal = pltpu.make_async_copy(cot_in, cot.at[x, own], lsem.at[5])

    for k in (0, 1, 2):
        tsend[k].start()
    for cp in wsend:
        cp.start()
    tlocal.start()
    clocal.start()

    @pl.when(c == p)
    def _():
        for cp in wlocal:
            cp.start()

    mask_sib = remote(mask.at[c], mask.at[c], mssem.at[7], mrsem.at[7], sib)
    mask_sib.start()
    mask_sib.wait()
    mask_out = [
        remote(mask.at[:, lax.div(j, 2) * 2 + p], masks.at[me], mssem.at[k], mrsem.at[k], where)
        for k, (j, where) in enumerate(peers)
    ]
    for cp in mask_out:
        cp.start()
    mask_own = pltpu.make_async_copy(mask.at[:, my_doc], masks.at[me], lsem.at[8])
    mask_own.start()

    def relay(copies):
        copies[0].wait_recv()
        copies[3].start()
        copies[5].start()
        copies[1].wait_recv()
        copies[4].start()
        copies[6].start()

    relay(tsend)
    for k in (0, 1, 2):
        csend[k].start()
    tsend[3].wait_recv()
    tsend[7].start()
    tsend[4].wait_recv()
    tsend[8].start()
    tlocal.wait()
    clocal.wait()

    def weights_here(ts):
        @pl.when(c == p)
        def _():
            for t in ts:
                wlocal[t].wait()

        @pl.when(c != p)
        def _():
            for t in ts:
                for h in (0, 1):
                    if t < 3:
                        ref = w.at[t, pl.ds(h * 2048, 2048)]
                    else:
                        ref = wov.at[pl.ds(h * 128, 128)]
                    remote(ref, ref, wssem.at[t], wrsem.at[t, h], sib).wait_recv()

    weights_here((0, 1, 2))
    for k in (2, 5, 6, 7, 8):
        tsend[k].wait_recv()

    def box(j, t):
        return gt.at[t, :, pl.ds(al(j * HDIM, HDIM), HDIM)]

    @pl.loop(0, 4)
    def _(doc):
        @pl.loop(0, 3)
        def _(t):
            got = jnp.dot(tok[doc], w[t], preferred_element_type=F32).astype(BF)
            gt[t, :, pl.ds(al(doc * 256, 256), 256)] = got

    mine = pl.ds(al(me * CHIP_ROWS + BLOCK, 64), CHIP_ROWS)

    def boxes(j, t0, n):
        return gt.at[pl.ds(t0, n), :, pl.ds(al(j * HDIM, HDIM), HDIM)]

    qkv = [
        remote(boxes(j, 0, 3), r.at[pl.ds(0, 3), mine], assem.at[k], arsem.at[k], where)
        for k, (j, where) in enumerate(peers)
    ]
    for cp in qkv:
        cp.start()
    qkv_own = pltpu.make_async_copy(boxes(me, 0, 3), r.at[pl.ds(0, 3), mine], lsem.at[6])
    qkv_own.start()

    relay(csend)
    weights_here((3,))

    def back(doc):
        got = lax.dot_general(cot[doc], wov[...], NT, preferred_element_type=F32).astype(BF)
        gt[3, :, pl.ds(al(doc * 256, 256), 256)] = got
        for h in (0, 1):
            j = 2 * doc + h
            where = device(x, lax.div(j, 4) * 2 + p, lax.rem(j, 4), c)

            @pl.when(j != me)
            def _():
                remote(box(j, 3), r.at[3, mine], bssem.at[j], brsem.at[me], where).start()

            @pl.when(j == me)
            def _():
                pltpu.make_async_copy(box(j, 3), r.at[3, mine], lsem.at[7]).start()

    csend[2].wait_recv()
    back(x)

    for cp in qkv:
        cp.wait()
    qkv_own.wait()
    for cp in mask_out:
        cp.wait()
    mask_own.wait()
    scale = HDIM**-0.5
    pos = jnp.broadcast_to(gpos[pl.ds(my_doc, 1), :], (128, 128))
    pos_t = pos.T
    lane = lax.broadcasted_iota(jnp.int32, (128, 128), 1)
    sub = lax.broadcasted_iota(jnp.int32, (128, 128), 0)
    low = lax.broadcasted_iota(jnp.int32, (128, 256), 0) < BLOCK

    def nt(a, b):
        return lax.dot_general(a, b, NT, preferred_element_type=F32)

    def tn(a, b):
        return lax.dot_general(a, b, TN, preferred_element_type=F32)

    def mm(a, b):
        return jnp.dot(a, b, preferred_element_type=F32)

    dkg[...] = jnp.zeros_like(dkg)
    dvg[...] = jnp.zeros_like(dvg)

    @pl.loop(0, 16)
    def _(i):
        rows = pl.ds(al(i * 128 + BLOCK, 64), 128)
        pick = (pos_t == i * 128 + lane).astype(F32).astype(BF)
        dkg[...] += mm(pick, r[1, rows])
        dvg[...] += mm(pick, r[2, rows])

    kg[...] = dkg[...].astype(BF)
    vg[...] = dvg[...].astype(BF)
    wz, wy = q_bufs[0], q_bufs[4]

    def saved(i):
        return (lax.div(i, 6), lax.rem(lax.div(i, 3), 2), pl.ds(al(lax.rem(i, 3) * 128, 128), 128))

    @pl.loop(0, 16)
    def _(i):
        rows = pl.ds(al(i * 128 + BLOCK, 64), 128)
        win = pl.ds(al(i * 128, 128), 256)
        q, k, v = r[0, rows], r[1, win], r[2, win]
        seen = masks[lax.div(i, 2), lax.rem(i, 2)]
        bias = jnp.where(low, seen[0:1], seen[1:2])
        sl = nt(q, k) * scale + bias
        sg = nt(q, kg[...]) * scale
        top = jnp.maximum(sl.max(-1, keepdims=True), sg.max(-1, keepdims=True))
        el, eg = jnp.exp(sl - top), jnp.exp(sg - top)
        inv = 1.0 / (el.sum(-1, keepdims=True) + eg.sum(-1, keepdims=True))
        plb, pgb = (el * inv).astype(BF), (eg * inv).astype(BF)
        a, b, rr = saved(i)
        wz[a, b, rr, pl.ds(0, 256)] = plb
        wz[a, b, rr, pl.ds(256, 128)] = pgb
        ctx = mm(plb, v) + mm(pgb, vg[...])
        j = lax.div(i, 2)
        wy[lax.div(j, 4), lax.rem(j, 4), pl.ds(al(lax.rem(i, 2) * 128, 128), 128), pl.ds(0, 128)] = ctx.astype(BF)

    def ctx_box(j):
        return wy.at[lax.div(j, 4), lax.rem(j, 4), pl.ds(0, 256), pl.ds(0, 128)]

    def spot(t0, n):
        rows = pl.ds(al(lax.div(me, 2) * CHIP_ROWS, CHIP_ROWS), CHIP_ROWS)
        return g.at[pl.ds(t0, n), rows, pl.ds(al(lax.rem(me, 2) * HDIM, HDIM), HDIM)]

    def spot_o():
        rows = pl.ds(al(lax.div(me, 2) * CHIP_ROWS, CHIP_ROWS), CHIP_ROWS)
        return g.at[3, rows, pl.ds(al(lax.rem(me, 2) * HDIM, HDIM), HDIM)]

    ctx_out = [
        remote(ctx_box(j), spot_o(), cssem.at[k], crsem.at[k], where) for k, (j, where) in enumerate(peers)
    ]
    for cp in ctx_out:
        cp.start()
    ctx_own = pltpu.make_async_copy(ctx_box(me), spot_o(), lsem.at[9])
    ctx_own.start()

    csend[5].wait_recv()
    back(xl)
    csend[6].wait_recv()
    back(xr)
    csend[3].wait_recv()
    csend[7].start()
    csend[4].wait_recv()
    csend[8].start()
    csend[7].wait_recv()
    csend[8].wait_recv()
    back(x2)

    at = {
        "up": up, "down": down, "yh": yh, "owner": c == p, "middle": c != p,
        "front": device(x, y, zr, c), "rear": device(x, y, zl, c),
        "above": device(x, up, z, c), "below": device(x, down, z, c),
    }
    groups = (z2, zr, zl, z)
    order = [(0, 0), (0, 1), (1, 1), (2, 0), (1, 0), (2, 1), (3, 0), (3, 1)]
    red_o = Reduce(at, HALF_O, o_bufs, o_sems)
    red_q = Reduce(at, HALF_Q, q_bufs, q_sems)

    def turn(t):
        for i in range(4):
            rows = pl.ds(i * 256, 256)
            gt[t, :, rows] = g[t, rows].T

    def piece(red, src, n, t0, count):
        o, ab = order[n]
        cols = pl.ds(al(ab * 2048 + groups[o] * 512, 512), 512)

        @pl.loop(0, count)
        def _(t):
            right_side = src[:, :, cols].reshape(1024, 512)
            acc = mm(gt[t0 + t], right_side).astype(BF)
            rows = pl.ds(al(t * 128, 128), 128)
            red.wz[o, ab, rows] = acc[:128]
            red.wy[ab, o, rows] = acc[128:]

        if n < 4:
            red.z[n].start()

    for j in range(8):

        @pl.when(j != me)
        def _():
            remote(box(j, 3), r.at[3, mine], bssem.at[j], brsem.at[j], sib).wait_send()

    pltpu.make_async_copy(box(me, 3), r.at[3, mine], lsem.at[7]).wait()
    for cp in ctx_out:
        cp.wait()
    ctx_own.wait()
    turn(3)
    for n in range(8):
        piece(red_o, cot, n, 3, 1)
    red_o.start_y()

    for j in range(8):

        @pl.when(j != me)
        def _():
            remote(box(j, 3), r.at[3, mine], bssem.at[j], brsem.at[j], sib).wait_recv()

    dkp[...] = jnp.zeros_like(dkp)
    dvp[...] = jnp.zeros_like(dvp)
    dkg[...] = jnp.zeros_like(dkg)
    dvg[...] = jnp.zeros_like(dvg)

    def out_box(i, t):
        j = lax.div(i, 2)
        return (t, pl.ds(al(lax.rem(i, 2) * 128, 128), 128), pl.ds(al(j * 128, 128), 128))

    @pl.loop(0, 16)
    def _(i):
        rows = pl.ds(al(i * 128 + BLOCK, 64), 128)
        win = pl.ds(al(i * 128, 128), 256)
        q, do, k, v = r[0, rows], r[3, rows], r[1, win], r[2, win]
        a, b, rr = saved(i)
        plb, pgb = wz[a, b, rr, pl.ds(0, 256)], wz[a, b, rr, pl.ds(256, 128)]
        dl, dg = nt(do, v), nt(do, vg[...])
        pf, pgf = plb.astype(F32), pgb.astype(F32)
        delta = (pf * dl).sum(-1, keepdims=True) + (pgf * dg).sum(-1, keepdims=True)
        sl = (pf * (dl - delta) * scale).astype(BF)
        sg = (pgf * (dg - delta) * scale).astype(BF)
        gt[out_box(i, 0)] = (mm(sl, k) + mm(sg, kg[...])).astype(BF)
        dkp[win] += tn(sl, q)
        dvp[win] += tn(plb, do)
        dkg[...] += tn(sg, q)
        dvg[...] += tn(pgb, do)

    def home(sems, t0, n):
        s, d = sems
        return [
            remote(boxes(j, t0, n), spot(t0, n), s.at[k], d.at[k], where) for k, (j, where) in enumerate(peers)
        ]

    home_q = home((dssem, drsem), 0, 1)
    for cp in home_q:
        cp.start()
    home_q_own = pltpu.make_async_copy(boxes(me, 0, 1), spot(0, 1), lsem.at[10])
    home_q_own.start()

    def split(a):
        high = a.astype(BF)
        return high, (a - high.astype(F32)).astype(BF)

    both = jnp.concatenate([jnp.concatenate(split(dkg[...]), 0), jnp.concatenate(split(dvg[...]), 0)], 1)

    @pl.loop(0, 16)
    def _(i):
        inner = pl.ds(al(i * 128 + BLOCK, 64), 128)
        put = (pos == i * 128 + sub).astype(F32).astype(BF)
        extra = mm(jnp.concatenate([put, put], 1), both)
        gt[out_box(i, 1)] = (dkp[inner] + extra[:, :128]).astype(BF)
        gt[out_box(i, 2)] = (dvp[inner] + extra[:, 128:]).astype(BF)

    home_kv = home((essem, ersem), 1, 2)
    for cp in home_kv:
        cp.start()
    home_kv_own = pltpu.make_async_copy(boxes(me, 1, 2), spot(1, 2), lsem.at[11])
    home_kv_own.start()

    red_o.dep_z()
    red_o.dep_y()
    for cp in tsend + csend + wsend:
        cp.wait_send()
    for cp in home_q + home_kv:
        cp.wait()
    home_q_own.wait()
    home_kv_own.wait()

    part = cot
    docs = (x2, xr, xl, x)
    to_sib = [remote(part.at[o, other], pr.at[o], sssem.at[o], srsem.at[o], sib) for o in range(4)]

    def tokens_part(o):
        rows = pl.ds(al(docs[o] * CHIP_ROWS, CHIP_ROWS), CHIP_ROWS)

        @pl.loop(0, 8)
        def _(n):
            cols = pl.ds(al(n * 512, 512), 512)
            a = jnp.concatenate([g[t, rows] for t in range(3)], 1)
            b = jnp.concatenate([w[t, cols] for t in range(3)], 1)
            part[o, :, cols] = nt(a, b).astype(BF)

        to_sib[o].start()

    xc = [
        remote(pr.at[0, pl.ds(0, 64)], xa.at[pl.ds(0, 64)], xssem.at[0], xrsem.at[0], right),
        remote(pr.at[0, pl.ds(64, 64)], xa.at[pl.ds(64, 64)], xssem.at[1], xrsem.at[1], left),
        remote(pr.at[1], xf.at[0], xssem.at[2], xrsem.at[2], right),
        remote(pr.at[2], xf.at[1], xssem.at[3], xrsem.at[3], left),
    ]

    def sum_rows(o, extra=None):
        @pl.loop(0, 8)
        def _(n):
            cols = pl.ds(al(n * 512, 512), 512)
            for h in range(2):
                rows = pl.ds(h * 64, 64)
                own_half = pl.ds(al(c * ROWS + h * 64, 64), 64)
                total = part[o, own_half, cols].astype(F32) + pr[o, rows, cols].astype(F32)
                if extra is not None and extra == h:
                    total += xa[rows, cols].astype(F32)
                pr[o, rows, cols] = total.astype(BF)

    tokens_part(0)
    for t in range(3):
        turn(t)
    for n in range(4):
        piece(red_q, tok, n, 0, 3)
    to_sib[0].wait_recv()
    sum_rows(0)
    xc[0].start()
    xc[1].start()
    for n in range(4, 8):
        piece(red_q, tok, n, 0, 3)
    red_q.start_y()
    for o in (1, 2, 3):
        tokens_part(o)
    red_q.dep_z()
    red_o.mid_z()
    red_o.mid_y()
    to_sib[1].wait_recv()
    xc[0].wait_recv()
    sum_rows(1, 0)
    xc[2].start()
    to_sib[2].wait_recv()
    xc[1].wait_recv()
    sum_rows(2, 1)
    xc[3].start()
    red_q.dep_y()
    red_o.last_z()
    red_o.last_y()
    to_sib[3].wait_recv()
    red_q.mid_z()
    red_q.mid_y()

    xc[2].wait_recv()
    xc[3].wait_recv()

    to_sib[3].wait_send()

    @pl.loop(0, 8)
    def _(n):
        cols = pl.ds(al(n * 512, 512), 512)
        total = part[3, own, cols].astype(F32) + pr[3, :, cols].astype(F32)
        total += xf[0, :, cols].astype(F32) + xf[1, :, cols].astype(F32)
        part[3, other, cols] = total.astype(BF)

    gt_copy = pltpu.make_async_copy(part.at[3, other], gt_out, lsem.at[12])
    gt_copy.start()
    red_q.last_z()
    red_q.last_y()

    outs = (gq_out, gk_out, gv_out, go_out)
    final = [remote(fs.at[1, t], outs[t], fssem.at[t], frsem.at[t], sib) for t in range(4)]
    final_own = [pltpu.make_async_copy(fs.at[0, t], outs[t], flsem.at[t]) for t in range(4)]

    @pl.when(c == p)
    def _():
        def put(t0):
            def run(head, n, value):
                lanes = pl.ds(head * 128, 128)
                for s in range(2):
                    core = c if s == 0 else 1 - c
                    got = value(pl.ds(al(core * 256, 256), 256))
                    if t0 + n < 3:
                        fs[s, n, :, lanes] = got.T
                    else:
                        fs[s, 3, lanes, :] = got

            return run

        red_o.result(put(3))
        final[3].start()
        final_own[3].start()
        red_q.result(put(0))
        for t in range(3):
            final[t].start()
            final_own[t].start()
        for t in range(4):
            final[t].wait_send()
            final_own[t].wait()

    @pl.when(c != p)
    def _():
        for cp in final:
            cp.wait_recv()

    red_o.drain()
    red_q.drain()
    for cp in to_sib[:3] + xc:
        cp.wait_send()
    gt_copy.wait()


def on_device(tokens, cotangent, w_query, w_key, w_value, w_output, global_pos, pattern):
    dma = pltpu.SemaphoreType.DMA
    vm = pltpu.VMEM
    square = jax.ShapeDtypeStruct((256, 256), F32)
    grad_tokens, gq, gk, gv, go = pl.pallas_call(
        kernel,
        out_shape=(jax.ShapeDtypeStruct((ROWS, D), BF), square, square, square, square),
        in_specs=[pl.BlockSpec(memory_space=pltpu.SMEM), pl.BlockSpec(memory_space=pltpu.VMEM)] + [ANY] * 6,
        out_specs=(ANY,) * 5,
        scratch_shapes=[
            vm((4, CHIP_ROWS, D), BF),
            vm((4, CHIP_ROWS, D), BF),
            vm((3, D, 256), BF),
            vm((256, D), BF),
            vm((4, 2176, HDIM), BF),
            vm((4, 1024, 256), BF),
            vm((4, 256, 1024), BF),
            vm((2, 8, 8, 256), F32),
            vm((8, 2, 8, 256), F32),
            vm((128, HDIM), BF), vm((128, HDIM), BF), vm((128, HDIM), F32), vm((128, HDIM), F32),
            vm((2176, HDIM), F32), vm((2176, HDIM), F32),
            vm((4, ROWS, D), BF),
            vm((ROWS, D), BF),
            vm((2, ROWS, D), BF),
            vm((2, 4, 256, 256), F32),
            *reduce_scratch(HALF_O),
            *reduce_scratch(HALF_Q),
            dma((2, 9)), dma((2, 9)), dma((4,)), dma((4, 2)), dma((13,)), dma((8,)), dma((8,)),
            dma((7,)), dma((7,)), dma((8,)), dma((8,)), dma((7,)), dma((7,)), dma((7,)), dma((7,)),
            dma((7,)), dma((7,)), dma((4,)), dma((4,)), dma((4,)), dma((4,)), dma((4,)), dma((4,)), dma((4,)),
        ],
        compiler_params=pltpu.CompilerParams(
            collective_id=0, has_side_effects=True, vmem_limit_bytes=63 << 20
        ),
        cost_estimate=pl.CostEstimate(flops=25 * 10**9, bytes_accessed=60 << 20, transcendentals=10**6),
    )(pattern, global_pos, tokens[0], cotangent[0], w_query, w_key, w_value, w_output)
    return grad_tokens[None], gq, gk, gv, go


def solution(mesh):
    in_specs = (
        P("fsdp", "seq", None),
        P("fsdp", "seq", None),
        P(None, "fsdp"),
        P(None, "fsdp"),
        P(None, "fsdp"),
        P("fsdp", None),
        P(),
        P(None, "seq", None),
    )
    out_specs = (
        P("fsdp", "seq", None),
        P("seq", "fsdp"),
        P("seq", "fsdp"),
        P("seq", "fsdp"),
        P("fsdp", "seq"),
    )
    return jax.shard_map(
        on_device, mesh=mesh, in_specs=in_specs, out_specs=out_specs, check_vma=False
    )
```

```python
import jax
import jax.numpy as jnp
from jax import lax
from jax.experimental import pallas as pl
from jax.experimental.pallas import tpu as pltpu
from jax.sharding import PartitionSpec as P

BLOCK = 64
HDIM = 128
ROWS = 128
CHIP_ROWS = 256
D = 4096
BF = jnp.bfloat16
F32 = jnp.float32
MESH = pl.DeviceIdType.MESH
ANY = pl.BlockSpec(memory_space=pl.ANY)
NT = (((1,), (1,)), ((), ()))
TN = (((0,), (0,)), ((), ()))


def place():
    f = lax.axis_index("fsdp")
    s = lax.axis_index("seq")
    x, p = lax.div(f, 2), lax.rem(f, 2)
    yh, z, c = lax.div(s, 8), lax.rem(lax.div(s, 2), 4), lax.rem(s, 2)
    return x, 2 * yh + p, z, c


def device(x, y, z, c):
    return {"seq": lax.div(y, 2) * 8 + z * 2 + c, "fsdp": x * 2 + lax.rem(y, 2)}


def mod4(v):
    return lax.rem(v + 4, 4)


def al(v, n):
    return pl.multiple_of(v, n)


def remote(src, dst, send, recv, where):
    return pltpu.make_async_remote_copy(
        src_ref=src, dst_ref=dst, send_sem=send, recv_sem=recv, device_id=where, device_id_type=MESH
    )


def meet(devices):
    barrier = pltpu.get_barrier_semaphore()
    for where in devices:
        pl.semaphore_signal(barrier, inc=1, device_id=where, device_id_type=MESH)
    pl.semaphore_wait(barrier, len(devices))


def chip_peer(x, y, z, c, k):
    j = lax.rem(lax.div(y, 2) * 4 + z + k, 8)
    return j, device(x, lax.div(j, 4) * 2 + lax.rem(y, 2), lax.rem(j, 4), c)


HALF_KV, HALF_Q, HALF_O = 256, 128, 128


class Reduce:
    def __init__(self, at, rows, bufs, sems):
        self.at, self.rows = at, rows
        self.wz, self.za, self.zf, self.yf, self.wy, self.yg, self.zb, self.zg = bufs
        ss, rs = sems
        half = rows // 2
        lo, hi = pl.ds(0, half), pl.ds(half, half)
        self.lo, self.hi = lo, hi
        wz, za, zf, yf, wy, yg, zb, zg = bufs
        up, down, yh = at["up"], at["down"], at["yh"]
        front, rear, above, below = at["front"], at["rear"], at["above"], at["below"]
        up_i, down_i = lax.div(up, 2), lax.div(down, 2)
        self.up_i, self.down_i, self.yh = up_i, down_i, yh

        def cp(i, src, dst, where):
            return remote(src, dst, ss.at[i], rs.at[i], where)

        self.z = [
            cp(0, wz.at[0, 0], za.at[0], front),
            cp(1, wz.at[0, 1], za.at[1], rear),
            cp(2, wz.at[1, 1], zf.at[0, 1], front),
            cp(3, wz.at[2, 0], zf.at[1, 0], rear),
            cp(4, wz.at[1, 0], zf.at[0, 0], front),
            cp(5, wz.at[2, 1], zf.at[1, 1], rear),
        ]
        self.give = [
            cp(6, wy.at[1 - yh, :, lo], yg.at[0, :, lo], above),
            cp(7, wy.at[1 - yh, :, hi], yg.at[1, :, lo], below),
        ]
        self.free = [
            cp(8, wy.at[up_i, :, hi], yg.at[0, :, hi], above),
            cp(9, wy.at[down_i, :, lo], yg.at[1, :, lo], below),
        ]
        self.dep = [
            cp(6, wy.at[up_i, :, lo], yg.at[0, :, lo], above),
            cp(7, wy.at[down_i, :, hi], yg.at[1, :, hi], below),
        ]
        self.zy_give = [
            cp(10, wz.at[3, 1 - yh, lo], yf.at[0, lo], above),
            cp(11, wz.at[3, 1 - yh, hi], yf.at[1, lo], below),
        ]
        self.zy_pass = [
            cp(12, wz.at[3, up_i], yf.at[0], above),
            cp(13, wz.at[3, down_i], yf.at[1], below),
        ]
        self.yz = [
            cp(14, wy.at[yh, 0, lo], zb.at[0], front),
            cp(15, wy.at[yh, 0, hi], zb.at[1], rear),
            cp(16, wy.at[yh, 1], zg.at[0], front),
            cp(17, wy.at[yh, 2], zg.at[1], rear),
        ]

    def add(self, rows, dst, *srcs):
        @pl.loop(0, rows // 64)
        def _(i):
            r = pl.ds(al(i * 64, 64), 64)
            total = dst[r].astype(F32)
            for s in srcs:
                total += s[r].astype(F32)
            dst[r] = total.astype(BF)

    def start_y(self):
        @pl.when(self.at["owner"])
        def _():
            for cp in self.give:
                cp.start()

        @pl.when(self.at["middle"])
        def _():
            for cp in self.free:
                cp.start()

    def dep_z(self):
        self.z[0].wait_recv()
        self.add(self.rows, self.wz.at[1, 0], self.za.at[0])
        self.z[4].start()
        self.z[1].wait_recv()
        self.add(self.rows, self.wz.at[2, 1], self.za.at[1])
        self.z[5].start()

    def dep_y(self):
        half = self.rows // 2

        @pl.when(self.at["middle"])
        def _():
            for i, (idx, part) in enumerate(((self.up_i, self.lo), (self.down_i, self.hi))):
                self.give[i].wait_recv()
                for o in range(4):
                    self.add(half, self.wy.at[idx, o, part], self.yg.at[i, o, self.lo])
                self.dep[i].start()

    def mid_z(self):
        for i in (2, 3, 4, 5):
            self.z[i].wait_recv()
        for ab in range(2):
            self.add(self.rows, self.wz.at[3, ab], self.zf.at[0, ab], self.zf.at[1, ab])

        @pl.when(self.at["owner"])
        def _():
            for cp in self.zy_give:
                cp.start()

    def mid_y(self):
        @pl.when(self.at["owner"])
        def _():
            for cp in self.free + self.dep:
                cp.wait_recv()
            for cp in self.give:
                cp.wait_send()
            for o in range(4):
                self.add(self.rows, self.wy.at[self.yh, o], self.yg.at[0, o], self.yg.at[1, o])
                if o == 0:
                    self.yz[0].start()
                    self.yz[1].start()

    def last_z(self):
        half = self.rows // 2

        @pl.when(self.at["middle"])
        def _():
            for i, (idx, part) in enumerate(((self.up_i, self.lo), (self.down_i, self.hi))):
                self.zy_give[i].wait_recv()
                self.add(half, self.wz.at[3, idx, part], self.yf.at[i, self.lo])
                self.zy_pass[i].start()

    def last_y(self):
        half = self.rows // 2

        @pl.when(self.at["owner"])
        def _():
            self.yz[0].wait_recv()
            self.add(half, self.wy.at[self.yh, 1, self.lo], self.zb.at[0])
            self.yz[2].start()
            self.yz[1].wait_recv()
            self.add(half, self.wy.at[self.yh, 2, self.hi], self.zb.at[1])
            self.yz[3].start()

    def result(self, put):
        for cp in self.zy_pass:
            cp.wait_recv()
        for n in range(self.rows // 128):
            rows = pl.ds(n * 128, 128)
            put(0, n, lambda cols: (
                self.wz[3, self.yh, rows, cols].astype(F32)
                + self.yf[0, rows, cols].astype(F32) + self.yf[1, rows, cols].astype(F32)))
        for cp in self.yz[2:]:
            cp.wait_recv()
        for n in range(self.rows // 128):
            rows = pl.ds(n * 128, 128)
            put(1, n, lambda cols: (
                self.wy[self.yh, 3, rows, cols].astype(F32)
                + self.zg[0, rows, cols].astype(F32) + self.zg[1, rows, cols].astype(F32)))

    def drain(self):
        for cp in self.z:
            cp.wait_send()

        @pl.when(self.at["owner"])
        def _():
            for cp in self.zy_give + self.yz:
                cp.wait_send()

        @pl.when(self.at["middle"])
        def _():
            for cp in self.free + self.dep + self.zy_pass:
                cp.wait_send()


def reduce_scratch(rows):
    vm = pltpu.VMEM
    return [
        vm((4, 2, rows, 512), BF), vm((2, rows, 512), BF), vm((2, 2, rows, 512), BF), vm((2, rows, 512), BF),
        vm((2, 4, rows, 512), BF), vm((2, 4, rows, 512), BF), vm((2, rows // 2, 512), BF), vm((2, rows, 512), BF),
        pltpu.SemaphoreType.DMA((18,)), pltpu.SemaphoreType.DMA((18,)),
    ]


def kernel(
    pat, gpos, tok_in, cot_in, wq, wk, wv, wo,
    gt_out, gq_out, gk_out, gv_out, go_out,
    tok, cot, w, wov, r, g, gt, mask, masks, kg, vg, dkg, dvg, dkp, dvp, pr, xa, xf, fs,
    *rest,
):
    (o_bufs, o_sems), (q_bufs, q_sems), (v_bufs, v_sems) = [(rest[i : i + 8], rest[i + 8 : i + 10]) for i in (0, 10, 20)]
    (ssem, rsem, wssem, wrsem, lsem, mssem, mrsem, assem, arsem, bssem, brsem,
     cssem, crsem, dssem, drsem, essem, ersem, sssem, srsem, xssem, xrsem, fssem, frsem, flsem) = rest[30:]
    x, y, z, c = place()
    p, yh = lax.rem(y, 2), lax.div(y, 2)
    seq = lax.axis_index("seq")
    xr, xl, x2 = mod4(x + 1), mod4(x - 1), mod4(x + 2)
    zr, zl, z2 = mod4(z + 1), mod4(z - 1), mod4(z + 2)
    up, down = mod4(y + 1), mod4(y - 1)
    right, left = device(xr, y, z, c), device(xl, y, z, c)
    sib = device(x, y, z, 1 - c)
    me = yh * 4 + z
    my_doc = lax.div(me, 2) * 2 + p
    peers = [chip_peer(x, y, z, c, k) for k in range(1, 8)]

    meet(
        [right, left, sib]
        + [device(x, v, z, core) for v in (up, down) for core in (0, 1)]
        + [where for _, where in peers]
    )
    own = pl.ds(al(c * ROWS, ROWS), ROWS)
    other = pl.ds(al((1 - c) * ROWS, ROWS), ROWS)
    first = pl.ds(al(c * ROWS, 64), 64)
    second = pl.ds(al(c * ROWS + 64, 64), 64)

    def sends(a, given, buf):
        def cp(kind, src, dst, where):
            return remote(src, dst, ssem.at[a, kind], rsem.at[a, kind], where)

        return [
            cp(0, given, buf.at[x, own], right),
            cp(1, given, buf.at[x, own], left),
            cp(2, given, buf.at[x, own], sib),
            cp(3, buf.at[xl, first], buf.at[xl, first], right),
            cp(4, buf.at[xr, second], buf.at[xr, second], left),
            cp(5, buf.at[xl, own], buf.at[xl, own], sib),
            cp(6, buf.at[xr, own], buf.at[xr, own], sib),
            cp(7, buf.at[x2, first], buf.at[x2, first], sib),
            cp(8, buf.at[x2, second], buf.at[x2, second], sib),
        ]

    tsend = sends(0, tok_in, tok)
    csend = sends(1, cot_in, cot)
    wdev = device(x, mod4(y + 1 + 2 * c), z, p)
    zhalf = lax.rem(z, 2)
    sources = (wq, wk, wv, wo)

    def quarter(t, ref, h, n):
        size = 1024 if t < 3 else 64
        rows = pl.ds(al((2 * h + n) * size, size), size)
        return ref.at[t, rows] if ref is w else ref.at[rows]

    def held(t):
        return w if t < 3 else wov

    wsend = [
        remote(quarter(t, src, zhalf, c), quarter(t, held(t), zhalf, c), wssem.at[t], wrsem.at[t, c], wdev)
        for t, src in enumerate(sources)
    ]
    zdev = (device(x, y, zr, c), device(x, y, zl, c))
    wpass = [
        [
            remote(
                quarter(t, held(t), zhalf, n), quarter(t, held(t), zhalf, n),
                wssem.at[4 + 2 * t + n], wrsem.at[4 + t, n], zdev[n],
            )
            for n in (0, 1)
        ]
        for t in range(4)
    ]

    wlocal = [pltpu.make_async_copy(src, w.at[t], lsem.at[t]) for t, src in enumerate((wq, wk, wv))]
    wlocal.append(pltpu.make_async_copy(wo, wov, lsem.at[3]))
    tlocal = pltpu.make_async_copy(tok_in, tok.at[x, own], lsem.at[4])
    clocal = pltpu.make_async_copy(cot_in, cot.at[x, own], lsem.at[5])

    for k in (0, 1, 2):
        tsend[k].start()
    for cp in wsend:
        cp.start()
    tlocal.start()
    clocal.start()

    @pl.when(c == p)
    def _():
        for cp in wlocal:
            cp.start()

    kb = lax.div(lax.broadcasted_iota(jnp.int32, (8, 256), 1), 64)
    upper = lax.broadcasted_iota(jnp.int32, (8, 256), 0) == 0

    @pl.loop(0, 8)
    def _(d):
        prev0 = jnp.where(seq > 0, pat[d, 0, 0], 0)
        next0, prev1 = pat[d, 0, 1], pat[d, 1, 0]
        next1 = jnp.where(seq < 15, pat[d, 1, 1], 0)
        m0 = jnp.where(kb == 0, prev0, jnp.where(kb == 1, 1, jnp.where(kb == 2, next0, 0)))
        m1 = jnp.where(kb == 0, 0, jnp.where(kb == 1, prev1, jnp.where(kb == 2, 1, next1)))
        mask[c, d] = jnp.where(jnp.where(upper, m0, m1) == 1, 0.0, -jnp.inf)

    for t in (1, 2):
        r[t, :BLOCK] = jnp.zeros((BLOCK, HDIM), BF)
        r[t, BLOCK + 2048 :] = jnp.zeros((BLOCK, HDIM), BF)

    mask_sib = remote(mask.at[c], mask.at[c], mssem.at[7], mrsem.at[7], sib)
    mask_sib.start()
    mask_sib.wait()
    mask_out = [
        remote(mask.at[:, lax.div(j, 2) * 2 + p], masks.at[me], mssem.at[k], mrsem.at[k], where)
        for k, (j, where) in enumerate(peers)
    ]
    for cp in mask_out:
        cp.start()
    mask_own = pltpu.make_async_copy(mask.at[:, my_doc], masks.at[me], lsem.at[8])
    mask_own.start()

    def relay(copies):
        copies[0].wait_recv()
        copies[3].start()
        copies[5].start()
        copies[1].wait_recv()
        copies[4].start()
        copies[6].start()

    def weights_pass():
        @pl.when(c != p)
        def _():
            for t in range(4):
                for n in (0, 1):
                    ref = quarter(t, held(t), zhalf, n)
                    remote(ref, ref, wssem.at[t], wrsem.at[t, n], sib).wait_recv()
                    wpass[t][n].start()

    def weights_here(ts):
        @pl.when(c == p)
        def _():
            for t in ts:
                wlocal[t].wait()

        @pl.when(c != p)
        def _():
            for t in ts:
                for n in (0, 1):
                    wpass[t][n].wait()

    mine = pl.ds(al(me * CHIP_ROWS + BLOCK, 64), CHIP_ROWS)

    def boxes(j, t0, n):
        return gt.at[pl.ds(t0, n), :, pl.ds(al(j * HDIM, HDIM), HDIM)]

    def box(j, t):
        return gt.at[t, :, pl.ds(al(j * HDIM, HDIM), HDIM)]

    def chip(j):
        return device(x, lax.div(j, 4) * 2 + p, lax.rem(j, 4), c)

    def project(doc, ts):
        for t in ts:
            got = jnp.dot(tok[doc], w[t], preferred_element_type=F32).astype(BF)
            gt[t, :, pl.ds(al(doc * 256, 256), 256)] = got

    def qkv(j):
        return remote(boxes(j, 0, 3), r.at[pl.ds(0, 3), mine], assem.at[j], arsem.at[me], chip(j))

    qkv_own = pltpu.make_async_copy(boxes(me, 0, 3), r.at[pl.ds(0, 3), mine], lsem.at[6])

    def send_qkv(doc):
        for h in (0, 1):
            j = 2 * doc + h

            @pl.when(j != me)
            def _():
                qkv(j).start()

            @pl.when(j == me)
            def _():
                qkv_own.start()

    weights_pass()
    relay(tsend)
    for k in (0, 1, 2):
        csend[k].start()
    tlocal.wait()
    clocal.wait()
    tsend[2].wait_recv()
    tsend[5].wait_recv()
    tsend[6].wait_recv()
    near = (x, xl, xr)
    weights_here((0,))
    for doc in near:
        project(doc, (0,))
    weights_here((1,))
    for doc in near:
        project(doc, (1,))
    tsend[3].wait_recv()
    tsend[7].start()
    tsend[4].wait_recv()
    tsend[8].start()
    weights_here((2,))
    for doc in near:
        project(doc, (2,))
        send_qkv(doc)
    tsend[7].wait_recv()
    tsend[8].wait_recv()
    project(x2, (0, 1, 2))
    send_qkv(x2)

    relay(csend)
    weights_here((3,))

    def back(doc):
        got = lax.dot_general(cot[doc], wov[...], NT, preferred_element_type=F32).astype(BF)
        gt[3, :, pl.ds(al(doc * 256, 256), 256)] = got
        for h in (0, 1):
            j = 2 * doc + h

            @pl.when(j != me)
            def _():
                remote(box(j, 3), r.at[3, mine], bssem.at[j], brsem.at[me], chip(j)).start()

            @pl.when(j == me)
            def _():
                pltpu.make_async_copy(box(j, 3), r.at[3, mine], lsem.at[7]).start()

    csend[2].wait_recv()
    back(x)
    csend[5].wait_recv()
    back(xl)
    csend[6].wait_recv()
    back(xr)

    for n in range(1, 8):
        j = lax.rem(me + n, 8)
        qkv(j).wait_send()
        remote(boxes(j, 0, 3), r.at[pl.ds(0, 3), mine], assem.at[j], arsem.at[j], sib).wait_recv()
    qkv_own.wait()
    for cp in mask_out:
        cp.wait()
    mask_own.wait()
    scale = HDIM**-0.5
    pos = jnp.broadcast_to(gpos[pl.ds(my_doc, 1), :], (128, 128))
    pos_t = pos.T
    lane = lax.broadcasted_iota(jnp.int32, (128, 128), 1)
    sub = lax.broadcasted_iota(jnp.int32, (128, 128), 0)
    low = lax.broadcasted_iota(jnp.int32, (128, 256), 0) < BLOCK

    def nt(a, b):
        return lax.dot_general(a, b, NT, preferred_element_type=F32)

    def tn(a, b):
        return lax.dot_general(a, b, TN, preferred_element_type=F32)

    def mm(a, b):
        return jnp.dot(a, b, preferred_element_type=F32)

    dkg[...] = jnp.zeros_like(dkg)
    dvg[...] = jnp.zeros_like(dvg)

    @pl.loop(0, 16)
    def _(i):
        rows = pl.ds(al(i * 128 + BLOCK, 64), 128)
        pick = (pos_t == i * 128 + lane).astype(F32).astype(BF)
        dkg[...] += mm(pick, r[1, rows])
        dvg[...] += mm(pick, r[2, rows])

    kg[...] = dkg[...].astype(BF)
    vg[...] = dvg[...].astype(BF)
    wz, wy = v_bufs[0], v_bufs[4]

    def saved(i):
        return (lax.div(i, 4), lax.rem(lax.div(i, 2), 2), pl.ds(al(lax.rem(i, 2) * 128, 128), 128))

    @pl.loop(0, 16)
    def _(i):
        rows = pl.ds(al(i * 128 + BLOCK, 64), 128)
        win = pl.ds(al(i * 128, 128), 256)
        q, k, v = r[0, rows], r[1, win], r[2, win]
        seen = masks[lax.div(i, 2), lax.rem(i, 2)]
        bias = jnp.where(low, seen[0:1], seen[1:2])
        sl = nt(q, k) * scale + bias
        sg = nt(q, kg[...]) * scale
        top = jnp.maximum(sl.max(-1, keepdims=True), sg.max(-1, keepdims=True))
        el, eg = jnp.exp(sl - top), jnp.exp(sg - top)
        inv = 1.0 / (el.sum(-1, keepdims=True) + eg.sum(-1, keepdims=True))
        plb, pgb = (el * inv).astype(BF), (eg * inv).astype(BF)
        a, b, rr = saved(i)
        wz[a, b, rr, pl.ds(0, 256)] = plb
        wz[a, b, rr, pl.ds(256, 128)] = pgb
        ctx = mm(plb, v) + mm(pgb, vg[...])
        j = lax.div(i, 2)
        wy[lax.div(j, 4), lax.rem(j, 4), pl.ds(al(lax.rem(i, 2) * 128, 128), 128), pl.ds(0, 128)] = ctx.astype(BF)

    def ctx_box(j):
        return wy.at[lax.div(j, 4), lax.rem(j, 4), pl.ds(0, 256), pl.ds(0, 128)]

    def spot(t0, n):
        rows = pl.ds(al(lax.div(me, 2) * CHIP_ROWS, CHIP_ROWS), CHIP_ROWS)
        return g.at[pl.ds(t0, n), rows, pl.ds(al(lax.rem(me, 2) * HDIM, HDIM), HDIM)]

    def spot_o():
        rows = pl.ds(al(lax.div(me, 2) * CHIP_ROWS, CHIP_ROWS), CHIP_ROWS)
        return g.at[3, rows, pl.ds(al(lax.rem(me, 2) * HDIM, HDIM), HDIM)]

    ctx_out = [
        remote(ctx_box(j), spot_o(), cssem.at[k], crsem.at[k], where) for k, (j, where) in enumerate(peers)
    ]
    for cp in ctx_out:
        cp.start()
    ctx_own = pltpu.make_async_copy(ctx_box(me), spot_o(), lsem.at[9])
    ctx_own.start()

    csend[3].wait_recv()
    csend[7].start()
    csend[4].wait_recv()
    csend[8].start()
    csend[7].wait_recv()
    csend[8].wait_recv()
    back(x2)

    at = {
        "up": up, "down": down, "yh": yh, "owner": c == p, "middle": c != p,
        "front": device(x, y, zr, c), "rear": device(x, y, zl, c),
        "above": device(x, up, z, c), "below": device(x, down, z, c),
    }
    groups = (z2, zr, zl, z)
    order = [(0, 0), (0, 1), (1, 1), (2, 0), (1, 0), (2, 1), (3, 0), (3, 1)]
    red_o = Reduce(at, HALF_O, o_bufs, o_sems)
    red_q = Reduce(at, HALF_Q, q_bufs, q_sems)
    red_v = Reduce(at, HALF_KV, v_bufs, v_sems)

    def turn(t):
        for i in range(4):
            rows = pl.ds(i * 256, 256)
            gt[t, :, rows] = g[t, rows].T

    def piece(red, src, n, t0, count):
        o, ab = order[n]
        cols = pl.ds(al(ab * 2048 + groups[o] * 512, 512), 512)

        @pl.loop(0, count)
        def _(t):
            right_side = src[:, :, cols].reshape(1024, 512)
            acc = mm(gt[t0 + t], right_side).astype(BF)
            rows = pl.ds(al(t * 128, 128), 128)
            red.wz[o, ab, rows] = acc[:128]
            red.wy[ab, o, rows] = acc[128:]

        if n < 4:
            red.z[n].start()

    for j in range(8):

        @pl.when(j != me)
        def _():
            remote(box(j, 3), r.at[3, mine], bssem.at[j], brsem.at[j], sib).wait_send()

    pltpu.make_async_copy(box(me, 3), r.at[3, mine], lsem.at[7]).wait()

    for j in range(8):

        @pl.when(j != me)
        def _():
            remote(box(j, 3), r.at[3, mine], bssem.at[j], brsem.at[j], sib).wait_recv()

    dkp[...] = jnp.zeros_like(dkp)
    dvp[...] = jnp.zeros_like(dvp)
    dkg[...] = jnp.zeros_like(dkg)
    dvg[...] = jnp.zeros_like(dvg)

    def out_box(i, t):
        j = lax.div(i, 2)
        return (t, pl.ds(al(lax.rem(i, 2) * 128, 128), 128), pl.ds(al(j * 128, 128), 128))

    def backward(i):
        rows = pl.ds(al(i * 128 + BLOCK, 64), 128)
        win = pl.ds(al(i * 128, 128), 256)
        q, do, k, v = r[0, rows], r[3, rows], r[1, win], r[2, win]
        a, b, rr = saved(i)
        plb, pgb = wz[a, b, rr, pl.ds(0, 256)], wz[a, b, rr, pl.ds(256, 128)]
        dl, dg = nt(do, v), nt(do, vg[...])
        pf, pgf = plb.astype(F32), pgb.astype(F32)
        delta = (pf * dl).sum(-1, keepdims=True) + (pgf * dg).sum(-1, keepdims=True)
        sl = (pf * (dl - delta) * scale).astype(BF)
        sg = (pgf * (dg - delta) * scale).astype(BF)
        gt[out_box(i, 0)] = (mm(sl, k) + mm(sg, kg[...])).astype(BF)
        dkp[win] += tn(sl, q)
        dvp[win] += tn(plb, do)
        dkg[...] += tn(sg, q)
        dvg[...] += tn(pgb, do)

    def home_q(j):
        return remote(box(j, 0), spot(0, 1).at[0], dssem.at[j], drsem.at[me], chip(j))

    home_q_own = pltpu.make_async_copy(box(me, 0), spot(0, 1).at[0], lsem.at[10])

    @pl.loop(1, 9)
    def _(n):
        j = lax.rem(me + n, 8)
        backward(2 * j)
        backward(2 * j + 1)

        @pl.when(n < 8)
        def _():
            home_q(j).start()

    home_q_own.start()

    def home(sems, t0, n):
        s, d = sems
        return [
            remote(boxes(j, t0, n), spot(t0, n), s.at[k], d.at[k], where) for k, (j, where) in enumerate(peers)
        ]

    def split(a):
        high = a.astype(BF)
        return high, (a - high.astype(F32)).astype(BF)

    both = jnp.concatenate([jnp.concatenate(split(dkg[...]), 0), jnp.concatenate(split(dvg[...]), 0)], 1)

    @pl.loop(0, 16)
    def _(i):
        inner = pl.ds(al(i * 128 + BLOCK, 64), 128)
        put = (pos == i * 128 + sub).astype(F32).astype(BF)
        extra = mm(jnp.concatenate([put, put], 1), both)
        gt[out_box(i, 1)] = (dkp[inner] + extra[:, :128]).astype(BF)
        gt[out_box(i, 2)] = (dvp[inner] + extra[:, 128:]).astype(BF)

    home_kv = home((essem, ersem), 1, 2)
    for cp in home_kv:
        cp.start()
    home_kv_own = pltpu.make_async_copy(boxes(me, 1, 2), spot(1, 2), lsem.at[11])
    home_kv_own.start()

    for cp in ctx_out:
        cp.wait()
    ctx_own.wait()
    turn(3)
    for n in range(8):
        piece(red_o, cot, n, 3, 1)
    red_o.start_y()
    for cp in tsend + csend + wsend:
        cp.wait_send()
    for n in range(1, 8):
        j = lax.rem(me + n, 8)
        home_q(j).wait_send()
        remote(box(j, 0), spot(0, 1).at[0], dssem.at[j], drsem.at[j], sib).wait_recv()
    home_q_own.wait()
    for cp in home_kv:
        cp.wait()
    home_kv_own.wait()

    part = cot
    docs = (x2, xr, xl, x)
    to_sib = [remote(part.at[o, other], pr.at[o], sssem.at[o], srsem.at[o], sib) for o in range(4)]

    def tokens_part(o):
        rows = pl.ds(al(docs[o] * CHIP_ROWS, CHIP_ROWS), CHIP_ROWS)

        @pl.loop(0, 8)
        def _(n):
            cols = pl.ds(al(n * 512, 512), 512)
            a = jnp.concatenate([g[t, rows] for t in range(3)], 1)
            b = jnp.concatenate([w[t, cols] for t in range(3)], 1)
            part[o, :, cols] = nt(a, b).astype(BF)

        to_sib[o].start()

    xc = [
        remote(pr.at[0, pl.ds(0, 64)], xa.at[pl.ds(0, 64)], xssem.at[0], xrsem.at[0], right),
        remote(pr.at[0, pl.ds(64, 64)], xa.at[pl.ds(64, 64)], xssem.at[1], xrsem.at[1], left),
        remote(pr.at[1], xf.at[0], xssem.at[2], xrsem.at[2], right),
        remote(pr.at[2], xf.at[1], xssem.at[3], xrsem.at[3], left),
    ]

    def sum_rows(o, extra=None):
        @pl.loop(0, 8)
        def _(n):
            cols = pl.ds(al(n * 512, 512), 512)
            for h in range(2):
                rows = pl.ds(h * 64, 64)
                own_half = pl.ds(al(c * ROWS + h * 64, 64), 64)
                total = part[o, own_half, cols].astype(F32) + pr[o, rows, cols].astype(F32)
                if extra is not None and extra == h:
                    total += xa[rows, cols].astype(F32)
                pr[o, rows, cols] = total.astype(BF)

    tokens_part(0)
    tokens_part(1)
    to_sib[0].wait_recv()
    sum_rows(0)
    xc[0].start()
    xc[1].start()
    turn(0)
    for n in range(8):
        piece(red_q, tok, n, 0, 1)
    red_q.start_y()
    tokens_part(2)
    turn(1)
    turn(2)
    for n in range(4):
        piece(red_v, tok, n, 1, 2)
    red_o.dep_z()
    red_o.dep_y()
    for n in range(4, 8):
        piece(red_v, tok, n, 1, 2)
    red_v.start_y()
    to_sib[1].wait_recv()
    xc[0].wait_recv()
    sum_rows(1, 0)
    xc[2].start()
    to_sib[2].wait_recv()
    xc[1].wait_recv()
    sum_rows(2, 1)
    xc[3].start()
    red_q.dep_z()
    red_q.dep_y()
    red_o.mid_z()
    red_o.mid_y()
    tokens_part(3)
    red_v.dep_z()
    red_v.dep_y()
    red_o.last_z()
    red_o.last_y()
    red_q.mid_z()
    red_q.mid_y()
    red_q.last_z()
    red_q.last_y()
    to_sib[3].wait_recv()
    red_v.mid_z()
    red_v.mid_y()

    xc[2].wait_recv()
    xc[3].wait_recv()

    to_sib[3].wait_send()

    @pl.loop(0, 8)
    def _(n):
        cols = pl.ds(al(n * 512, 512), 512)
        total = part[3, own, cols].astype(F32) + pr[3, :, cols].astype(F32)
        total += xf[0, :, cols].astype(F32) + xf[1, :, cols].astype(F32)
        part[3, other, cols] = total.astype(BF)

    gt_copy = pltpu.make_async_copy(part.at[3, other], gt_out, lsem.at[12])
    gt_copy.start()
    red_v.last_z()
    red_v.last_y()

    outs = (gq_out, gk_out, gv_out, go_out)
    final = [remote(fs.at[1, t], outs[t], fssem.at[t], frsem.at[t], sib) for t in range(4)]
    final_own = [pltpu.make_async_copy(fs.at[0, t], outs[t], flsem.at[t]) for t in range(4)]

    @pl.when(c == p)
    def _():
        def put(t0):
            def run(head, n, value):
                lanes = pl.ds(head * 128, 128)
                for s in range(2):
                    core = c if s == 0 else 1 - c
                    got = value(pl.ds(al(core * 256, 256), 256))
                    if t0 + n < 3:
                        fs[s, t0 + n, :, lanes] = got.T
                    else:
                        fs[s, 3, lanes, :] = got

            return run

        red_o.result(put(3))
        final[3].start()
        final_own[3].start()
        red_q.result(put(0))
        final[0].start()
        final_own[0].start()
        red_v.result(put(1))
        for t in (1, 2):
            final[t].start()
            final_own[t].start()
        for t in range(4):
            final[t].wait_send()
            final_own[t].wait()

    @pl.when(c != p)
    def _():
        for cp in final:
            cp.wait_recv()

    red_o.drain()
    red_q.drain()
    red_v.drain()
    for cp in to_sib[:3] + xc:
        cp.wait_send()
    gt_copy.wait()


def on_device(tokens, cotangent, w_query, w_key, w_value, w_output, global_pos, pattern):
    dma = pltpu.SemaphoreType.DMA
    vm = pltpu.VMEM
    square = jax.ShapeDtypeStruct((256, 256), F32)
    grad_tokens, gq, gk, gv, go = pl.pallas_call(
        kernel,
        out_shape=(jax.ShapeDtypeStruct((ROWS, D), BF), square, square, square, square),
        in_specs=[pl.BlockSpec(memory_space=pltpu.SMEM), pl.BlockSpec(memory_space=pltpu.VMEM)] + [ANY] * 6,
        out_specs=(ANY,) * 5,
        scratch_shapes=[
            vm((4, CHIP_ROWS, D), BF),
            vm((4, CHIP_ROWS, D), BF),
            vm((3, D, 256), BF),
            vm((256, D), BF),
            vm((4, 2176, HDIM), BF),
            vm((4, 1024, 256), BF),
            vm((4, 256, 1024), BF),
            vm((2, 8, 8, 256), F32),
            vm((8, 2, 8, 256), F32),
            vm((128, HDIM), BF), vm((128, HDIM), BF), vm((128, HDIM), F32), vm((128, HDIM), F32),
            vm((2176, HDIM), F32), vm((2176, HDIM), F32),
            vm((4, ROWS, D), BF),
            vm((ROWS, D), BF),
            vm((2, ROWS, D), BF),
            vm((2, 4, 256, 256), F32),
            *reduce_scratch(HALF_O),
            *reduce_scratch(HALF_Q),
            *reduce_scratch(HALF_KV),
            dma((2, 9)), dma((2, 9)), dma((12,)), dma((8, 2)), dma((13,)), dma((8,)), dma((8,)),
            dma((8,)), dma((8,)), dma((8,)), dma((8,)), dma((7,)), dma((7,)), dma((8,)), dma((8,)),
            dma((7,)), dma((7,)), dma((4,)), dma((4,)), dma((4,)), dma((4,)), dma((4,)), dma((4,)), dma((4,)),
        ],
        compiler_params=pltpu.CompilerParams(
            collective_id=0, has_side_effects=True, vmem_limit_bytes=63 << 20
        ),
        cost_estimate=pl.CostEstimate(flops=25 * 10**9, bytes_accessed=60 << 20, transcendentals=10**6),
    )(pattern, global_pos, tokens[0], cotangent[0], w_query, w_key, w_value, w_output)
    return grad_tokens[None], gq, gk, gv, go


def solution(mesh):
    in_specs = (
        P("fsdp", "seq", None),
        P("fsdp", "seq", None),
        P(None, "fsdp"),
        P(None, "fsdp"),
        P(None, "fsdp"),
        P("fsdp", None),
        P(),
        P(None, "seq", None),
    )
    out_specs = (
        P("fsdp", "seq", None),
        P("seq", "fsdp"),
        P("seq", "fsdp"),
        P("seq", "fsdp"),
        P("fsdp", "seq"),
    )
    return jax.shard_map(
        on_device, mesh=mesh, in_specs=in_specs, out_specs=out_specs, check_vma=False
    )
```

```python
import jax
import jax.numpy as jnp
from jax import lax
from jax.experimental import pallas as pl
from jax.experimental.pallas import tpu as pltpu
from jax.sharding import PartitionSpec as P

BLOCK = 64
HDIM = 128
ROWS = 128
CHIP_ROWS = 256
D = 4096
BF = jnp.bfloat16
F32 = jnp.float32
MESH = pl.DeviceIdType.MESH
ANY = pl.BlockSpec(memory_space=pl.ANY)
NT = (((1,), (1,)), ((), ()))
TN = (((0,), (0,)), ((), ()))


def place():
    f = lax.axis_index("fsdp")
    s = lax.axis_index("seq")
    x, p = lax.div(f, 2), lax.rem(f, 2)
    yh, z, c = lax.div(s, 8), lax.rem(lax.div(s, 2), 4), lax.rem(s, 2)
    return x, 2 * yh + p, z, c


def device(x, y, z, c):
    return {"seq": lax.div(y, 2) * 8 + z * 2 + c, "fsdp": x * 2 + lax.rem(y, 2)}


def mod4(v):
    return lax.rem(v + 4, 4)


def al(v, n):
    return pl.multiple_of(v, n)


def remote(src, dst, send, recv, where):
    return pltpu.make_async_remote_copy(
        src_ref=src, dst_ref=dst, send_sem=send, recv_sem=recv, device_id=where, device_id_type=MESH
    )


def meet(devices):
    barrier = pltpu.get_barrier_semaphore()
    for where in devices:
        pl.semaphore_signal(barrier, inc=1, device_id=where, device_id_type=MESH)
    pl.semaphore_wait(barrier, len(devices))


def chip_peer(x, y, z, c, k):
    j = lax.rem(lax.div(y, 2) * 4 + z + k, 8)
    return j, device(x, lax.div(j, 4) * 2 + lax.rem(y, 2), lax.rem(j, 4), c)


HALF_KV, HALF_Q, HALF_O = 256, 128, 128


class Reduce:
    def __init__(self, at, rows, bufs, sems):
        self.at, self.rows = at, rows
        self.wz, self.za, self.zf, self.yf, self.wy, self.yg, self.zb, self.zg = bufs
        ss, rs = sems
        half = rows // 2
        lo, hi = pl.ds(0, half), pl.ds(half, half)
        self.lo, self.hi = lo, hi
        wz, za, zf, yf, wy, yg, zb, zg = bufs
        up, down, yh = at["up"], at["down"], at["yh"]
        front, rear, above, below = at["front"], at["rear"], at["above"], at["below"]
        up_i, down_i = lax.div(up, 2), lax.div(down, 2)
        self.up_i, self.down_i, self.yh = up_i, down_i, yh

        def cp(i, src, dst, where):
            return remote(src, dst, ss.at[i], rs.at[i], where)

        self.z = [
            cp(0, wz.at[0, 0], za.at[0], front),
            cp(1, wz.at[0, 1], za.at[1], rear),
            cp(2, wz.at[1, 1], zf.at[0, 1], front),
            cp(3, wz.at[2, 0], zf.at[1, 0], rear),
            cp(4, wz.at[1, 0], zf.at[0, 0], front),
            cp(5, wz.at[2, 1], zf.at[1, 1], rear),
        ]
        self.give = [
            cp(6, wy.at[1 - yh, :, lo], yg.at[0, :, lo], above),
            cp(7, wy.at[1 - yh, :, hi], yg.at[1, :, lo], below),
        ]
        self.free = [
            cp(8, wy.at[up_i, :, hi], yg.at[0, :, hi], above),
            cp(9, wy.at[down_i, :, lo], yg.at[1, :, lo], below),
        ]
        self.dep = [
            cp(6, wy.at[up_i, :, lo], yg.at[0, :, lo], above),
            cp(7, wy.at[down_i, :, hi], yg.at[1, :, hi], below),
        ]
        self.zy_give = [
            cp(10, wz.at[3, 1 - yh, lo], yf.at[0, lo], above),
            cp(11, wz.at[3, 1 - yh, hi], yf.at[1, lo], below),
        ]
        self.zy_pass = [
            cp(12, wz.at[3, up_i], yf.at[0], above),
            cp(13, wz.at[3, down_i], yf.at[1], below),
        ]
        self.yz = [
            cp(14, wy.at[yh, 0, lo], zb.at[0], front),
            cp(15, wy.at[yh, 0, hi], zb.at[1], rear),
            cp(16, wy.at[yh, 1], zg.at[0], front),
            cp(17, wy.at[yh, 2], zg.at[1], rear),
        ]

    def add(self, rows, dst, *srcs):
        @pl.loop(0, rows // 64)
        def _(i):
            r = pl.ds(al(i * 64, 64), 64)
            total = dst[r].astype(F32)
            for s in srcs:
                total += s[r].astype(F32)
            dst[r] = total.astype(BF)

    def start_y(self):
        @pl.when(self.at["owner"])
        def _():
            for cp in self.give:
                cp.start()

        @pl.when(self.at["middle"])
        def _():
            for cp in self.free:
                cp.start()

    def dep_z(self):
        self.z[0].wait_recv()
        self.add(self.rows, self.wz.at[1, 0], self.za.at[0])
        self.z[4].start()
        self.z[1].wait_recv()
        self.add(self.rows, self.wz.at[2, 1], self.za.at[1])
        self.z[5].start()

    def dep_y(self):
        half = self.rows // 2

        @pl.when(self.at["middle"])
        def _():
            for i, (idx, part) in enumerate(((self.up_i, self.lo), (self.down_i, self.hi))):
                self.give[i].wait_recv()
                for o in range(4):
                    self.add(half, self.wy.at[idx, o, part], self.yg.at[i, o, self.lo])
                self.dep[i].start()

    def mid_z(self):
        for i in (2, 3, 4, 5):
            self.z[i].wait_recv()
        for ab in range(2):
            self.add(self.rows, self.wz.at[3, ab], self.zf.at[0, ab], self.zf.at[1, ab])

        @pl.when(self.at["owner"])
        def _():
            for cp in self.zy_give:
                cp.start()

    def mid_y(self):
        @pl.when(self.at["owner"])
        def _():
            for cp in self.free + self.dep:
                cp.wait_recv()
            for cp in self.give:
                cp.wait_send()
            for o in range(4):
                self.add(self.rows, self.wy.at[self.yh, o], self.yg.at[0, o], self.yg.at[1, o])
                if o == 0:
                    self.yz[0].start()
                    self.yz[1].start()

    def last_z(self):
        half = self.rows // 2

        @pl.when(self.at["middle"])
        def _():
            for i, (idx, part) in enumerate(((self.up_i, self.lo), (self.down_i, self.hi))):
                self.zy_give[i].wait_recv()
                self.add(half, self.wz.at[3, idx, part], self.yf.at[i, self.lo])
                self.zy_pass[i].start()

    def last_y(self):
        half = self.rows // 2

        @pl.when(self.at["owner"])
        def _():
            self.yz[0].wait_recv()
            self.add(half, self.wy.at[self.yh, 1, self.lo], self.zb.at[0])
            self.yz[2].start()
            self.yz[1].wait_recv()
            self.add(half, self.wy.at[self.yh, 2, self.hi], self.zb.at[1])
            self.yz[3].start()

    def result(self, put):
        for cp in self.zy_pass:
            cp.wait_recv()
        for n in range(self.rows // 128):
            rows = pl.ds(n * 128, 128)
            put(0, n, lambda cols: (
                self.wz[3, self.yh, rows, cols].astype(F32)
                + self.yf[0, rows, cols].astype(F32) + self.yf[1, rows, cols].astype(F32)))
        for cp in self.yz[2:]:
            cp.wait_recv()
        for n in range(self.rows // 128):
            rows = pl.ds(n * 128, 128)
            put(1, n, lambda cols: (
                self.wy[self.yh, 3, rows, cols].astype(F32)
                + self.zg[0, rows, cols].astype(F32) + self.zg[1, rows, cols].astype(F32)))

    def drain(self):
        for cp in self.z:
            cp.wait_send()

        @pl.when(self.at["owner"])
        def _():
            for cp in self.zy_give + self.yz:
                cp.wait_send()

        @pl.when(self.at["middle"])
        def _():
            for cp in self.free + self.dep + self.zy_pass:
                cp.wait_send()


def reduce_scratch(rows):
    vm = pltpu.VMEM
    return [
        vm((4, 2, rows, 512), BF), vm((2, rows, 512), BF), vm((2, 2, rows, 512), BF), vm((2, rows, 512), BF),
        vm((2, 4, rows, 512), BF), vm((2, 4, rows, 512), BF), vm((2, rows // 2, 512), BF), vm((2, rows, 512), BF),
        pltpu.SemaphoreType.DMA((18,)), pltpu.SemaphoreType.DMA((18,)),
    ]


def kernel(
    pat, gpos, tok_in, cot_in, wq, wk, wv, wo,
    gt_out, gq_out, gk_out, gv_out, go_out,
    tok, cot, w, wov, r, g, gt, mask, masks, kg, vg, dkg, dvg, dkp, dvp, pr, xa, xf, fs,
    *rest,
):
    (o_bufs, o_sems), (q_bufs, q_sems), (v_bufs, v_sems) = [(rest[i : i + 8], rest[i + 8 : i + 10]) for i in (0, 10, 20)]
    (ssem, rsem, wssem, wrsem, lsem, mssem, mrsem, assem, arsem, bssem, brsem,
     cssem, crsem, dssem, drsem, essem, ersem, sssem, srsem, xssem, xrsem, fssem, frsem, flsem) = rest[30:]
    x, y, z, c = place()
    p, yh = lax.rem(y, 2), lax.div(y, 2)
    seq = lax.axis_index("seq")
    xr, xl, x2 = mod4(x + 1), mod4(x - 1), mod4(x + 2)
    zr, zl, z2 = mod4(z + 1), mod4(z - 1), mod4(z + 2)
    up, down = mod4(y + 1), mod4(y - 1)
    right, left = device(xr, y, z, c), device(xl, y, z, c)
    sib = device(x, y, z, 1 - c)
    me = yh * 4 + z
    my_doc = lax.div(me, 2) * 2 + p
    peers = [chip_peer(x, y, z, c, k) for k in range(1, 8)]

    meet(
        [right, left, sib]
        + [device(x, v, z, core) for v in (up, down) for core in (0, 1)]
        + [where for _, where in peers]
    )
    own = pl.ds(al(c * ROWS, ROWS), ROWS)
    other = pl.ds(al((1 - c) * ROWS, ROWS), ROWS)
    first = pl.ds(al(c * ROWS, 64), 64)
    second = pl.ds(al(c * ROWS + 64, 64), 64)

    def sends(a, given, buf):
        def cp(kind, src, dst, where):
            return remote(src, dst, ssem.at[a, kind], rsem.at[a, kind], where)

        return [
            cp(0, given, buf.at[x, own], right),
            cp(1, given, buf.at[x, own], left),
            cp(2, given, buf.at[x, own], sib),
            cp(3, buf.at[xl, first], buf.at[xl, first], right),
            cp(4, buf.at[xr, second], buf.at[xr, second], left),
            cp(5, buf.at[xl, own], buf.at[xl, own], sib),
            cp(6, buf.at[xr, own], buf.at[xr, own], sib),
            cp(7, buf.at[x2, first], buf.at[x2, first], sib),
            cp(8, buf.at[x2, second], buf.at[x2, second], sib),
        ]

    tsend = sends(0, tok_in, tok)
    csend = sends(1, cot_in, cot)
    wdev = device(x, mod4(y + 1 + 2 * c), z, p)
    zhalf = lax.rem(z, 2)
    sources = (wq, wk, wv, wo)

    def quarter(t, ref, h, n):
        size = 1024 if t < 3 else 64
        rows = pl.ds(al((2 * h + n) * size, size), size)
        return ref.at[t, rows] if ref is w else ref.at[rows]

    def held(t):
        return w if t < 3 else wov

    wsend = [
        remote(quarter(t, src, zhalf, c), quarter(t, held(t), zhalf, c), wssem.at[t], wrsem.at[t, c], wdev)
        for t, src in enumerate(sources)
    ]
    zdev = (device(x, y, zr, c), device(x, y, zl, c))
    wpass = [
        [
            remote(
                quarter(t, held(t), zhalf, n), quarter(t, held(t), zhalf, n),
                wssem.at[4 + 2 * t + n], wrsem.at[4 + t, n], zdev[n],
            )
            for n in (0, 1)
        ]
        for t in range(4)
    ]

    wlocal = [pltpu.make_async_copy(src, w.at[t], lsem.at[t]) for t, src in enumerate((wq, wk, wv))]
    wlocal.append(pltpu.make_async_copy(wo, wov, lsem.at[3]))
    tlocal = pltpu.make_async_copy(tok_in, tok.at[x, own], lsem.at[4])
    clocal = pltpu.make_async_copy(cot_in, cot.at[x, own], lsem.at[5])

    for k in (0, 1, 2):
        tsend[k].start()
    for cp in wsend:
        cp.start()
    tlocal.start()
    clocal.start()

    @pl.when(c == p)
    def _():
        for cp in wlocal:
            cp.start()

    kb = lax.div(lax.broadcasted_iota(jnp.int32, (8, 256), 1), 64)
    upper = lax.broadcasted_iota(jnp.int32, (8, 256), 0) == 0

    @pl.loop(0, 8)
    def _(d):
        prev0 = jnp.where(seq > 0, pat[d, 0, 0], 0)
        next0, prev1 = pat[d, 0, 1], pat[d, 1, 0]
        next1 = jnp.where(seq < 15, pat[d, 1, 1], 0)
        m0 = jnp.where(kb == 0, prev0, jnp.where(kb == 1, 1, jnp.where(kb == 2, next0, 0)))
        m1 = jnp.where(kb == 0, 0, jnp.where(kb == 1, prev1, jnp.where(kb == 2, 1, next1)))
        mask[c, d] = jnp.where(jnp.where(upper, m0, m1) == 1, 0.0, -jnp.inf)

    for t in (1, 2):
        r[t, :BLOCK] = jnp.zeros((BLOCK, HDIM), BF)
        r[t, BLOCK + 2048 :] = jnp.zeros((BLOCK, HDIM), BF)

    mask_sib = remote(mask.at[c], mask.at[c], mssem.at[7], mrsem.at[7], sib)
    mask_sib.start()
    mask_sib.wait()
    mask_out = [
        remote(mask.at[:, lax.div(j, 2) * 2 + p], masks.at[me], mssem.at[k], mrsem.at[k], where)
        for k, (j, where) in enumerate(peers)
    ]
    for cp in mask_out:
        cp.start()
    mask_own = pltpu.make_async_copy(mask.at[:, my_doc], masks.at[me], lsem.at[8])
    mask_own.start()

    def relay(copies):
        copies[0].wait_recv()
        copies[3].start()
        copies[5].start()
        copies[1].wait_recv()
        copies[4].start()
        copies[6].start()

    def weights_pass():
        @pl.when(c != p)
        def _():
            for t in range(4):
                for n in (0, 1):
                    ref = quarter(t, held(t), zhalf, n)
                    remote(ref, ref, wssem.at[t], wrsem.at[t, n], sib).wait_recv()
                    wpass[t][n].start()

    def weights_here(ts):
        @pl.when(c == p)
        def _():
            for t in ts:
                wlocal[t].wait()

        @pl.when(c != p)
        def _():
            for t in ts:
                for n in (0, 1):
                    wpass[t][n].wait()

    mine = pl.ds(al(me * CHIP_ROWS + BLOCK, 64), CHIP_ROWS)

    def boxes(j, t0, n):
        return gt.at[pl.ds(t0, n), :, pl.ds(al(j * HDIM, HDIM), HDIM)]

    def box(j, t):
        return gt.at[t, :, pl.ds(al(j * HDIM, HDIM), HDIM)]

    def chip(j):
        return device(x, lax.div(j, 4) * 2 + p, lax.rem(j, 4), c)

    def project(doc, t):
        got = jnp.dot(tok[doc], w[t], preferred_element_type=F32).astype(BF)
        gt[t, :, pl.ds(al(doc * 256, 256), 256)] = got

    def project_near(t):
        @pl.loop(0, 3)
        def _(n):
            project(lax.rem(x + n + lax.div(n, 2), 4), t)

    def qkv(j):
        return remote(boxes(j, 0, 3), r.at[pl.ds(0, 3), mine], assem.at[j], arsem.at[me], chip(j))

    qkv_own = pltpu.make_async_copy(boxes(me, 0, 3), r.at[pl.ds(0, 3), mine], lsem.at[6])

    def send_qkv(last):
        for n in range(8):
            j = lax.rem(me + n, 8)
            here = lax.div(j, 2) == x2
            here = here if last else jnp.logical_not(here)
            if n == 0:

                @pl.when(here)
                def _():
                    qkv_own.start()

            else:

                @pl.when(here)
                def _():
                    qkv(j).start()

    weights_pass()
    relay(tsend)
    for k in (0, 1, 2):
        csend[k].start()
    tlocal.wait()
    clocal.wait()
    tsend[2].wait_recv()
    tsend[5].wait_recv()
    tsend[6].wait_recv()
    weights_here((0,))
    project_near(0)
    weights_here((1,))
    project_near(1)
    tsend[3].wait_recv()
    tsend[7].start()
    tsend[4].wait_recv()
    tsend[8].start()
    weights_here((2,))
    project_near(2)
    send_qkv(False)
    tsend[7].wait_recv()
    tsend[8].wait_recv()

    @pl.loop(0, 3)
    def _(t):
        project(x2, t)

    send_qkv(True)

    relay(csend)
    weights_here((3,))

    def back(doc):
        got = lax.dot_general(cot[doc], wov[...], NT, preferred_element_type=F32).astype(BF)
        gt[3, :, pl.ds(al(doc * 256, 256), 256)] = got
        for h in (0, 1):
            j = 2 * doc + h

            @pl.when(j != me)
            def _():
                remote(box(j, 3), r.at[3, mine], bssem.at[j], brsem.at[me], chip(j)).start()

            @pl.when(j == me)
            def _():
                pltpu.make_async_copy(box(j, 3), r.at[3, mine], lsem.at[7]).start()

    csend[2].wait_recv()
    back(x)
    csend[5].wait_recv()
    back(xl)
    csend[6].wait_recv()
    back(xr)

    for n in range(1, 8):
        j = lax.rem(me + n, 8)
        qkv(j).wait_send()
        remote(boxes(j, 0, 3), r.at[pl.ds(0, 3), mine], assem.at[j], arsem.at[j], sib).wait_recv()
    qkv_own.wait()
    for cp in mask_out:
        cp.wait()
    mask_own.wait()
    scale = HDIM**-0.5
    pos = jnp.broadcast_to(gpos[pl.ds(my_doc, 1), :], (128, 128))
    pos_t = pos.T
    lane = lax.broadcasted_iota(jnp.int32, (128, 128), 1)
    sub = lax.broadcasted_iota(jnp.int32, (128, 128), 0)
    low = lax.broadcasted_iota(jnp.int32, (128, 256), 0) < BLOCK

    def nt(a, b):
        return lax.dot_general(a, b, NT, preferred_element_type=F32)

    def tn(a, b):
        return lax.dot_general(a, b, TN, preferred_element_type=F32)

    def mm(a, b):
        return jnp.dot(a, b, preferred_element_type=F32)

    dkg[...] = jnp.zeros_like(dkg)
    dvg[...] = jnp.zeros_like(dvg)

    @pl.loop(0, 16)
    def _(i):
        rows = pl.ds(al(i * 128 + BLOCK, 64), 128)
        pick = (pos_t == i * 128 + lane).astype(F32).astype(BF)
        dkg[...] += mm(pick, r[1, rows])
        dvg[...] += mm(pick, r[2, rows])

    kg[...] = dkg[...].astype(BF)
    vg[...] = dvg[...].astype(BF)
    wz, wy = v_bufs[0], v_bufs[4]

    def saved(i):
        return (lax.div(i, 4), lax.rem(lax.div(i, 2), 2), pl.ds(al(lax.rem(i, 2) * 128, 128), 128))

    def forward(j):
        tiles = (2 * j, 2 * j + 1)
        rows = [pl.ds(al(i * 128 + BLOCK, 64), 128) for i in tiles]
        wins = [pl.ds(al(i * 128, 128), 256) for i in tiles]
        qs = [r[0, a] for a in rows]
        ks, vs = [r[1, a] for a in wins], [r[2, a] for a in wins]
        kgv, vgv = kg[...], vg[...]
        sls = [nt(q, k) for q, k in zip(qs, ks)]
        sgs = [nt(q, kgv) * scale for q in qs]
        for h in (0, 1):
            seen = masks[j, h]
            sls[h] = sls[h] * scale + jnp.where(low, seen[0:1], seen[1:2])
        tops = [jnp.maximum(a.max(-1, keepdims=True), b.max(-1, keepdims=True)) for a, b in zip(sls, sgs)]
        els = [jnp.exp(a - t) for a, t in zip(sls, tops)]
        egs = [jnp.exp(a - t) for a, t in zip(sgs, tops)]
        invs = [1.0 / (a.sum(-1, keepdims=True) + b.sum(-1, keepdims=True)) for a, b in zip(els, egs)]
        pls = [(a * t).astype(BF) for a, t in zip(els, invs)]
        pgs = [(a * t).astype(BF) for a, t in zip(egs, invs)]
        ctx = [(mm(a, v) + mm(b, vgv)).astype(BF) for a, b, v in zip(pls, pgs, vs)]
        for h in (0, 1):
            a, b, rr = saved(tiles[h])
            wz[a, b, rr, pl.ds(0, 256)] = pls[h]
            wz[a, b, rr, pl.ds(256, 128)] = pgs[h]
            wy[lax.div(j, 4), lax.rem(j, 4), pl.ds(h * 128, 128), pl.ds(0, 128)] = ctx[h]

    pl.loop(0, 5)(forward)
    csend[3].wait_recv()
    csend[7].start()
    csend[4].wait_recv()
    csend[8].start()
    csend[7].wait_recv()
    csend[8].wait_recv()
    back(x2)
    pl.loop(5, 8)(forward)

    def ctx_box(j):
        return wy.at[lax.div(j, 4), lax.rem(j, 4), pl.ds(0, 256), pl.ds(0, 128)]

    def spot(t0, n):
        rows = pl.ds(al(lax.div(me, 2) * CHIP_ROWS, CHIP_ROWS), CHIP_ROWS)
        return g.at[pl.ds(t0, n), rows, pl.ds(al(lax.rem(me, 2) * HDIM, HDIM), HDIM)]

    def spot_o():
        rows = pl.ds(al(lax.div(me, 2) * CHIP_ROWS, CHIP_ROWS), CHIP_ROWS)
        return g.at[3, rows, pl.ds(al(lax.rem(me, 2) * HDIM, HDIM), HDIM)]

    ctx_out = [
        remote(ctx_box(j), spot_o(), cssem.at[k], crsem.at[k], where) for k, (j, where) in enumerate(peers)
    ]
    for cp in ctx_out:
        cp.start()
    ctx_own = pltpu.make_async_copy(ctx_box(me), spot_o(), lsem.at[9])
    ctx_own.start()

    at = {
        "up": up, "down": down, "yh": yh, "owner": c == p, "middle": c != p,
        "front": device(x, y, zr, c), "rear": device(x, y, zl, c),
        "above": device(x, up, z, c), "below": device(x, down, z, c),
    }
    groups = (z2, zr, zl, z)
    order = [(0, 0), (0, 1), (1, 1), (2, 0), (1, 0), (2, 1), (3, 0), (3, 1)]
    red_o = Reduce(at, HALF_O, o_bufs, o_sems)
    red_q = Reduce(at, HALF_Q, q_bufs, q_sems)
    red_v = Reduce(at, HALF_KV, v_bufs, v_sems)

    def turn(t):
        for i in range(4):
            rows = pl.ds(i * 256, 256)
            gt[t, :, rows] = g[t, rows].T

    def piece(red, src, n, t0, count):
        o, ab = order[n]

        @pl.loop(0, 2)
        def _(h):
            lanes = pl.ds(al(h * 256, 256), 256)
            here = pl.ds(al(ab * 2048 + groups[o] * 512 + h * 256, 256), 256)
            left_side = gt[pl.ds(t0, count)].reshape(count * 256, 1024)
            acc = mm(left_side, src[:, :, here].reshape(1024, 256)).astype(BF)
            for t in range(count):
                rows = pl.ds(t * 128, 128)
                red.wz[o, ab, rows, lanes] = acc[t * 256 : t * 256 + 128]
                red.wy[ab, o, rows, lanes] = acc[t * 256 + 128 : t * 256 + 256]

        if n < 4:
            red.z[n].start()

    for j in range(8):

        @pl.when(j != me)
        def _():
            remote(box(j, 3), r.at[3, mine], bssem.at[j], brsem.at[j], sib).wait_send()

    pltpu.make_async_copy(box(me, 3), r.at[3, mine], lsem.at[7]).wait()

    for j in range(8):

        @pl.when(j != me)
        def _():
            remote(box(j, 3), r.at[3, mine], bssem.at[j], brsem.at[j], sib).wait_recv()

    dkp[...] = jnp.zeros_like(dkp)
    dvp[...] = jnp.zeros_like(dvp)
    dkg[...] = jnp.zeros_like(dkg)
    dvg[...] = jnp.zeros_like(dvg)

    def out_box(i, t):
        j = lax.div(i, 2)
        return (t, pl.ds(al(lax.rem(i, 2) * 128, 128), 128), pl.ds(al(j * 128, 128), 128))

    def backward(j):
        tiles = (2 * j, 2 * j + 1)
        rows = [pl.ds(al(i * 128 + BLOCK, 64), 128) for i in tiles]
        wins = [pl.ds(al(i * 128, 128), 256) for i in tiles]
        qs, dos = [r[0, a] for a in rows], [r[3, a] for a in rows]
        ks, vs = [r[1, a] for a in wins], [r[2, a] for a in wins]
        kgv, vgv = kg[...], vg[...]
        spots = [saved(i) for i in tiles]
        pls = [wz[a, b, rr, pl.ds(0, 256)] for a, b, rr in spots]
        pgs = [wz[a, b, rr, pl.ds(256, 128)] for a, b, rr in spots]
        dls = [nt(d, v) for d, v in zip(dos, vs)]
        dgs = [nt(d, vgv) for d in dos]
        dvl = [tn(a, d) for a, d in zip(pls, dos)]
        dvs = tn(jnp.concatenate(pgs, 0), jnp.concatenate(dos, 0))
        pfs, pgf = [a.astype(F32) for a in pls], [a.astype(F32) for a in pgs]
        deltas = [
            (a * d).sum(-1, keepdims=True) + (b * e).sum(-1, keepdims=True) for a, d, b, e in zip(pfs, dls, pgf, dgs)
        ]
        sls = [(a * (d - t) * scale).astype(BF) for a, d, t in zip(pfs, dls, deltas)]
        sgs = [(a * (d - t) * scale).astype(BF) for a, d, t in zip(pgf, dgs, deltas)]
        gqs = [(mm(a, k) + mm(b, kgv)).astype(BF) for a, b, k in zip(sls, sgs, ks)]
        dkl = [tn(a, q) for a, q in zip(sls, qs)]
        dks = tn(jnp.concatenate(sgs, 0), jnp.concatenate(qs, 0))
        for h in (0, 1):
            gt[out_box(tiles[h], 0)] = gqs[h]
        for h in (0, 1):
            dkp[wins[h]] += dkl[h]
            dvp[wins[h]] += dvl[h]
        dkg[...] += dks
        dvg[...] += dvs

    def home_q(j):
        return remote(box(j, 0), spot(0, 1).at[0], dssem.at[j], drsem.at[me], chip(j))

    home_q_own = pltpu.make_async_copy(box(me, 0), spot(0, 1).at[0], lsem.at[10])

    @pl.loop(1, 9)
    def _(n):
        j = lax.rem(me + n, 8)
        backward(j)

        @pl.when(n < 8)
        def _():
            home_q(j).start()

    home_q_own.start()

    def home(sems, t0, n):
        s, d = sems
        return [
            remote(boxes(j, t0, n), spot(t0, n), s.at[k], d.at[k], where) for k, (j, where) in enumerate(peers)
        ]

    def split(a):
        high = a.astype(BF)
        return high, (a - high.astype(F32)).astype(BF)

    both = jnp.concatenate([jnp.concatenate(split(dkg[...]), 0), jnp.concatenate(split(dvg[...]), 0)], 1)

    @pl.loop(0, 16)
    def _(i):
        inner = pl.ds(al(i * 128 + BLOCK, 64), 128)
        put = (pos == i * 128 + sub).astype(F32).astype(BF)
        extra = mm(jnp.concatenate([put, put], 1), both)
        gt[out_box(i, 1)] = (dkp[inner] + extra[:, :128]).astype(BF)
        gt[out_box(i, 2)] = (dvp[inner] + extra[:, 128:]).astype(BF)

    home_kv = home((essem, ersem), 1, 2)
    for cp in home_kv:
        cp.start()
    home_kv_own = pltpu.make_async_copy(boxes(me, 1, 2), spot(1, 2), lsem.at[11])
    home_kv_own.start()

    for cp in ctx_out:
        cp.wait()
    ctx_own.wait()
    turn(3)
    for n in range(8):
        piece(red_o, cot, n, 3, 1)
    red_o.start_y()
    for cp in tsend + csend + wsend:
        cp.wait_send()
    for n in range(1, 8):
        j = lax.rem(me + n, 8)
        home_q(j).wait_send()
        remote(box(j, 0), spot(0, 1).at[0], dssem.at[j], drsem.at[j], sib).wait_recv()
    home_q_own.wait()
    turn(0)
    for n in range(8):
        piece(red_q, tok, n, 0, 1)
    red_q.start_y()
    for cp in home_kv:
        cp.wait()
    home_kv_own.wait()

    part = cot
    docs = (x2, xr, xl, x)
    to_sib = [remote(part.at[o, other], pr.at[o], sssem.at[o], srsem.at[o], sib) for o in range(4)]

    def tokens_part(o):
        rows = pl.ds(al(docs[o] * CHIP_ROWS, CHIP_ROWS), CHIP_ROWS)

        @pl.loop(0, 8)
        def _(n):
            cols = pl.ds(al(n * 512, 512), 512)
            a = jnp.concatenate([g[t, rows] for t in range(3)], 1)
            b = jnp.concatenate([w[t, cols] for t in range(3)], 1)
            part[o, :, cols] = nt(a, b).astype(BF)

        to_sib[o].start()

    xc = [
        remote(pr.at[0, pl.ds(0, 64)], xa.at[pl.ds(0, 64)], xssem.at[0], xrsem.at[0], right),
        remote(pr.at[0, pl.ds(64, 64)], xa.at[pl.ds(64, 64)], xssem.at[1], xrsem.at[1], left),
        remote(pr.at[1], xf.at[0], xssem.at[2], xrsem.at[2], right),
        remote(pr.at[2], xf.at[1], xssem.at[3], xrsem.at[3], left),
    ]

    def sum_rows(o, extra=None):
        @pl.loop(0, 8)
        def _(n):
            cols = pl.ds(al(n * 512, 512), 512)
            for h in range(2):
                rows = pl.ds(h * 64, 64)
                own_half = pl.ds(al(c * ROWS + h * 64, 64), 64)
                total = part[o, own_half, cols].astype(F32) + pr[o, rows, cols].astype(F32)
                if extra is not None and extra == h:
                    total += xa[rows, cols].astype(F32)
                pr[o, rows, cols] = total.astype(BF)

    tokens_part(0)
    turn(1)
    turn(2)
    to_sib[0].wait_recv()
    sum_rows(0)
    xc[0].start()
    xc[1].start()
    for n in range(4):
        piece(red_v, tok, n, 1, 2)
    tokens_part(1)
    tokens_part(2)
    red_o.dep_z()
    red_o.dep_y()
    for n in range(4, 8):
        piece(red_v, tok, n, 1, 2)
    red_v.start_y()
    to_sib[1].wait_recv()
    xc[0].wait_recv()
    sum_rows(1, 0)
    xc[2].start()
    to_sib[2].wait_recv()
    xc[1].wait_recv()
    sum_rows(2, 1)
    xc[3].start()
    red_q.dep_z()
    red_q.dep_y()
    red_o.mid_z()
    red_o.mid_y()
    tokens_part(3)
    red_v.dep_z()
    red_v.dep_y()
    red_o.last_z()
    red_o.last_y()
    red_q.mid_z()
    red_q.mid_y()
    red_q.last_z()
    red_q.last_y()
    to_sib[3].wait_recv()
    red_v.mid_z()
    red_v.mid_y()

    xc[2].wait_recv()
    xc[3].wait_recv()

    to_sib[3].wait_send()

    @pl.loop(0, 8)
    def _(n):
        cols = pl.ds(al(n * 512, 512), 512)
        total = part[3, own, cols].astype(F32) + pr[3, :, cols].astype(F32)
        total += xf[0, :, cols].astype(F32) + xf[1, :, cols].astype(F32)
        part[3, other, cols] = total.astype(BF)

    gt_copy = pltpu.make_async_copy(part.at[3, other], gt_out, lsem.at[12])
    gt_copy.start()
    red_v.last_z()
    red_v.last_y()

    outs = (gq_out, gk_out, gv_out, go_out)
    final = [remote(fs.at[1, t], outs[t], fssem.at[t], frsem.at[t], sib) for t in range(4)]
    final_own = [pltpu.make_async_copy(fs.at[0, t], outs[t], flsem.at[t]) for t in range(4)]

    @pl.when(c == p)
    def _():
        def put(t0):
            def run(head, n, value):
                lanes = pl.ds(head * 128, 128)
                for s in range(2):
                    core = c if s == 0 else 1 - c
                    got = value(pl.ds(al(core * 256, 256), 256))
                    if t0 + n < 3:
                        fs[s, t0 + n, :, lanes] = got.T
                    else:
                        fs[s, 3, lanes, :] = got

            return run

        red_o.result(put(3))
        final[3].start()
        final_own[3].start()
        red_q.result(put(0))
        final[0].start()
        final_own[0].start()
        red_v.result(put(1))
        for t in (1, 2):
            final[t].start()
            final_own[t].start()
        for t in range(4):
            final[t].wait_send()
            final_own[t].wait()

    @pl.when(c != p)
    def _():
        for cp in final:
            cp.wait_recv()

    red_o.drain()
    red_q.drain()
    red_v.drain()
    for cp in to_sib[:3] + xc:
        cp.wait_send()
    gt_copy.wait()


def on_device(tokens, cotangent, w_query, w_key, w_value, w_output, global_pos, pattern):
    dma = pltpu.SemaphoreType.DMA
    vm = pltpu.VMEM
    square = jax.ShapeDtypeStruct((256, 256), F32)
    grad_tokens, gq, gk, gv, go = pl.pallas_call(
        kernel,
        out_shape=(jax.ShapeDtypeStruct((ROWS, D), BF), square, square, square, square),
        in_specs=[pl.BlockSpec(memory_space=pltpu.SMEM), pl.BlockSpec(memory_space=pltpu.VMEM)] + [ANY] * 6,
        out_specs=(ANY,) * 5,
        scratch_shapes=[
            vm((4, CHIP_ROWS, D), BF),
            vm((4, CHIP_ROWS, D), BF),
            vm((3, D, 256), BF),
            vm((256, D), BF),
            vm((4, 2176, HDIM), BF),
            vm((4, 1024, 256), BF),
            vm((4, 256, 1024), BF),
            vm((2, 8, 8, 256), F32),
            vm((8, 2, 8, 256), F32),
            vm((128, HDIM), BF), vm((128, HDIM), BF), vm((128, HDIM), F32), vm((128, HDIM), F32),
            vm((2176, HDIM), F32), vm((2176, HDIM), F32),
            vm((4, ROWS, D), BF),
            vm((ROWS, D), BF),
            vm((2, ROWS, D), BF),
            vm((2, 4, 256, 256), F32),
            *reduce_scratch(HALF_O),
            *reduce_scratch(HALF_Q),
            *reduce_scratch(HALF_KV),
            dma((2, 9)), dma((2, 9)), dma((12,)), dma((8, 2)), dma((13,)), dma((8,)), dma((8,)),
            dma((8,)), dma((8,)), dma((8,)), dma((8,)), dma((7,)), dma((7,)), dma((8,)), dma((8,)),
            dma((7,)), dma((7,)), dma((4,)), dma((4,)), dma((4,)), dma((4,)), dma((4,)), dma((4,)), dma((4,)),
        ],
        compiler_params=pltpu.CompilerParams(
            collective_id=0, has_side_effects=True, vmem_limit_bytes=63 << 20
        ),
        cost_estimate=pl.CostEstimate(flops=25 * 10**9, bytes_accessed=60 << 20, transcendentals=10**6),
    )(pattern, global_pos, tokens[0], cotangent[0], w_query, w_key, w_value, w_output)
    return grad_tokens[None], gq, gk, gv, go


def solution(mesh):
    in_specs = (
        P("fsdp", "seq", None),
        P("fsdp", "seq", None),
        P(None, "fsdp"),
        P(None, "fsdp"),
        P(None, "fsdp"),
        P("fsdp", None),
        P(),
        P(None, "seq", None),
    )
    out_specs = (
        P("fsdp", "seq", None),
        P("seq", "fsdp"),
        P("seq", "fsdp"),
        P("seq", "fsdp"),
        P("fsdp", "seq"),
    )
    return jax.shard_map(
        on_device, mesh=mesh, in_specs=in_specs, out_specs=out_specs, check_vma=False
    )
```

```python
import jax
import jax.numpy as jnp
from jax import lax
from jax.experimental import pallas as pl
from jax.experimental.pallas import tpu as pltpu
from jax.sharding import PartitionSpec as P

BLOCK = 64
HDIM = 128
ROWS = 128
CHIP_ROWS = 256
D = 4096
BF = jnp.bfloat16
F32 = jnp.float32
MESH = pl.DeviceIdType.MESH
ANY = pl.BlockSpec(memory_space=pl.ANY)
NT = (((1,), (1,)), ((), ()))
TN = (((0,), (0,)), ((), ()))


def place():
    f = lax.axis_index("fsdp")
    s = lax.axis_index("seq")
    x, p = lax.div(f, 2), lax.rem(f, 2)
    yh, z, c = lax.div(s, 8), lax.rem(lax.div(s, 2), 4), lax.rem(s, 2)
    return x, 2 * yh + p, z, c


def device(x, y, z, c):
    return {"seq": lax.div(y, 2) * 8 + z * 2 + c, "fsdp": x * 2 + lax.rem(y, 2)}


def mod4(v):
    return lax.rem(v + 4, 4)


def al(v, n):
    return pl.multiple_of(v, n)


def remote(src, dst, send, recv, where):
    return pltpu.make_async_remote_copy(
        src_ref=src, dst_ref=dst, send_sem=send, recv_sem=recv, device_id=where, device_id_type=MESH
    )


def meet(devices):
    barrier = pltpu.get_barrier_semaphore()
    for where in devices:
        pl.semaphore_signal(barrier, inc=1, device_id=where, device_id_type=MESH)
    pl.semaphore_wait(barrier, len(devices))


def chip_peer(x, y, z, c, k):
    j = lax.rem(lax.div(y, 2) * 4 + z + k, 8)
    return j, device(x, lax.div(j, 4) * 2 + lax.rem(y, 2), lax.rem(j, 4), c)


HALF_KV, HALF_Q, HALF_O = 256, 128, 128


class Reduce:
    def __init__(self, at, rows, bufs, sems):
        self.at, self.rows = at, rows
        self.wz, self.za, self.zf, self.yf, self.wy, self.yg, self.zb, self.zg = bufs
        ss, rs = sems
        half = rows // 2
        lo, hi = pl.ds(0, half), pl.ds(half, half)
        self.lo, self.hi = lo, hi
        wz, za, zf, yf, wy, yg, zb, zg = bufs
        up, down, yh = at["up"], at["down"], at["yh"]
        front, rear, above, below = at["front"], at["rear"], at["above"], at["below"]
        up_i, down_i = lax.div(up, 2), lax.div(down, 2)
        self.up_i, self.down_i, self.yh = up_i, down_i, yh

        def cp(i, src, dst, where):
            return remote(src, dst, ss.at[i], rs.at[i], where)

        self.z = [
            cp(0, wz.at[0, 0], za.at[0], front),
            cp(1, wz.at[0, 1], za.at[1], rear),
            cp(2, wz.at[1, 1], zf.at[0, 1], front),
            cp(3, wz.at[2, 0], zf.at[1, 0], rear),
            cp(4, wz.at[1, 0], zf.at[0, 0], front),
            cp(5, wz.at[2, 1], zf.at[1, 1], rear),
        ]
        self.give = [
            cp(6, wy.at[1 - yh, :, lo], yg.at[0, :, lo], above),
            cp(7, wy.at[1 - yh, :, hi], yg.at[1, :, lo], below),
        ]
        self.free = [
            cp(8, wy.at[up_i, :, hi], yg.at[0, :, hi], above),
            cp(9, wy.at[down_i, :, lo], yg.at[1, :, lo], below),
        ]
        self.dep = [
            cp(6, wy.at[up_i, :, lo], yg.at[0, :, lo], above),
            cp(7, wy.at[down_i, :, hi], yg.at[1, :, hi], below),
        ]
        self.zy_give = [
            cp(10, wz.at[3, 1 - yh, lo], yf.at[0, lo], above),
            cp(11, wz.at[3, 1 - yh, hi], yf.at[1, lo], below),
        ]
        self.zy_pass = [
            cp(12, wz.at[3, up_i], yf.at[0], above),
            cp(13, wz.at[3, down_i], yf.at[1], below),
        ]
        self.yz = [
            cp(14, wy.at[yh, 0, lo], zb.at[0], front),
            cp(15, wy.at[yh, 0, hi], zb.at[1], rear),
            cp(16, wy.at[yh, 1], zg.at[0], front),
            cp(17, wy.at[yh, 2], zg.at[1], rear),
        ]

    def add(self, rows, dst, *srcs):
        @pl.loop(0, rows // 64)
        def _(i):
            r = pl.ds(al(i * 64, 64), 64)
            total = dst[r].astype(F32)
            for s in srcs:
                total += s[r].astype(F32)
            dst[r] = total.astype(BF)

    def start_y(self):
        @pl.when(self.at["owner"])
        def _():
            for cp in self.give:
                cp.start()

        @pl.when(self.at["middle"])
        def _():
            for cp in self.free:
                cp.start()

    def dep_z(self):
        self.z[0].wait_recv()
        self.add(self.rows, self.wz.at[1, 0], self.za.at[0])
        self.z[4].start()
        self.z[1].wait_recv()
        self.add(self.rows, self.wz.at[2, 1], self.za.at[1])
        self.z[5].start()

    def dep_y(self):
        half = self.rows // 2

        @pl.when(self.at["middle"])
        def _():
            for i, (idx, part) in enumerate(((self.up_i, self.lo), (self.down_i, self.hi))):
                self.give[i].wait_recv()
                for o in range(4):
                    self.add(half, self.wy.at[idx, o, part], self.yg.at[i, o, self.lo])
                self.dep[i].start()

    def mid_z(self):
        for i in (2, 3, 4, 5):
            self.z[i].wait_recv()
        for ab in range(2):
            self.add(self.rows, self.wz.at[3, ab], self.zf.at[0, ab], self.zf.at[1, ab])

        @pl.when(self.at["owner"])
        def _():
            for cp in self.zy_give:
                cp.start()

    def mid_y(self):
        @pl.when(self.at["owner"])
        def _():
            for cp in self.free + self.dep:
                cp.wait_recv()
            for cp in self.give:
                cp.wait_send()
            for o in range(4):
                self.add(self.rows, self.wy.at[self.yh, o], self.yg.at[0, o], self.yg.at[1, o])
                if o == 0:
                    self.yz[0].start()
                    self.yz[1].start()

    def last_z(self):
        half = self.rows // 2

        @pl.when(self.at["middle"])
        def _():
            for i, (idx, part) in enumerate(((self.up_i, self.lo), (self.down_i, self.hi))):
                self.zy_give[i].wait_recv()
                self.add(half, self.wz.at[3, idx, part], self.yf.at[i, self.lo])
                self.zy_pass[i].start()

    def last_y(self):
        half = self.rows // 2

        @pl.when(self.at["owner"])
        def _():
            self.yz[0].wait_recv()
            self.add(half, self.wy.at[self.yh, 1, self.lo], self.zb.at[0])
            self.yz[2].start()
            self.yz[1].wait_recv()
            self.add(half, self.wy.at[self.yh, 2, self.hi], self.zb.at[1])
            self.yz[3].start()

    def result(self, put):
        for cp in self.zy_pass:
            cp.wait_recv()
        for n in range(self.rows // 128):
            rows = pl.ds(n * 128, 128)
            put(0, n, lambda cols: (
                self.wz[3, self.yh, rows, cols].astype(F32)
                + self.yf[0, rows, cols].astype(F32) + self.yf[1, rows, cols].astype(F32)))
        for cp in self.yz[2:]:
            cp.wait_recv()
        for n in range(self.rows // 128):
            rows = pl.ds(n * 128, 128)
            put(1, n, lambda cols: (
                self.wy[self.yh, 3, rows, cols].astype(F32)
                + self.zg[0, rows, cols].astype(F32) + self.zg[1, rows, cols].astype(F32)))

    def drain(self):
        for cp in self.z:
            cp.wait_send()

        @pl.when(self.at["owner"])
        def _():
            for cp in self.zy_give + self.yz:
                cp.wait_send()

        @pl.when(self.at["middle"])
        def _():
            for cp in self.free + self.dep + self.zy_pass:
                cp.wait_send()


def reduce_scratch(rows):
    vm = pltpu.VMEM
    return [
        vm((4, 2, rows, 512), BF), vm((2, rows, 512), BF), vm((2, 2, rows, 512), BF), vm((2, rows, 512), BF),
        vm((2, 4, rows, 512), BF), vm((2, 4, rows, 512), BF), vm((2, rows // 2, 512), BF), vm((2, rows, 512), BF),
        pltpu.SemaphoreType.DMA((18,)), pltpu.SemaphoreType.DMA((18,)),
    ]


def kernel(
    pat, gpos, tok_in, cot_in, wq, wk, wv, wo,
    gt_out, gq_out, gk_out, gv_out, go_out,
    tok, cot, w, wov, r, g, gt, mask, masks, kg, vg, dkg, dvg, dkp, dvp, pr, xa, xf, fs,
    *rest,
):
    (o_bufs, o_sems), (q_bufs, q_sems), (v_bufs, v_sems) = [(rest[i : i + 8], rest[i + 8 : i + 10]) for i in (0, 10, 20)]
    (ssem, rsem, wssem, wrsem, lsem, mssem, mrsem, assem, arsem, bssem, brsem,
     cssem, crsem, dssem, drsem, essem, ersem, sssem, srsem, xssem, xrsem, fssem, frsem, flsem) = rest[30:]
    x, y, z, c = place()
    p, yh = lax.rem(y, 2), lax.div(y, 2)
    seq = lax.axis_index("seq")
    xr, xl, x2 = mod4(x + 1), mod4(x - 1), mod4(x + 2)
    zr, zl, z2 = mod4(z + 1), mod4(z - 1), mod4(z + 2)
    up, down = mod4(y + 1), mod4(y - 1)
    right, left = device(xr, y, z, c), device(xl, y, z, c)
    sib = device(x, y, z, 1 - c)
    me = yh * 4 + z
    my_doc = lax.div(me, 2) * 2 + p
    peers = [chip_peer(x, y, z, c, k) for k in range(1, 8)]

    meet(
        [right, left, sib]
        + [device(x, v, z, core) for v in (up, down) for core in (0, 1)]
        + [where for _, where in peers]
    )
    own = pl.ds(al(c * ROWS, ROWS), ROWS)
    other = pl.ds(al((1 - c) * ROWS, ROWS), ROWS)
    first = pl.ds(al(c * ROWS, 64), 64)
    second = pl.ds(al(c * ROWS + 64, 64), 64)

    def sends(a, given, buf):
        def cp(kind, src, dst, where):
            return remote(src, dst, ssem.at[a, kind], rsem.at[a, kind], where)

        return [
            cp(0, given, buf.at[x, own], right),
            cp(1, given, buf.at[x, own], left),
            cp(2, given, buf.at[x, own], sib),
            cp(3, buf.at[xl, first], buf.at[xl, first], right),
            cp(4, buf.at[xr, second], buf.at[xr, second], left),
            cp(5, buf.at[xl, own], buf.at[xl, own], sib),
            cp(6, buf.at[xr, own], buf.at[xr, own], sib),
            cp(7, buf.at[x2, first], buf.at[x2, first], sib),
            cp(8, buf.at[x2, second], buf.at[x2, second], sib),
        ]

    tsend = sends(0, tok_in, tok)
    csend = sends(1, cot_in, cot)
    wdev = device(x, mod4(y + 1 + 2 * c), z, p)
    zhalf = lax.rem(z, 2)
    sources = (wq, wk, wv, wo)

    def quarter(t, ref, h, n):
        size = 1024 if t < 3 else 64
        rows = pl.ds(al((2 * h + n) * size, size), size)
        return ref.at[t, rows] if ref is w else ref.at[rows]

    def held(t):
        return w if t < 3 else wov

    wsend = [
        remote(quarter(t, src, zhalf, c), quarter(t, held(t), zhalf, c), wssem.at[t], wrsem.at[t, c], wdev)
        for t, src in enumerate(sources)
    ]
    zdev = (device(x, y, zr, c), device(x, y, zl, c))
    wpass = [
        [
            remote(
                quarter(t, held(t), zhalf, n), quarter(t, held(t), zhalf, n),
                wssem.at[4 + 2 * t + n], wrsem.at[4 + t, n], zdev[n],
            )
            for n in (0, 1)
        ]
        for t in range(4)
    ]

    wlocal = [pltpu.make_async_copy(src, w.at[t], lsem.at[t]) for t, src in enumerate((wq, wk, wv))]
    wlocal.append(pltpu.make_async_copy(wo, wov, lsem.at[3]))
    tlocal = pltpu.make_async_copy(tok_in, tok.at[x, own], lsem.at[4])
    clocal = pltpu.make_async_copy(cot_in, cot.at[x, own], lsem.at[5])

    for k in (0, 1, 2):
        tsend[k].start()
    for cp in wsend:
        cp.start()
    tlocal.start()
    clocal.start()

    @pl.when(c == p)
    def _():
        for cp in wlocal:
            cp.start()

    kb = lax.div(lax.broadcasted_iota(jnp.int32, (8, 256), 1), 64)
    upper = lax.broadcasted_iota(jnp.int32, (8, 256), 0) == 0

    @pl.loop(0, 8)
    def _(d):
        prev0 = jnp.where(seq > 0, pat[d, 0, 0], 0)
        next0, prev1 = pat[d, 0, 1], pat[d, 1, 0]
        next1 = jnp.where(seq < 15, pat[d, 1, 1], 0)
        m0 = jnp.where(kb == 0, prev0, jnp.where(kb == 1, 1, jnp.where(kb == 2, next0, 0)))
        m1 = jnp.where(kb == 0, 0, jnp.where(kb == 1, prev1, jnp.where(kb == 2, 1, next1)))
        mask[c, d] = jnp.where(jnp.where(upper, m0, m1) == 1, 0.0, -jnp.inf)

    for t in (1, 2):
        r[t, :BLOCK] = jnp.zeros((BLOCK, HDIM), BF)
        r[t, BLOCK + 2048 :] = jnp.zeros((BLOCK, HDIM), BF)

    mask_sib = remote(mask.at[c], mask.at[c], mssem.at[7], mrsem.at[7], sib)
    mask_sib.start()
    mask_sib.wait()
    mask_out = [
        remote(mask.at[:, lax.div(j, 2) * 2 + p], masks.at[me], mssem.at[k], mrsem.at[k], where)
        for k, (j, where) in enumerate(peers)
    ]
    for cp in mask_out:
        cp.start()
    mask_own = pltpu.make_async_copy(mask.at[:, my_doc], masks.at[me], lsem.at[8])
    mask_own.start()

    def relay(copies):
        copies[0].wait_recv()
        copies[3].start()
        copies[5].start()
        copies[1].wait_recv()
        copies[4].start()
        copies[6].start()

    def weights_pass():
        @pl.when(c != p)
        def _():
            for t in range(4):
                for n in (0, 1):
                    ref = quarter(t, held(t), zhalf, n)
                    remote(ref, ref, wssem.at[t], wrsem.at[t, n], sib).wait_recv()
                    wpass[t][n].start()

    def weights_here(ts):
        @pl.when(c == p)
        def _():
            for t in ts:
                wlocal[t].wait()

        @pl.when(c != p)
        def _():
            for t in ts:
                for n in (0, 1):
                    wpass[t][n].wait()

    mine = pl.ds(al(me * CHIP_ROWS + BLOCK, 64), CHIP_ROWS)

    def boxes(j, t0, n):
        return gt.at[pl.ds(t0, n), :, pl.ds(al(j * HDIM, HDIM), HDIM)]

    def box(j, t):
        return gt.at[t, :, pl.ds(al(j * HDIM, HDIM), HDIM)]

    def chip(j):
        return device(x, lax.div(j, 4) * 2 + p, lax.rem(j, 4), c)

    def project(doc, t):
        got = jnp.dot(tok[doc], w[t], preferred_element_type=F32).astype(BF)
        gt[t, :, pl.ds(al(doc * 256, 256), 256)] = got

    def project_near(t):
        @pl.loop(0, 3)
        def _(n):
            project(lax.rem(x + n + lax.div(n, 2), 4), t)

    def qkv(j):
        return remote(boxes(j, 0, 3), r.at[pl.ds(0, 3), mine], assem.at[j], arsem.at[me], chip(j))

    qkv_own = pltpu.make_async_copy(boxes(me, 0, 3), r.at[pl.ds(0, 3), mine], lsem.at[6])

    def send_qkv(last):
        for n in range(8):
            j = lax.rem(me + n, 8)
            here = lax.div(j, 2) == x2
            here = here if last else jnp.logical_not(here)
            if n == 0:

                @pl.when(here)
                def _():
                    qkv_own.start()

            else:

                @pl.when(here)
                def _():
                    qkv(j).start()

    weights_pass()
    relay(tsend)
    for k in (0, 1, 2):
        csend[k].start()
    tlocal.wait()
    clocal.wait()
    tsend[2].wait_recv()
    tsend[5].wait_recv()
    tsend[6].wait_recv()
    weights_here((0,))
    project_near(0)
    weights_here((1,))
    project_near(1)
    tsend[3].wait_recv()
    tsend[7].start()
    tsend[4].wait_recv()
    tsend[8].start()
    weights_here((2,))
    project_near(2)
    send_qkv(False)
    tsend[7].wait_recv()
    tsend[8].wait_recv()

    @pl.loop(0, 3)
    def _(t):
        project(x2, t)

    send_qkv(True)

    relay(csend)
    weights_here((3,))

    def back(doc):
        got = lax.dot_general(cot[doc], wov[...], NT, preferred_element_type=F32).astype(BF)
        gt[3, :, pl.ds(al(doc * 256, 256), 256)] = got
        for h in (0, 1):
            j = 2 * doc + h

            @pl.when(j != me)
            def _():
                remote(box(j, 3), r.at[3, mine], bssem.at[j], brsem.at[me], chip(j)).start()

            @pl.when(j == me)
            def _():
                pltpu.make_async_copy(box(j, 3), r.at[3, mine], lsem.at[7]).start()

    csend[2].wait_recv()
    back(x)
    csend[5].wait_recv()
    back(xl)
    csend[6].wait_recv()
    back(xr)

    for n in range(1, 8):
        j = lax.rem(me + n, 8)
        qkv(j).wait_send()
        remote(boxes(j, 0, 3), r.at[pl.ds(0, 3), mine], assem.at[j], arsem.at[j], sib).wait_recv()
    qkv_own.wait()
    for cp in mask_out:
        cp.wait()
    mask_own.wait()
    scale = HDIM**-0.5
    pos = jnp.broadcast_to(gpos[pl.ds(my_doc, 1), :], (128, 128))
    pos_t = pos.T
    lane = lax.broadcasted_iota(jnp.int32, (128, 128), 1)
    sub = lax.broadcasted_iota(jnp.int32, (128, 128), 0)
    low = lax.broadcasted_iota(jnp.int32, (128, 256), 0) < BLOCK

    def nt(a, b):
        return lax.dot_general(a, b, NT, preferred_element_type=F32)

    def tn(a, b):
        return lax.dot_general(a, b, TN, preferred_element_type=F32)

    def mm(a, b):
        return jnp.dot(a, b, preferred_element_type=F32)

    dkg[...] = jnp.zeros_like(dkg)
    dvg[...] = jnp.zeros_like(dvg)

    @pl.loop(0, 16)
    def _(i):
        rows = pl.ds(al(i * 128 + BLOCK, 64), 128)
        pick = (pos_t == i * 128 + lane).astype(F32).astype(BF)
        dkg[...] += mm(pick, r[1, rows])
        dvg[...] += mm(pick, r[2, rows])

    kg[...] = dkg[...].astype(BF)
    vg[...] = dvg[...].astype(BF)
    wz, wy = v_bufs[0], v_bufs[4]

    def saved(i):
        return (lax.div(i, 4), lax.rem(lax.div(i, 2), 2), pl.ds(al(lax.rem(i, 2) * 128, 128), 128))

    def forward(j):
        tiles = (2 * j, 2 * j + 1)
        rows = [pl.ds(al(i * 128 + BLOCK, 64), 128) for i in tiles]
        wins = [pl.ds(al(i * 128, 128), 256) for i in tiles]
        qs = [r[0, a] for a in rows]
        ks, vs = [r[1, a] for a in wins], [r[2, a] for a in wins]
        kgv, vgv = kg[...], vg[...]
        sls = [nt(q, k) for q, k in zip(qs, ks)]
        sgs = [nt(q, kgv) * scale for q in qs]
        for h in (0, 1):
            seen = masks[j, h]
            sls[h] = sls[h] * scale + jnp.where(low, seen[0:1], seen[1:2])
        tops = [jnp.maximum(a.max(-1, keepdims=True), b.max(-1, keepdims=True)) for a, b in zip(sls, sgs)]
        els = [jnp.exp(a - t) for a, t in zip(sls, tops)]
        egs = [jnp.exp(a - t) for a, t in zip(sgs, tops)]
        invs = [1.0 / (a.sum(-1, keepdims=True) + b.sum(-1, keepdims=True)) for a, b in zip(els, egs)]
        pls = [(a * t).astype(BF) for a, t in zip(els, invs)]
        pgs = [(a * t).astype(BF) for a, t in zip(egs, invs)]
        ctx = [(mm(a, v) + mm(b, vgv)).astype(BF) for a, b, v in zip(pls, pgs, vs)]
        for h in (0, 1):
            a, b, rr = saved(tiles[h])
            wz[a, b, rr, pl.ds(0, 256)] = pls[h]
            wz[a, b, rr, pl.ds(256, 128)] = pgs[h]
            wy[lax.div(j, 4), lax.rem(j, 4), pl.ds(h * 128, 128), pl.ds(0, 128)] = ctx[h]

    pl.loop(0, 5)(forward)
    csend[3].wait_recv()
    csend[7].start()
    csend[4].wait_recv()
    csend[8].start()
    csend[7].wait_recv()
    csend[8].wait_recv()
    back(x2)
    pl.loop(5, 8)(forward)

    def ctx_box(j):
        return wy.at[lax.div(j, 4), lax.rem(j, 4), pl.ds(0, 256), pl.ds(0, 128)]

    def spot(t0, n):
        rows = pl.ds(al(lax.div(me, 2) * CHIP_ROWS, CHIP_ROWS), CHIP_ROWS)
        return g.at[pl.ds(t0, n), rows, pl.ds(al(lax.rem(me, 2) * HDIM, HDIM), HDIM)]

    def spot_o():
        rows = pl.ds(al(lax.div(me, 2) * CHIP_ROWS, CHIP_ROWS), CHIP_ROWS)
        return g.at[3, rows, pl.ds(al(lax.rem(me, 2) * HDIM, HDIM), HDIM)]

    ctx_out = [
        remote(ctx_box(j), spot_o(), cssem.at[k], crsem.at[k], where) for k, (j, where) in enumerate(peers)
    ]
    for cp in ctx_out:
        cp.start()
    ctx_own = pltpu.make_async_copy(ctx_box(me), spot_o(), lsem.at[9])
    ctx_own.start()

    at = {
        "up": up, "down": down, "yh": yh, "owner": c == p, "middle": c != p,
        "front": device(x, y, zr, c), "rear": device(x, y, zl, c),
        "above": device(x, up, z, c), "below": device(x, down, z, c),
    }
    groups = (z2, zr, zl, z)
    order = [(0, 0), (0, 1), (1, 1), (2, 0), (1, 0), (2, 1), (3, 0), (3, 1)]
    red_o = Reduce(at, HALF_O, o_bufs, o_sems)
    red_q = Reduce(at, HALF_Q, q_bufs, q_sems)
    red_v = Reduce(at, HALF_KV, v_bufs, v_sems)

    def turn(t):
        for i in range(4):
            rows = pl.ds(i * 256, 256)
            gt[t, :, rows] = g[t, rows].T

    def piece(red, src, n, t0, count):
        o, ab = order[n]

        @pl.loop(0, 2)
        def _(h):
            lanes = pl.ds(al(h * 256, 256), 256)
            here = pl.ds(al(ab * 2048 + groups[o] * 512 + h * 256, 256), 256)
            left_side = gt[pl.ds(t0, count)].reshape(count * 256, 1024)
            acc = mm(left_side, src[:, :, here].reshape(1024, 256)).astype(BF)
            for t in range(count):
                rows = pl.ds(t * 128, 128)
                red.wz[o, ab, rows, lanes] = acc[t * 256 : t * 256 + 128]
                red.wy[ab, o, rows, lanes] = acc[t * 256 + 128 : t * 256 + 256]

        if n < 4:
            red.z[n].start()

    for j in range(8):

        @pl.when(j != me)
        def _():
            remote(box(j, 3), r.at[3, mine], bssem.at[j], brsem.at[j], sib).wait_send()

    pltpu.make_async_copy(box(me, 3), r.at[3, mine], lsem.at[7]).wait()

    for j in range(8):

        @pl.when(j != me)
        def _():
            remote(box(j, 3), r.at[3, mine], bssem.at[j], brsem.at[j], sib).wait_recv()

    dkp[...] = jnp.zeros_like(dkp)
    dvp[...] = jnp.zeros_like(dvp)
    dkg[...] = jnp.zeros_like(dkg)
    dvg[...] = jnp.zeros_like(dvg)

    def out_box(i, t):
        j = lax.div(i, 2)
        return (t, pl.ds(al(lax.rem(i, 2) * 128, 128), 128), pl.ds(al(j * 128, 128), 128))

    def backward(j):
        tiles = (2 * j, 2 * j + 1)
        rows = [pl.ds(al(i * 128 + BLOCK, 64), 128) for i in tiles]
        wins = [pl.ds(al(i * 128, 128), 256) for i in tiles]
        qs, dos = [r[0, a] for a in rows], [r[3, a] for a in rows]
        ks, vs = [r[1, a] for a in wins], [r[2, a] for a in wins]
        kgv, vgv = kg[...], vg[...]
        spots = [saved(i) for i in tiles]
        pls = [wz[a, b, rr, pl.ds(0, 256)] for a, b, rr in spots]
        pgs = [wz[a, b, rr, pl.ds(256, 128)] for a, b, rr in spots]
        dls = [nt(d, v) for d, v in zip(dos, vs)]
        dgs = [nt(d, vgv) for d in dos]
        dvl = [tn(a, d) for a, d in zip(pls, dos)]
        dvs = tn(jnp.concatenate(pgs, 0), jnp.concatenate(dos, 0))
        pfs, pgf = [a.astype(F32) for a in pls], [a.astype(F32) for a in pgs]
        deltas = [
            (a * d).sum(-1, keepdims=True) + (b * e).sum(-1, keepdims=True) for a, d, b, e in zip(pfs, dls, pgf, dgs)
        ]
        sls = [(a * (d - t) * scale).astype(BF) for a, d, t in zip(pfs, dls, deltas)]
        sgs = [(a * (d - t) * scale).astype(BF) for a, d, t in zip(pgf, dgs, deltas)]
        gqs = [(mm(a, k) + mm(b, kgv)).astype(BF) for a, b, k in zip(sls, sgs, ks)]
        dkl = [tn(a, q) for a, q in zip(sls, qs)]
        dks = tn(jnp.concatenate(sgs, 0), jnp.concatenate(qs, 0))
        for h in (0, 1):
            gt[out_box(tiles[h], 0)] = gqs[h]
        for h in (0, 1):
            dkp[wins[h]] += dkl[h]
            dvp[wins[h]] += dvl[h]
        dkg[...] += dks
        dvg[...] += dvs

    def home_q(j):
        return remote(box(j, 0), spot(0, 1).at[0], dssem.at[j], drsem.at[me], chip(j))

    home_q_own = pltpu.make_async_copy(box(me, 0), spot(0, 1).at[0], lsem.at[10])

    @pl.loop(1, 9)
    def _(n):
        j = lax.rem(me + n, 8)
        backward(j)

        @pl.when(n < 8)
        def _():
            home_q(j).start()

    home_q_own.start()

    def home(sems, t0, n):
        s, d = sems
        return [
            remote(boxes(j, t0, n), spot(t0, n), s.at[k], d.at[k], where) for k, (j, where) in enumerate(peers)
        ]

    def split(a):
        high = a.astype(BF)
        return high, (a - high.astype(F32)).astype(BF)

    both = jnp.concatenate([jnp.concatenate(split(dkg[...]), 0), jnp.concatenate(split(dvg[...]), 0)], 1)

    @pl.loop(0, 16)
    def _(i):
        inner = pl.ds(al(i * 128 + BLOCK, 64), 128)
        put = (pos == i * 128 + sub).astype(F32).astype(BF)
        extra = mm(jnp.concatenate([put, put], 1), both)
        gt[out_box(i, 1)] = (dkp[inner] + extra[:, :128]).astype(BF)
        gt[out_box(i, 2)] = (dvp[inner] + extra[:, 128:]).astype(BF)

    home_kv = home((essem, ersem), 1, 2)
    for cp in home_kv:
        cp.start()
    home_kv_own = pltpu.make_async_copy(boxes(me, 1, 2), spot(1, 2), lsem.at[11])
    home_kv_own.start()

    for cp in ctx_out:
        cp.wait()
    ctx_own.wait()
    turn(3)
    for n in range(8):
        piece(red_o, cot, n, 3, 1)
    red_o.start_y()
    for cp in tsend + csend + wsend:
        cp.wait_send()
    for n in range(1, 8):
        j = lax.rem(me + n, 8)
        home_q(j).wait_send()
        remote(box(j, 0), spot(0, 1).at[0], dssem.at[j], drsem.at[j], sib).wait_recv()
    home_q_own.wait()
    turn(0)
    for n in range(8):
        piece(red_q, tok, n, 0, 1)
    red_q.start_y()
    for cp in home_kv:
        cp.wait()
    home_kv_own.wait()

    part = cot
    docs = (x2, xr, xl, x)
    to_sib = [remote(part.at[o, other], pr.at[o], sssem.at[o], srsem.at[o], sib) for o in range(4)]

    def tokens_part(o):
        rows = pl.ds(al(docs[o] * CHIP_ROWS, CHIP_ROWS), CHIP_ROWS)

        @pl.loop(0, 8)
        def _(n):
            cols = pl.ds(al(n * 512, 512), 512)
            a = jnp.concatenate([g[t, rows] for t in range(3)], 1)
            b = jnp.concatenate([w[t, cols] for t in range(3)], 1)
            part[o, :, cols] = nt(a, b).astype(BF)

        to_sib[o].start()

    xc = [
        remote(pr.at[0, pl.ds(0, 64)], xa.at[pl.ds(0, 64)], xssem.at[0], xrsem.at[0], right),
        remote(pr.at[0, pl.ds(64, 64)], xa.at[pl.ds(64, 64)], xssem.at[1], xrsem.at[1], left),
        remote(pr.at[1], xf.at[0], xssem.at[2], xrsem.at[2], right),
        remote(pr.at[2], xf.at[1], xssem.at[3], xrsem.at[3], left),
    ]

    def sum_rows(o, extra=None):
        @pl.loop(0, 8)
        def _(n):
            cols = pl.ds(al(n * 512, 512), 512)
            for h in range(2):
                rows = pl.ds(h * 64, 64)
                own_half = pl.ds(al(c * ROWS + h * 64, 64), 64)
                total = part[o, own_half, cols].astype(F32) + pr[o, rows, cols].astype(F32)
                if extra is not None and extra == h:
                    total += xa[rows, cols].astype(F32)
                pr[o, rows, cols] = total.astype(BF)

    tokens_part(0)
    tokens_part(1)
    to_sib[0].wait_recv()
    sum_rows(0)
    xc[0].start()
    xc[1].start()
    tokens_part(2)
    turn(1)
    turn(2)
    for n in range(0, 4):
        piece(red_v, tok, n, 1, 2)
    red_o.dep_z()
    red_o.dep_y()
    red_q.dep_z()
    red_q.dep_y()
    for n in range(4, 8):
        piece(red_v, tok, n, 1, 2)
    red_v.start_y()
    to_sib[1].wait_recv()
    xc[0].wait_recv()
    sum_rows(1, 0)
    xc[2].start()
    to_sib[2].wait_recv()
    xc[1].wait_recv()
    sum_rows(2, 1)
    xc[3].start()
    red_v.dep_z()
    red_v.dep_y()
    red_o.mid_z()
    red_o.mid_y()
    tokens_part(3)
    red_o.last_z()
    red_o.last_y()
    red_q.mid_z()
    red_q.mid_y()
    red_q.last_z()
    red_q.last_y()
    to_sib[3].wait_recv()
    red_v.mid_z()
    red_v.mid_y()

    xc[2].wait_recv()
    xc[3].wait_recv()

    to_sib[3].wait_send()

    @pl.loop(0, 8)
    def _(n):
        cols = pl.ds(al(n * 512, 512), 512)
        total = part[3, own, cols].astype(F32) + pr[3, :, cols].astype(F32)
        total += xf[0, :, cols].astype(F32) + xf[1, :, cols].astype(F32)
        part[3, other, cols] = total.astype(BF)

    gt_copy = pltpu.make_async_copy(part.at[3, other], gt_out, lsem.at[12])
    gt_copy.start()
    red_v.last_z()
    red_v.last_y()

    outs = (gq_out, gk_out, gv_out, go_out)
    final = [remote(fs.at[1, t], outs[t], fssem.at[t], frsem.at[t], sib) for t in range(4)]
    final_own = [pltpu.make_async_copy(fs.at[0, t], outs[t], flsem.at[t]) for t in range(4)]

    @pl.when(c == p)
    def _():
        def put(t0):
            def run(head, n, value):
                lanes = pl.ds(head * 128, 128)
                for s in range(2):
                    core = c if s == 0 else 1 - c
                    got = value(pl.ds(al(core * 256, 256), 256))
                    if t0 + n < 3:
                        fs[s, t0 + n, :, lanes] = got.T
                    else:
                        fs[s, 3, lanes, :] = got

            return run

        red_o.result(put(3))
        final[3].start()
        final_own[3].start()
        red_q.result(put(0))
        final[0].start()
        final_own[0].start()
        red_v.result(put(1))
        for t in (1, 2):
            final[t].start()
            final_own[t].start()
        for t in range(4):
            final[t].wait_send()
            final_own[t].wait()

    @pl.when(c != p)
    def _():
        for cp in final:
            cp.wait_recv()

    red_o.drain()
    red_q.drain()
    red_v.drain()
    for cp in to_sib[:3] + xc:
        cp.wait_send()
    gt_copy.wait()


def on_device(tokens, cotangent, w_query, w_key, w_value, w_output, global_pos, pattern):
    dma = pltpu.SemaphoreType.DMA
    vm = pltpu.VMEM
    square = jax.ShapeDtypeStruct((256, 256), F32)
    grad_tokens, gq, gk, gv, go = pl.pallas_call(
        kernel,
        out_shape=(jax.ShapeDtypeStruct((ROWS, D), BF), square, square, square, square),
        in_specs=[pl.BlockSpec(memory_space=pltpu.SMEM), pl.BlockSpec(memory_space=pltpu.VMEM)] + [ANY] * 6,
        out_specs=(ANY,) * 5,
        scratch_shapes=[
            vm((4, CHIP_ROWS, D), BF),
            vm((4, CHIP_ROWS, D), BF),
            vm((3, D, 256), BF),
            vm((256, D), BF),
            vm((4, 2176, HDIM), BF),
            vm((4, 1024, 256), BF),
            vm((4, 256, 1024), BF),
            vm((2, 8, 8, 256), F32),
            vm((8, 2, 8, 256), F32),
            vm((128, HDIM), BF), vm((128, HDIM), BF), vm((128, HDIM), F32), vm((128, HDIM), F32),
            vm((2176, HDIM), F32), vm((2176, HDIM), F32),
            vm((4, ROWS, D), BF),
            vm((ROWS, D), BF),
            vm((2, ROWS, D), BF),
            vm((2, 4, 256, 256), F32),
            *reduce_scratch(HALF_O),
            *reduce_scratch(HALF_Q),
            *reduce_scratch(HALF_KV),
            dma((2, 9)), dma((2, 9)), dma((12,)), dma((8, 2)), dma((13,)), dma((8,)), dma((8,)),
            dma((8,)), dma((8,)), dma((8,)), dma((8,)), dma((7,)), dma((7,)), dma((8,)), dma((8,)),
            dma((7,)), dma((7,)), dma((4,)), dma((4,)), dma((4,)), dma((4,)), dma((4,)), dma((4,)), dma((4,)),
        ],
        compiler_params=pltpu.CompilerParams(
            collective_id=0, has_side_effects=True, vmem_limit_bytes=63 << 20
        ),
        cost_estimate=pl.CostEstimate(flops=25 * 10**9, bytes_accessed=60 << 20, transcendentals=10**6),
    )(pattern, global_pos, tokens[0], cotangent[0], w_query, w_key, w_value, w_output)
    return grad_tokens[None], gq, gk, gv, go


def solution(mesh):
    in_specs = (
        P("fsdp", "seq", None),
        P("fsdp", "seq", None),
        P(None, "fsdp"),
        P(None, "fsdp"),
        P(None, "fsdp"),
        P("fsdp", None),
        P(),
        P(None, "seq", None),
    )
    out_specs = (
        P("fsdp", "seq", None),
        P("seq", "fsdp"),
        P("seq", "fsdp"),
        P("seq", "fsdp"),
        P("fsdp", "seq"),
    )
    return jax.shard_map(
        on_device, mesh=mesh, in_specs=in_specs, out_specs=out_specs, check_vma=False
    )
```

```python
import jax
import jax.numpy as jnp
from jax import lax
from jax.experimental import pallas as pl
from jax.experimental.pallas import tpu as pltpu
from jax.sharding import PartitionSpec as P

BLOCK = 64
HDIM = 128
ROWS = 128
CHIP_ROWS = 256
D = 4096
BF = jnp.bfloat16
F32 = jnp.float32
MESH = pl.DeviceIdType.MESH
ANY = pl.BlockSpec(memory_space=pl.ANY)
NT = (((1,), (1,)), ((), ()))
TN = (((0,), (0,)), ((), ()))


def place():
    f = lax.axis_index("fsdp")
    s = lax.axis_index("seq")
    x, p = lax.div(f, 2), lax.rem(f, 2)
    yh, z, c = lax.div(s, 8), lax.rem(lax.div(s, 2), 4), lax.rem(s, 2)
    return x, 2 * yh + p, z, c


def device(x, y, z, c):
    return {"seq": lax.div(y, 2) * 8 + z * 2 + c, "fsdp": x * 2 + lax.rem(y, 2)}


def mod4(v):
    return lax.rem(v + 4, 4)


def al(v, n):
    return pl.multiple_of(v, n)


def remote(src, dst, send, recv, where):
    return pltpu.make_async_remote_copy(
        src_ref=src, dst_ref=dst, send_sem=send, recv_sem=recv, device_id=where, device_id_type=MESH
    )


def meet(devices):
    barrier = pltpu.get_barrier_semaphore()
    for where in devices:
        pl.semaphore_signal(barrier, inc=1, device_id=where, device_id_type=MESH)
    pl.semaphore_wait(barrier, len(devices))


def chip_peer(x, y, z, c, k):
    j = lax.rem(lax.div(y, 2) * 4 + z + k, 8)
    return j, device(x, lax.div(j, 4) * 2 + lax.rem(y, 2), lax.rem(j, 4), c)


HALF_KV, HALF_Q, HALF_O = 256, 128, 128


class Reduce:
    def __init__(self, at, rows, bufs, sems):
        self.at, self.rows = at, rows
        self.wz, self.za, self.zf, self.yf, self.wy, self.yg, self.zb, self.zg = bufs
        ss, rs = sems
        half = rows // 2
        lo, hi = pl.ds(0, half), pl.ds(half, half)
        self.lo, self.hi = lo, hi
        wz, za, zf, yf, wy, yg, zb, zg = bufs
        up, down, yh = at["up"], at["down"], at["yh"]
        front, rear, above, below = at["front"], at["rear"], at["above"], at["below"]
        up_i, down_i = lax.div(up, 2), lax.div(down, 2)
        self.up_i, self.down_i, self.yh = up_i, down_i, yh

        def cp(i, src, dst, where):
            return remote(src, dst, ss.at[i], rs.at[i], where)

        self.z = [
            cp(0, wz.at[0, 0], za.at[0], front),
            cp(1, wz.at[0, 1], za.at[1], rear),
            cp(2, wz.at[1, 1], zf.at[0, 1], front),
            cp(3, wz.at[2, 0], zf.at[1, 0], rear),
            cp(4, wz.at[1, 0], zf.at[0, 0], front),
            cp(5, wz.at[2, 1], zf.at[1, 1], rear),
        ]
        self.give = [
            cp(6, wy.at[1 - yh, :, lo], yg.at[0, :, lo], above),
            cp(7, wy.at[1 - yh, :, hi], yg.at[1, :, lo], below),
        ]
        self.free = [
            cp(8, wy.at[up_i, :, hi], yg.at[0, :, hi], above),
            cp(9, wy.at[down_i, :, lo], yg.at[1, :, lo], below),
        ]
        self.dep = [
            cp(6, wy.at[up_i, :, lo], yg.at[0, :, lo], above),
            cp(7, wy.at[down_i, :, hi], yg.at[1, :, hi], below),
        ]
        self.zy_give = [
            cp(10, wz.at[3, 1 - yh, lo], yf.at[0, lo], above),
            cp(11, wz.at[3, 1 - yh, hi], yf.at[1, lo], below),
        ]
        self.zy_pass = [
            cp(12, wz.at[3, up_i], yf.at[0], above),
            cp(13, wz.at[3, down_i], yf.at[1], below),
        ]
        self.yz = [
            cp(14, wy.at[yh, 0, lo], zb.at[0], front),
            cp(15, wy.at[yh, 0, hi], zb.at[1], rear),
            cp(16, wy.at[yh, 1], zg.at[0], front),
            cp(17, wy.at[yh, 2], zg.at[1], rear),
        ]

    def add(self, rows, dst, *srcs):
        @pl.loop(0, rows // 64)
        def _(i):
            r = pl.ds(al(i * 64, 64), 64)
            total = dst[r].astype(F32)
            for s in srcs:
                total += s[r].astype(F32)
            dst[r] = total.astype(BF)

    def start_y(self):
        @pl.when(self.at["owner"])
        def _():
            for cp in self.give:
                cp.start()

        @pl.when(self.at["middle"])
        def _():
            for cp in self.free:
                cp.start()

    def dep_z(self):
        self.z[0].wait_recv()
        self.add(self.rows, self.wz.at[1, 0], self.za.at[0])
        self.z[4].start()
        self.z[1].wait_recv()
        self.add(self.rows, self.wz.at[2, 1], self.za.at[1])
        self.z[5].start()

    def dep_y(self):
        half = self.rows // 2

        @pl.when(self.at["middle"])
        def _():
            for i, (idx, part) in enumerate(((self.up_i, self.lo), (self.down_i, self.hi))):
                self.give[i].wait_recv()
                for o in range(4):
                    self.add(half, self.wy.at[idx, o, part], self.yg.at[i, o, self.lo])
                self.dep[i].start()

    def mid_z(self):
        for i in (2, 3, 4, 5):
            self.z[i].wait_recv()
        for ab in range(2):
            self.add(self.rows, self.wz.at[3, ab], self.zf.at[0, ab], self.zf.at[1, ab])

        @pl.when(self.at["owner"])
        def _():
            for cp in self.zy_give:
                cp.start()

    def mid_y(self):
        @pl.when(self.at["owner"])
        def _():
            for cp in self.free + self.dep:
                cp.wait_recv()
            for cp in self.give:
                cp.wait_send()
            for o in range(4):
                self.add(self.rows, self.wy.at[self.yh, o], self.yg.at[0, o], self.yg.at[1, o])
                if o == 0:
                    self.yz[0].start()
                    self.yz[1].start()

    def last_z(self):
        half = self.rows // 2

        @pl.when(self.at["middle"])
        def _():
            for i, (idx, part) in enumerate(((self.up_i, self.lo), (self.down_i, self.hi))):
                self.zy_give[i].wait_recv()
                self.add(half, self.wz.at[3, idx, part], self.yf.at[i, self.lo])
                self.zy_pass[i].start()

    def last_y(self):
        half = self.rows // 2

        @pl.when(self.at["owner"])
        def _():
            self.yz[0].wait_recv()
            self.add(half, self.wy.at[self.yh, 1, self.lo], self.zb.at[0])
            self.yz[2].start()
            self.yz[1].wait_recv()
            self.add(half, self.wy.at[self.yh, 2, self.hi], self.zb.at[1])
            self.yz[3].start()

    def result(self, put):
        for cp in self.zy_pass:
            cp.wait_recv()
        for n in range(self.rows // 128):
            rows = pl.ds(n * 128, 128)
            put(0, n, lambda cols: (
                self.wz[3, self.yh, rows, cols].astype(F32)
                + self.yf[0, rows, cols].astype(F32) + self.yf[1, rows, cols].astype(F32)))
        for cp in self.yz[2:]:
            cp.wait_recv()
        for n in range(self.rows // 128):
            rows = pl.ds(n * 128, 128)
            put(1, n, lambda cols: (
                self.wy[self.yh, 3, rows, cols].astype(F32)
                + self.zg[0, rows, cols].astype(F32) + self.zg[1, rows, cols].astype(F32)))

    def drain(self):
        for cp in self.z:
            cp.wait_send()

        @pl.when(self.at["owner"])
        def _():
            for cp in self.zy_give + self.yz:
                cp.wait_send()

        @pl.when(self.at["middle"])
        def _():
            for cp in self.free + self.dep + self.zy_pass:
                cp.wait_send()


def reduce_scratch(rows):
    vm = pltpu.VMEM
    return [
        vm((4, 2, rows, 512), BF), vm((2, rows, 512), BF), vm((2, 2, rows, 512), BF), vm((2, rows, 512), BF),
        vm((2, 4, rows, 512), BF), vm((2, 4, rows, 512), BF), vm((2, rows // 2, 512), BF), vm((2, rows, 512), BF),
        pltpu.SemaphoreType.DMA((18,)), pltpu.SemaphoreType.DMA((18,)),
    ]


def kernel(
    pat, gpos, tok_in, cot_in, wq, wk, wv, wo,
    gt_out, gq_out, gk_out, gv_out, go_out,
    tok, cot, w, wov, r, g, gt, mask, masks, kg, vg, dkg, dvg, dkp, dvp, pr, xa, xf, fs,
    *rest,
):
    (o_bufs, o_sems), (q_bufs, q_sems), (v_bufs, v_sems) = [(rest[i : i + 8], rest[i + 8 : i + 10]) for i in (0, 10, 20)]
    (ssem, rsem, wssem, wrsem, lsem, mssem, mrsem, assem, arsem, bssem, brsem,
     cssem, crsem, dssem, drsem, essem, ersem, sssem, srsem, xssem, xrsem, fssem, frsem, flsem) = rest[30:]
    x, y, z, c = place()
    p, yh = lax.rem(y, 2), lax.div(y, 2)
    seq = lax.axis_index("seq")
    xr, xl, x2 = mod4(x + 1), mod4(x - 1), mod4(x + 2)
    zr, zl, z2 = mod4(z + 1), mod4(z - 1), mod4(z + 2)
    up, down = mod4(y + 1), mod4(y - 1)
    right, left = device(xr, y, z, c), device(xl, y, z, c)
    sib = device(x, y, z, 1 - c)
    me = yh * 4 + z
    my_doc = lax.div(me, 2) * 2 + p
    peers = [chip_peer(x, y, z, c, k) for k in range(1, 8)]

    meet(
        [right, left, sib]
        + [device(x, v, z, core) for v in (up, down) for core in (0, 1)]
        + [where for _, where in peers]
    )
    own = pl.ds(al(c * ROWS, ROWS), ROWS)
    other = pl.ds(al((1 - c) * ROWS, ROWS), ROWS)
    first = pl.ds(al(c * ROWS, 64), 64)
    second = pl.ds(al(c * ROWS + 64, 64), 64)

    def sends(a, given, buf):
        def cp(kind, src, dst, where):
            return remote(src, dst, ssem.at[a, kind], rsem.at[a, kind], where)

        return [
            cp(0, given, buf.at[x, own], right),
            cp(1, given, buf.at[x, own], left),
            cp(2, given, buf.at[x, own], sib),
            cp(3, buf.at[xl, first], buf.at[xl, first], right),
            cp(4, buf.at[xr, second], buf.at[xr, second], left),
            cp(5, buf.at[xl, own], buf.at[xl, own], sib),
            cp(6, buf.at[xr, own], buf.at[xr, own], sib),
            cp(7, buf.at[x2, first], buf.at[x2, first], sib),
            cp(8, buf.at[x2, second], buf.at[x2, second], sib),
        ]

    tsend = sends(0, tok_in, tok)
    csend = sends(1, cot_in, cot)
    wdev = device(x, mod4(y + 1 + 2 * c), z, p)
    zhalf = lax.rem(z, 2)
    sources = (wq, wk, wv, wo)

    def quarter(t, ref, h, n):
        size = 1024 if t < 3 else 64
        rows = pl.ds(al((2 * h + n) * size, size), size)
        return ref.at[t, rows] if ref is w else ref.at[rows]

    def held(t):
        return w if t < 3 else wov

    wsend = [
        remote(quarter(t, src, zhalf, c), quarter(t, held(t), zhalf, c), wssem.at[t], wrsem.at[t, c], wdev)
        for t, src in enumerate(sources)
    ]
    zdev = (device(x, y, zr, c), device(x, y, zl, c))
    wpass = [
        [
            remote(
                quarter(t, held(t), zhalf, n), quarter(t, held(t), zhalf, n),
                wssem.at[4 + 2 * t + n], wrsem.at[4 + t, n], zdev[n],
            )
            for n in (0, 1)
        ]
        for t in range(4)
    ]

    wlocal = [pltpu.make_async_copy(src, w.at[t], lsem.at[t]) for t, src in enumerate((wq, wk, wv))]
    wlocal.append(pltpu.make_async_copy(wo, wov, lsem.at[3]))
    tlocal = pltpu.make_async_copy(tok_in, tok.at[x, own], lsem.at[4])
    clocal = pltpu.make_async_copy(cot_in, cot.at[x, own], lsem.at[5])

    for k in (0, 1, 2):
        tsend[k].start()
    for cp in wsend:
        cp.start()
    tlocal.start()
    clocal.start()

    @pl.when(c == p)
    def _():
        for cp in wlocal:
            cp.start()

    kb = lax.div(lax.broadcasted_iota(jnp.int32, (8, 256), 1), 64)
    upper = lax.broadcasted_iota(jnp.int32, (8, 256), 0) == 0

    @pl.loop(0, 8)
    def _(d):
        prev0 = jnp.where(seq > 0, pat[d, 0, 0], 0)
        next0, prev1 = pat[d, 0, 1], pat[d, 1, 0]
        next1 = jnp.where(seq < 15, pat[d, 1, 1], 0)
        m0 = jnp.where(kb == 0, prev0, jnp.where(kb == 1, 1, jnp.where(kb == 2, next0, 0)))
        m1 = jnp.where(kb == 0, 0, jnp.where(kb == 1, prev1, jnp.where(kb == 2, 1, next1)))
        mask[c, d] = jnp.where(jnp.where(upper, m0, m1) == 1, 0.0, -jnp.inf)

    for t in (1, 2):
        r[t, :BLOCK] = jnp.zeros((BLOCK, HDIM), BF)
        r[t, BLOCK + 2048 :] = jnp.zeros((BLOCK, HDIM), BF)

    mask_sib = remote(mask.at[c], mask.at[c], mssem.at[7], mrsem.at[7], sib)
    mask_sib.start()
    mask_sib.wait()
    mask_out = [
        remote(mask.at[:, lax.div(j, 2) * 2 + p], masks.at[me], mssem.at[k], mrsem.at[k], where)
        for k, (j, where) in enumerate(peers)
    ]
    for cp in mask_out:
        cp.start()
    mask_own = pltpu.make_async_copy(mask.at[:, my_doc], masks.at[me], lsem.at[8])
    mask_own.start()

    def relay(copies):
        copies[0].wait_recv()
        copies[3].start()
        copies[5].start()
        copies[1].wait_recv()
        copies[4].start()
        copies[6].start()

    def weights_pass():
        @pl.when(c != p)
        def _():
            for t in range(4):
                for n in (0, 1):
                    ref = quarter(t, held(t), zhalf, n)
                    remote(ref, ref, wssem.at[t], wrsem.at[t, n], sib).wait_recv()
                    wpass[t][n].start()

    def weights_here(ts):
        @pl.when(c == p)
        def _():
            for t in ts:
                wlocal[t].wait()

        @pl.when(c != p)
        def _():
            for t in ts:
                for n in (0, 1):
                    wpass[t][n].wait()

    mine = pl.ds(al(me * CHIP_ROWS + BLOCK, 64), CHIP_ROWS)

    def boxes(j, t0, n):
        return gt.at[pl.ds(t0, n), :, pl.ds(al(j * HDIM, HDIM), HDIM)]

    def box(j, t):
        return gt.at[t, :, pl.ds(al(j * HDIM, HDIM), HDIM)]

    def chip(j):
        return device(x, lax.div(j, 4) * 2 + p, lax.rem(j, 4), c)

    def project(doc, t):
        got = jnp.dot(tok[doc], w[t], preferred_element_type=F32).astype(BF)
        gt[t, :, pl.ds(al(doc * 256, 256), 256)] = got

    def project_near(t):
        @pl.loop(0, 3)
        def _(n):
            project(lax.rem(x + n + lax.div(n, 2), 4), t)

    def qkv(j):
        return remote(boxes(j, 0, 3), r.at[pl.ds(0, 3), mine], assem.at[j], arsem.at[me], chip(j))

    qkv_own = pltpu.make_async_copy(boxes(me, 0, 3), r.at[pl.ds(0, 3), mine], lsem.at[6])

    def send_qkv(last):
        for n in range(8):
            j = lax.rem(me + n, 8)
            here = lax.div(j, 2) == x2
            here = here if last else jnp.logical_not(here)
            if n == 0:

                @pl.when(here)
                def _():
                    qkv_own.start()

            else:

                @pl.when(here)
                def _():
                    qkv(j).start()

    weights_pass()
    relay(tsend)
    for k in (0, 1, 2):
        csend[k].start()
    tlocal.wait()
    clocal.wait()
    tsend[2].wait_recv()
    tsend[5].wait_recv()
    tsend[6].wait_recv()
    weights_here((0,))
    project_near(0)
    weights_here((1,))
    project_near(1)
    tsend[3].wait_recv()
    tsend[7].start()
    tsend[4].wait_recv()
    tsend[8].start()
    weights_here((2,))
    project_near(2)
    send_qkv(False)
    tsend[7].wait_recv()
    tsend[8].wait_recv()

    @pl.loop(0, 3)
    def _(t):
        project(x2, t)

    send_qkv(True)

    relay(csend)
    weights_here((3,))

    def back(doc):
        got = lax.dot_general(cot[doc], wov[...], NT, preferred_element_type=F32).astype(BF)
        gt[3, :, pl.ds(al(doc * 256, 256), 256)] = got
        for h in (0, 1):
            j = 2 * doc + h

            @pl.when(j != me)
            def _():
                remote(box(j, 3), r.at[3, mine], bssem.at[j], brsem.at[me], chip(j)).start()

            @pl.when(j == me)
            def _():
                pltpu.make_async_copy(box(j, 3), r.at[3, mine], lsem.at[7]).start()

    csend[2].wait_recv()
    back(x)
    csend[5].wait_recv()
    back(xl)
    csend[6].wait_recv()
    back(xr)

    for n in range(1, 8):
        j = lax.rem(me + n, 8)
        qkv(j).wait_send()
        remote(boxes(j, 0, 3), r.at[pl.ds(0, 3), mine], assem.at[j], arsem.at[j], sib).wait_recv()
    qkv_own.wait()
    for cp in mask_out:
        cp.wait()
    mask_own.wait()
    scale = HDIM**-0.5
    pos = jnp.broadcast_to(gpos[pl.ds(my_doc, 1), :], (128, 128))
    pos_t = pos.T
    lane = lax.broadcasted_iota(jnp.int32, (128, 128), 1)
    sub = lax.broadcasted_iota(jnp.int32, (128, 128), 0)
    low = lax.broadcasted_iota(jnp.int32, (128, 256), 0) < BLOCK

    def nt(a, b):
        return lax.dot_general(a, b, NT, preferred_element_type=F32)

    def tn(a, b):
        return lax.dot_general(a, b, TN, preferred_element_type=F32)

    def mm(a, b):
        return jnp.dot(a, b, preferred_element_type=F32)

    dkg[...] = jnp.zeros_like(dkg)
    dvg[...] = jnp.zeros_like(dvg)

    @pl.loop(0, 16)
    def _(i):
        rows = pl.ds(al(i * 128 + BLOCK, 64), 128)
        pick = (pos_t == i * 128 + lane).astype(F32).astype(BF)
        dkg[...] += mm(pick, r[1, rows])
        dvg[...] += mm(pick, r[2, rows])

    kg[...] = dkg[...].astype(BF)
    vg[...] = dvg[...].astype(BF)
    wz, wy = v_bufs[0], v_bufs[4]

    def saved(i):
        return (lax.div(i, 4), lax.rem(lax.div(i, 2), 2), pl.ds(al(lax.rem(i, 2) * 128, 128), 128))

    def forward(j):
        tiles = (2 * j, 2 * j + 1)
        rows = [pl.ds(al(i * 128 + BLOCK, 64), 128) for i in tiles]
        wins = [pl.ds(al(i * 128, 128), 256) for i in tiles]
        qs = [r[0, a] for a in rows]
        ks, vs = [r[1, a] for a in wins], [r[2, a] for a in wins]
        kgv, vgv = kg[...], vg[...]
        sls = [nt(q, k) for q, k in zip(qs, ks)]
        sgs = [nt(q, kgv) * scale for q in qs]
        for h in (0, 1):
            seen = masks[j, h]
            sls[h] = sls[h] * scale + jnp.where(low, seen[0:1], seen[1:2])
        tops = [jnp.maximum(a.max(-1, keepdims=True), b.max(-1, keepdims=True)) for a, b in zip(sls, sgs)]
        els = [jnp.exp(a - t) for a, t in zip(sls, tops)]
        egs = [jnp.exp(a - t) for a, t in zip(sgs, tops)]
        invs = [1.0 / (a.sum(-1, keepdims=True) + b.sum(-1, keepdims=True)) for a, b in zip(els, egs)]
        pls = [(a * t).astype(BF) for a, t in zip(els, invs)]
        pgs = [(a * t).astype(BF) for a, t in zip(egs, invs)]
        ctx = [(mm(a, v) + mm(b, vgv)).astype(BF) for a, b, v in zip(pls, pgs, vs)]
        for h in (0, 1):
            a, b, rr = saved(tiles[h])
            wz[a, b, rr, pl.ds(0, 256)] = pls[h]
            wz[a, b, rr, pl.ds(256, 128)] = pgs[h]
            wy[lax.div(j, 4), lax.rem(j, 4), pl.ds(h * 128, 128), pl.ds(0, 128)] = ctx[h]

    pl.loop(0, 5)(forward)
    csend[3].wait_recv()
    csend[7].start()
    csend[4].wait_recv()
    csend[8].start()
    csend[7].wait_recv()
    csend[8].wait_recv()
    back(x2)
    pl.loop(5, 8)(forward)

    def ctx_box(j):
        return wy.at[lax.div(j, 4), lax.rem(j, 4), pl.ds(0, 256), pl.ds(0, 128)]

    def spot(t0, n):
        rows = pl.ds(al(lax.div(me, 2) * CHIP_ROWS, CHIP_ROWS), CHIP_ROWS)
        return g.at[pl.ds(t0, n), rows, pl.ds(al(lax.rem(me, 2) * HDIM, HDIM), HDIM)]

    def spot_o():
        rows = pl.ds(al(lax.div(me, 2) * CHIP_ROWS, CHIP_ROWS), CHIP_ROWS)
        return g.at[3, rows, pl.ds(al(lax.rem(me, 2) * HDIM, HDIM), HDIM)]

    ctx_out = [
        remote(ctx_box(j), spot_o(), cssem.at[k], crsem.at[k], where) for k, (j, where) in enumerate(peers)
    ]
    for cp in ctx_out:
        cp.start()
    ctx_own = pltpu.make_async_copy(ctx_box(me), spot_o(), lsem.at[9])
    ctx_own.start()

    at = {
        "up": up, "down": down, "yh": yh, "owner": c == p, "middle": c != p,
        "front": device(x, y, zr, c), "rear": device(x, y, zl, c),
        "above": device(x, up, z, c), "below": device(x, down, z, c),
    }
    groups = (z2, zr, zl, z)
    order = [(0, 0), (0, 1), (1, 1), (2, 0), (1, 0), (2, 1), (3, 0), (3, 1)]
    red_o = Reduce(at, HALF_O, o_bufs, o_sems)
    red_q = Reduce(at, HALF_Q, q_bufs, q_sems)
    red_v = Reduce(at, HALF_KV, v_bufs, v_sems)

    def turn(t):
        for i in range(4):
            rows = pl.ds(i * 256, 256)
            gt[t, :, rows] = g[t, rows].T

    def piece(red, src, n, t0, count):
        o, ab = order[n]

        @pl.loop(0, 2)
        def _(h):
            lanes = pl.ds(al(h * 256, 256), 256)
            here = pl.ds(al(ab * 2048 + groups[o] * 512 + h * 256, 256), 256)
            left_side = gt[pl.ds(t0, count)].reshape(count * 256, 1024)
            acc = mm(left_side, src[:, :, here].reshape(1024, 256)).astype(BF)
            for t in range(count):
                rows = pl.ds(t * 128, 128)
                red.wz[o, ab, rows, lanes] = acc[t * 256 : t * 256 + 128]
                red.wy[ab, o, rows, lanes] = acc[t * 256 + 128 : t * 256 + 256]

        if n < 4:
            red.z[n].start()

    for j in range(8):

        @pl.when(j != me)
        def _():
            remote(box(j, 3), r.at[3, mine], bssem.at[j], brsem.at[j], sib).wait_send()

    pltpu.make_async_copy(box(me, 3), r.at[3, mine], lsem.at[7]).wait()

    for j in range(8):

        @pl.when(j != me)
        def _():
            remote(box(j, 3), r.at[3, mine], bssem.at[j], brsem.at[j], sib).wait_recv()

    dkp[...] = jnp.zeros_like(dkp)
    dvp[...] = jnp.zeros_like(dvp)
    dkg[...] = jnp.zeros_like(dkg)
    dvg[...] = jnp.zeros_like(dvg)

    def out_box(i, t):
        j = lax.div(i, 2)
        return (t, pl.ds(al(lax.rem(i, 2) * 128, 128), 128), pl.ds(al(j * 128, 128), 128))

    def backward(j):
        tiles = (2 * j, 2 * j + 1)
        rows = [pl.ds(al(i * 128 + BLOCK, 64), 128) for i in tiles]
        wins = [pl.ds(al(i * 128, 128), 256) for i in tiles]
        qs, dos = [r[0, a] for a in rows], [r[3, a] for a in rows]
        ks, vs = [r[1, a] for a in wins], [r[2, a] for a in wins]
        kgv, vgv = kg[...], vg[...]
        spots = [saved(i) for i in tiles]
        pls = [wz[a, b, rr, pl.ds(0, 256)] for a, b, rr in spots]
        pgs = [wz[a, b, rr, pl.ds(256, 128)] for a, b, rr in spots]
        dls = [nt(d, v) for d, v in zip(dos, vs)]
        dgs = [nt(d, vgv) for d in dos]
        dvl = [tn(a, d) for a, d in zip(pls, dos)]
        dvs = tn(jnp.concatenate(pgs, 0), jnp.concatenate(dos, 0))
        pfs, pgf = [a.astype(F32) for a in pls], [a.astype(F32) for a in pgs]
        deltas = [
            (a * d).sum(-1, keepdims=True) + (b * e).sum(-1, keepdims=True) for a, d, b, e in zip(pfs, dls, pgf, dgs)
        ]
        sls = [(a * (d - t) * scale).astype(BF) for a, d, t in zip(pfs, dls, deltas)]
        sgs = [(a * (d - t) * scale).astype(BF) for a, d, t in zip(pgf, dgs, deltas)]
        gqs = [(mm(a, k) + mm(b, kgv)).astype(BF) for a, b, k in zip(sls, sgs, ks)]
        dkl = [tn(a, q) for a, q in zip(sls, qs)]
        dks = tn(jnp.concatenate(sgs, 0), jnp.concatenate(qs, 0))
        for h in (0, 1):
            gt[out_box(tiles[h], 0)] = gqs[h]
        for h in (0, 1):
            dkp[wins[h]] += dkl[h]
            dvp[wins[h]] += dvl[h]
        dkg[...] += dks
        dvg[...] += dvs

    def home_q(j):
        return remote(box(j, 0), spot(0, 1).at[0], dssem.at[j], drsem.at[me], chip(j))

    home_q_own = pltpu.make_async_copy(box(me, 0), spot(0, 1).at[0], lsem.at[10])

    @pl.loop(1, 9)
    def _(n):
        j = lax.rem(me + n, 8)
        backward(j)

        @pl.when(n < 8)
        def _():
            home_q(j).start()

    home_q_own.start()

    def split(a):
        high = a.astype(BF)
        return high, (a - high.astype(F32)).astype(BF)

    both = jnp.concatenate([jnp.concatenate(split(dkg[...]), 0), jnp.concatenate(split(dvg[...]), 0)], 1)

    def finish(i):
        inner = pl.ds(al(i * 128 + BLOCK, 64), 128)
        put = (pos == i * 128 + sub).astype(F32).astype(BF)
        extra = mm(jnp.concatenate([put, put], 1), both)
        gt[out_box(i, 1)] = (dkp[inner] + extra[:, :128]).astype(BF)
        gt[out_box(i, 2)] = (dvp[inner] + extra[:, 128:]).astype(BF)

    def home_kv(j):
        return remote(boxes(j, 1, 2), spot(1, 2), essem.at[j], ersem.at[me], chip(j))

    @pl.loop(1, 9)
    def _(n):
        j = lax.rem(me + n, 8)
        finish(2 * j)
        finish(2 * j + 1)

        @pl.when(n < 8)
        def _():
            home_kv(j).start()

    home_kv_own = pltpu.make_async_copy(boxes(me, 1, 2), spot(1, 2), lsem.at[11])
    home_kv_own.start()

    for cp in ctx_out:
        cp.wait()
    ctx_own.wait()
    turn(3)
    for n in range(8):
        piece(red_o, cot, n, 3, 1)
    red_o.start_y()
    for cp in tsend + csend + wsend:
        cp.wait_send()
    for n in range(1, 8):
        j = lax.rem(me + n, 8)
        home_q(j).wait_send()
        remote(box(j, 0), spot(0, 1).at[0], dssem.at[j], drsem.at[j], sib).wait_recv()
    home_q_own.wait()
    turn(0)
    for n in range(8):
        piece(red_q, tok, n, 0, 1)
    red_q.start_y()
    for n in range(1, 8):
        j = lax.rem(me + n, 8)
        home_kv(j).wait_send()
        remote(boxes(j, 1, 2), spot(1, 2), essem.at[j], ersem.at[j], sib).wait_recv()
    home_kv_own.wait()

    part = cot
    docs = (x2, xr, xl, x)
    to_sib = [remote(part.at[o, other], pr.at[o], sssem.at[o], srsem.at[o], sib) for o in range(4)]

    def tokens_part(o):
        rows = pl.ds(al(docs[o] * CHIP_ROWS, CHIP_ROWS), CHIP_ROWS)

        @pl.loop(0, 8)
        def _(n):
            cols = pl.ds(al(n * 512, 512), 512)
            a = jnp.concatenate([g[t, rows] for t in range(3)], 1)
            b = jnp.concatenate([w[t, cols] for t in range(3)], 1)
            part[o, :, cols] = nt(a, b).astype(BF)

        to_sib[o].start()

    xc = [
        remote(pr.at[0, pl.ds(0, 64)], xa.at[pl.ds(0, 64)], xssem.at[0], xrsem.at[0], right),
        remote(pr.at[0, pl.ds(64, 64)], xa.at[pl.ds(64, 64)], xssem.at[1], xrsem.at[1], left),
        remote(pr.at[1], xf.at[0], xssem.at[2], xrsem.at[2], right),
        remote(pr.at[2], xf.at[1], xssem.at[3], xrsem.at[3], left),
    ]

    def sum_rows(o, extra=None):
        @pl.loop(0, 8)
        def _(n):
            cols = pl.ds(al(n * 512, 512), 512)
            for h in range(2):
                rows = pl.ds(h * 64, 64)
                own_half = pl.ds(al(c * ROWS + h * 64, 64), 64)
                total = part[o, own_half, cols].astype(F32) + pr[o, rows, cols].astype(F32)
                if extra is not None and extra == h:
                    total += xa[rows, cols].astype(F32)
                pr[o, rows, cols] = total.astype(BF)

    tokens_part(0)
    tokens_part(1)
    to_sib[0].wait_recv()
    sum_rows(0)
    xc[0].start()
    xc[1].start()
    tokens_part(2)
    turn(1)
    turn(2)
    for n in range(0, 4):
        piece(red_v, tok, n, 1, 2)
    red_o.dep_z()
    red_o.dep_y()
    red_q.dep_z()
    red_q.dep_y()
    for n in range(4, 8):
        piece(red_v, tok, n, 1, 2)
    red_v.start_y()
    to_sib[1].wait_recv()
    xc[0].wait_recv()
    sum_rows(1, 0)
    xc[2].start()
    to_sib[2].wait_recv()
    xc[1].wait_recv()
    sum_rows(2, 1)
    xc[3].start()
    red_v.dep_z()
    red_v.dep_y()
    red_o.mid_z()
    red_o.mid_y()
    tokens_part(3)
    red_o.last_z()
    red_o.last_y()
    red_q.mid_z()
    red_q.mid_y()
    red_q.last_z()
    red_q.last_y()
    to_sib[3].wait_recv()
    red_v.mid_z()
    red_v.mid_y()

    xc[2].wait_recv()
    xc[3].wait_recv()

    to_sib[3].wait_send()

    @pl.loop(0, 8)
    def _(n):
        cols = pl.ds(al(n * 512, 512), 512)
        total = part[3, own, cols].astype(F32) + pr[3, :, cols].astype(F32)
        total += xf[0, :, cols].astype(F32) + xf[1, :, cols].astype(F32)
        part[3, other, cols] = total.astype(BF)

    gt_copy = pltpu.make_async_copy(part.at[3, other], gt_out, lsem.at[12])
    gt_copy.start()
    red_v.last_z()
    red_v.last_y()

    outs = (gq_out, gk_out, gv_out, go_out)
    final = [remote(fs.at[1, t], outs[t], fssem.at[t], frsem.at[t], sib) for t in range(4)]
    final_own = [pltpu.make_async_copy(fs.at[0, t], outs[t], flsem.at[t]) for t in range(4)]

    @pl.when(c == p)
    def _():
        def put(t0):
            def run(head, n, value):
                lanes = pl.ds(head * 128, 128)
                for s in range(2):
                    core = c if s == 0 else 1 - c
                    got = value(pl.ds(al(core * 256, 256), 256))
                    if t0 + n < 3:
                        fs[s, t0 + n, :, lanes] = got.T
                    else:
                        fs[s, 3, lanes, :] = got

            return run

        red_o.result(put(3))
        final[3].start()
        final_own[3].start()
        red_q.result(put(0))
        final[0].start()
        final_own[0].start()
        red_v.result(put(1))
        for t in (1, 2):
            final[t].start()
            final_own[t].start()
        for t in range(4):
            final[t].wait_send()
            final_own[t].wait()

    @pl.when(c != p)
    def _():
        for cp in final:
            cp.wait_recv()

    red_o.drain()
    red_q.drain()
    red_v.drain()
    for cp in to_sib[:3] + xc:
        cp.wait_send()
    gt_copy.wait()


def on_device(tokens, cotangent, w_query, w_key, w_value, w_output, global_pos, pattern):
    dma = pltpu.SemaphoreType.DMA
    vm = pltpu.VMEM
    square = jax.ShapeDtypeStruct((256, 256), F32)
    grad_tokens, gq, gk, gv, go = pl.pallas_call(
        kernel,
        out_shape=(jax.ShapeDtypeStruct((ROWS, D), BF), square, square, square, square),
        in_specs=[pl.BlockSpec(memory_space=pltpu.SMEM), pl.BlockSpec(memory_space=pltpu.VMEM)] + [ANY] * 6,
        out_specs=(ANY,) * 5,
        scratch_shapes=[
            vm((4, CHIP_ROWS, D), BF),
            vm((4, CHIP_ROWS, D), BF),
            vm((3, D, 256), BF),
            vm((256, D), BF),
            vm((4, 2176, HDIM), BF),
            vm((4, 1024, 256), BF),
            vm((4, 256, 1024), BF),
            vm((2, 8, 8, 256), F32),
            vm((8, 2, 8, 256), F32),
            vm((128, HDIM), BF), vm((128, HDIM), BF), vm((128, HDIM), F32), vm((128, HDIM), F32),
            vm((2176, HDIM), F32), vm((2176, HDIM), F32),
            vm((4, ROWS, D), BF),
            vm((ROWS, D), BF),
            vm((2, ROWS, D), BF),
            vm((2, 4, 256, 256), F32),
            *reduce_scratch(HALF_O),
            *reduce_scratch(HALF_Q),
            *reduce_scratch(HALF_KV),
            dma((2, 9)), dma((2, 9)), dma((12,)), dma((8, 2)), dma((13,)), dma((8,)), dma((8,)),
            dma((8,)), dma((8,)), dma((8,)), dma((8,)), dma((7,)), dma((7,)), dma((8,)), dma((8,)),
            dma((8,)), dma((8,)), dma((4,)), dma((4,)), dma((4,)), dma((4,)), dma((4,)), dma((4,)), dma((4,)),
        ],
        compiler_params=pltpu.CompilerParams(
            collective_id=0, has_side_effects=True, vmem_limit_bytes=63 << 20
        ),
        cost_estimate=pl.CostEstimate(flops=25 * 10**9, bytes_accessed=60 << 20, transcendentals=10**6),
    )(pattern, global_pos, tokens[0], cotangent[0], w_query, w_key, w_value, w_output)
    return grad_tokens[None], gq, gk, gv, go


def solution(mesh):
    in_specs = (
        P("fsdp", "seq", None),
        P("fsdp", "seq", None),
        P(None, "fsdp"),
        P(None, "fsdp"),
        P(None, "fsdp"),
        P("fsdp", None),
        P(),
        P(None, "seq", None),
    )
    out_specs = (
        P("fsdp", "seq", None),
        P("seq", "fsdp"),
        P("seq", "fsdp"),
        P("seq", "fsdp"),
        P("fsdp", "seq"),
    )
    return jax.shard_map(
        on_device, mesh=mesh, in_specs=in_specs, out_specs=out_specs, check_vma=False
    )
```
